32 devices in a mesh: batch: 4 (over y, core), blk: 8 (over z, x).
Axes of the slice: x: 2, y: 2, z: 4, core: 2. Of those that a mesh axis runs over, the one named last changes fastest.
Arguments:
- inputs: bfloat16 [12, 2048, 1024], P('batch', 'blk'), may hold values from -6 to 6
- ln_attn: float32 [1024], replicated, may hold values from 0.1 to 1.9
- w_query: bfloat16 [1024, 1024], replicated, may hold values from -0.1875 to 0.1875
- w_key: bfloat16 [1024, 1024], replicated, may hold values from -0.1875 to 0.1875
- w_value: bfloat16 [1024, 1024], replicated, may hold values from -0.1875 to 0.1875
- w_out: bfloat16 [1024, 1024], replicated, may hold values from -0.1875 to 0.1875
- head_scale: float32 [16], replicated, may hold values from 0.5 to 2
- ln_post: float32 [1024], replicated, may hold values from 0.1 to 1.9
- ln_ffn: float32 [1024], replicated, may hold values from 0.1 to 1.9
- w_fc1: bfloat16 [1024, 4096], replicated, may hold values from -0.1875 to 0.1875
- ln_mid: float32 [4096], replicated, may hold values from 0.1 to 1.9
- w_fc2: bfloat16 [4096, 1024], replicated, may hold values from -0.09375 to 0.09375
- offsets: int32 [12, 4], P('batch'), may hold values from 0 to 2047, as said below
- cotangent: bfloat16 [12, 2048, 1024], P('batch', 'blk'), may hold values from -6 to 6
Outputs:
- layer_out: bfloat16 [12, 2048, 1024], P('batch', 'blk')
- grad_inputs: float32 [12, 2048, 1024], P('batch', 'blk')
- grad_ln_attn: float32 [1024], P('blk')
- grad_w_query: float32 [1024, 1024], P('blk')
- grad_w_key: float32 [1024, 1024], P('blk')
- grad_w_value: float32 [1024, 1024], P('blk')
- grad_w_out: float32 [1024, 1024], P('blk')
- grad_head_scale: float32 [16], replicated
- grad_ln_post: float32 [1024], P('blk')
- grad_ln_ffn: float32 [1024], P('blk')
- grad_w_fc1: float32 [1024, 4096], P('blk')
- grad_ln_mid: float32 [4096], P('blk')
- grad_w_fc2: float32 [4096, 1024], P('blk')
The draws below stay inside these ranges and needn't reach their ends.
Inputs may be any that keep to these rules, and one draw needn't show every extreme that they name: In each row offsets rise strictly from offsets[r, 0] = 0. In each aligned block of 3 rows one row has a document that begins within its first 256 positions and ends within its last 256, and its last document is a single position.
All inputs are finite; a program needn't handle non-finite values.
Results may differ from the reference program's by a relative error of at most 0.02.
Values may be sent and summed in bfloat16 or wider, within the bound.
No kernel may reach another device: no remote copies, remote signals or barrier semaphores. Data moves between devices by JAX's collectives and lax.ppermute only.
A program may use at most 256 MiB of HBM per device.

```python
import math
import jax
import jax.numpy as jnp
from jax import lax

D = 1024
HEADS = 16
HEAD_DIM = 64
FF = 4096
LEN = 2048
ROWS_DEV = 3
SPAN_LEN = 256
ROWS = 12


def draw_offsets(key, part):
    key = jax.random.fold_in(key, 11)
    subkeys = jax.random.split(key, 5)
    row_ids = jnp.arange(ROWS, dtype=jnp.int32)
    chosen = jax.random.randint(subkeys[0], (ROWS // ROWS_DEV,), 0, ROWS_DEV)
    long_rows = row_ids % ROWS_DEV == jnp.repeat(chosen, ROWS_DEV)
    first_start = jax.random.randint(subkeys[1], (ROWS,), 1, SPAN_LEN)
    second_long = jax.random.randint(subkeys[2], (ROWS,), LEN - SPAN_LEN, LEN - 1)
    second_free = jax.random.randint(subkeys[3], (ROWS,), SPAN_LEN, LEN // 2)
    third_free = jax.random.randint(subkeys[4], (ROWS,), LEN // 2, LEN)
    second_start = jnp.where(long_rows, second_long, second_free)
    third_start = jnp.where(long_rows, LEN - 1, third_free)
    zero_start = jnp.zeros((ROWS,), jnp.int32)
    return jnp.stack([zero_start, first_start, second_start, third_start], axis=1).astype(jnp.int32)


def shard_levels(key, extent, shards, least, high):
    def one(axis_at, blocks):
        steps = jax.random.uniform(jax.random.fold_in(jax.random.fold_in(key, 6), axis_at), (blocks,), jnp.float32, least / len(shards), high / len(shards))
        return jnp.repeat(jnp.exp(steps), extent[axis_at] // blocks).reshape((-1,) + (1,) * (len(extent) - axis_at - 1))

    loudness = one(*shards[0])
    for cut in shards[1:]:
        loudness = loudness * one(*cut)
    return loudness


def gaussian(rng, extent, width, reach, cuts=(), kind=jnp.bfloat16):
    values = jax.random.normal(rng, extent, jnp.float32) * width
    if len(cuts) > 0:
        values = shard_levels(rng, extent, cuts, -0.22, 0.18) * values
    return jnp.clip(values, min=-reach, max=reach).astype(kind)


def setup_inputs(seed: int = 0) -> dict:
    keys = jax.random.split(jax.random.key(seed), 15)
    inputs = gaussian(keys[0], (ROWS, LEN, D), 1.0, 6.0, ((0, 4), (1, 8)))
    ln_attn = jnp.clip(1.0 + 0.18 * jax.random.normal(keys[1], (D,), jnp.float32), 0.1, 1.9)
    w_query = gaussian(keys[2], (D, D), D ** -0.5, 0.1875)
    w_key = gaussian(keys[3], (D, D), D ** -0.5, 0.1875)
    w_value = gaussian(keys[4], (D, D), D ** -0.5, 0.1875)
    w_out = gaussian(keys[5], (D, D), D ** -0.5, 0.1875)
    head_scale = jnp.clip(jnp.exp(jax.random.uniform(keys[6], (HEADS,), jnp.float32, math.log(0.5), math.log(2.0))), 0.5, 2.0)
    ln_post = jnp.clip(1.0 + 0.18 * jax.random.normal(keys[7], (D,), jnp.float32), 0.1, 1.9)
    ln_ffn = jnp.clip(1.0 + 0.18 * jax.random.normal(keys[8], (D,), jnp.float32), 0.1, 1.9)
    w_fc1 = gaussian(keys[9], (D, FF), D ** -0.5, 0.1875)
    ln_mid = jnp.clip(1.0 + 0.18 * jax.random.normal(keys[10], (FF,), jnp.float32), 0.1, 1.9)
    w_fc2 = gaussian(keys[11], (FF, D), FF ** -0.5, 0.09375)
    offsets = draw_offsets(jax.random.fold_in(keys[14], 71), 0)
    cotangent = gaussian(keys[13], (ROWS, LEN, D), 1.0, 6.0, ((0, 4), (1, 8)))
    return {"inputs": inputs, "ln_attn": ln_attn, "w_query": w_query, "w_key": w_key, "w_value": w_value, "w_out": w_out, "head_scale": head_scale, "ln_post": ln_post, "ln_ffn": ln_ffn, "w_fc1": w_fc1, "ln_mid": ln_mid, "w_fc2": w_fc2, "offsets": offsets, "cotangent": cotangent}


@jax.custom_vjp
def low(v):
    return lax.optimization_barrier(v.astype(jnp.bfloat16)).astype(jnp.float32)

@jax.custom_vjp
def low_back(v):
    return v

def low_keep(v):
    return (low(v), None)

def low_pass(kept, grad):
    return (grad,)

def back_keep(v):
    return (v, None)

def back_low(kept, grad):
    return (low(grad),)
low.defvjp(low_keep, low_pass)
low_back.defvjp(back_keep, back_low)
EPSILON = 1e-05
MASKED = -1e+30
HIGHEST = lax.Precision.HIGHEST

def layer_norm(rows_in, gain_vec):
    average = lax.optimization_barrier(jnp.mean(rows_in, axis=-1, keepdims=True))
    centred = rows_in - average
    variance = lax.optimization_barrier(jnp.mean(centred * centred, axis=-1, keepdims=True))
    return centred * lax.rsqrt(variance + EPSILON) * gain_vec

def row_forward(row_in, params, doc_ids):
    ln_attn, w_query, w_key, w_value, w_out, head_scale, ln_post, ln_ffn, w_fc1, ln_mid, w_fc2 = params
    normed = low(layer_norm(row_in, ln_attn))

    def project(weight):
        return low_back(low(jnp.dot(normed, weight, precision=HIGHEST))).reshape(LEN, HEADS, HEAD_DIM)
    query_heads = project(w_query)
    key_heads = project(w_key)
    value_heads = project(w_value)
    positions = jnp.arange(LEN, dtype=jnp.int32)
    query_block_len = min(512, LEN)
    block_total = LEN // query_block_len

    def attend(query_pack):
        query_blk, query_pos, query_doc = query_pack
        raw_scores = jnp.einsum('qhe,khe->hqk', query_blk, key_heads, precision=HIGHEST) * HEAD_DIM ** (-0.5)
        raw_scores = low_back(raw_scores)
        allowed = (positions[None, :] <= query_pos[:, None]) & (doc_ids[None, :] == query_doc[:, None])
        masked = jnp.where(allowed[None], raw_scores, MASKED)
        row_top = lax.optimization_barrier(jnp.max(masked, axis=-1, keepdims=True))
        exp_terms = jnp.exp(masked - row_top)
        prob_rows = low(exp_terms / lax.optimization_barrier(jnp.sum(exp_terms, axis=-1, keepdims=True)))
        return low_back(jnp.einsum('hqk,khe->qhe', prob_rows, value_heads, precision=HIGHEST))
    attn_out = lax.map(jax.checkpoint(attend), (query_heads.reshape(block_total, query_block_len, HEADS, HEAD_DIM), positions.reshape(block_total, query_block_len), doc_ids.reshape(block_total, query_block_len)))
    attn_out = attn_out.reshape(LEN, HEADS, HEAD_DIM)
    scaled = low((attn_out * head_scale[None, :, None]).reshape(LEN, D))
    attn_proj = low_back(jnp.dot(scaled, w_out, precision=HIGHEST))
    residual = row_in + layer_norm(attn_proj, ln_post)
    ffn_in = low(layer_norm(residual, ln_ffn))
    pre_act = low_back(jnp.dot(ffn_in, w_fc1, precision=HIGHEST))
    mid_act = low(layer_norm(jax.nn.gelu(pre_act, approximate=False), ln_mid))
    return residual + low_back(jnp.dot(mid_act, w_fc2, precision=HIGHEST))

def reference(inputs, ln_attn, w_query, w_key, w_value, w_out, head_scale, ln_post, ln_ffn, w_fc1, ln_mid, w_fc2, offsets, cotangent):
    params = (ln_attn.astype(jnp.float32), w_query.astype(jnp.float32), w_key.astype(jnp.float32), w_value.astype(jnp.float32), w_out.astype(jnp.float32), head_scale.astype(jnp.float32), ln_post.astype(jnp.float32), ln_ffn.astype(jnp.float32), w_fc1.astype(jnp.float32), ln_mid.astype(jnp.float32), w_fc2.astype(jnp.float32))
    positions = jnp.arange(LEN, dtype=jnp.int32)

    def one_row(totals, row_data):
        row_in, row_offsets, row_cot = row_data
        doc_ids = lax.optimization_barrier(jnp.sum((row_offsets[:, None] <= positions[None, :]).astype(jnp.int32), axis=0)) - 1

        def forward_of(x_in, weights):
            return row_forward(x_in, weights, doc_ids)
        row_out, pullback = jax.vjp(forward_of, row_in.astype(jnp.float32), params)
        grad_in, grad_params = pullback(row_cot.astype(jnp.float32))
        return (jax.tree.map(jnp.add, totals, grad_params), (row_out.astype(jnp.bfloat16), grad_in))
    totals, (layer_out, grad_inputs) = lax.scan(one_row, jax.tree.map(jnp.zeros_like, params), (inputs, offsets, cotangent))
    return (layer_out, grad_inputs, totals[0], totals[1], totals[2], totals[3], totals[4], totals[5], totals[6], totals[7], totals[8], totals[9], totals[10])
```

```python
import functools

import jax
import jax.numpy as jnp
from jax import lax
from jax.experimental import pallas as pl
from jax.experimental.pallas import tpu as pltpu
from jax.sharding import PartitionSpec as P

EPSILON = 1e-05
MASKED = -1e30
VMEM_BYTES = 56 * 1024 * 1024
F32 = jnp.float32
BF16 = jnp.bfloat16
LAST = (((1,), (1,)), ((), ()))
FIRST = (((0,), (0,)), ((), ()))


def dot_last(left, right):
    return lax.dot_general(left, right, LAST, preferred_element_type=F32)


def dot_first(left, right):
    return lax.dot_general(left, right, FIRST, preferred_element_type=F32)


def doc_start(offs_ref, row, pos):
    start = jnp.zeros_like(pos)
    for d in range(offs_ref.shape[1]):
        first = offs_ref[row, d]
        start = jnp.where(pos >= first, first, start)
    return start


def doc_end(offs_ref, row, pos, length):
    end = jnp.int32(length)
    for d in reversed(range(offs_ref.shape[1])):
        first = offs_ref[row, d]
        end = jnp.where(first > pos, first, end)
    return end


def head_lanes(shape, head, head_dim):
    lane = lax.broadcasted_iota(jnp.int32, shape, 1)
    return (lane >= head * head_dim) & (lane < (head + 1) * head_dim)


def attend_kernel(heads, head_dim, offs_ref, qkv_ref, scale_ref, out_ref, lse_ref, score_ref):
    blocks, _, _, span, width = qkv_ref.shape
    wide = score_ref.shape[-1]
    per = wide // span
    row = pl.program_id(0)
    lanes = min(128, wide)
    score_scale = head_dim ** (-0.5)

    def query_block(i, carry):
        first_pos = i * span
        queries = qkv_ref[i, 0, 0] * jnp.asarray(score_scale, BF16)
        query_head = [
            jnp.where(head_lanes((span, width), h, head_dim), queries, 0).astype(BF16)
            for h in range(heads)
        ]
        query_pos = first_pos + lax.broadcasted_iota(jnp.int32, (span, 1), 0)
        query_start = doc_start(offs_ref, row, query_pos)
        low = doc_start(offs_ref, row, first_pos) // wide
        high = (first_pos + span - 1) // wide + 1

        def score_step(j, tops):
            keys = qkv_ref[pl.ds(j * per, per), 0, 1].reshape(wide, width)
            key_pos = j * wide + lax.broadcasted_iota(jnp.int32, (span, wide), 1)
            allowed = (key_pos >= query_start) & (key_pos <= query_pos)
            new = []
            for h in range(heads):
                scores = jnp.where(allowed, dot_last(query_head[h], keys), MASKED)
                score_ref[h, j] = scores
                top = tops[h]
                for c in range(0, wide, lanes):
                    top = jnp.maximum(top, scores[:, c : c + lanes])
                new.append(top)
            return tuple(new)

        tops = lax.fori_loop(
            low, high, score_step, tuple(jnp.full((span, lanes), MASKED, F32) for h in range(heads))
        )
        tops = [jnp.max(top, axis=1, keepdims=True) for top in tops]

        def value_step(j, state):
            values = qkv_ref[pl.ds(j * per, per), 0, 2].reshape(wide, width)
            new = []
            for h in range(heads):
                total, acc = state[h]
                probs = jnp.exp(score_ref[h, j] - tops[h])
                for c in range(0, wide, lanes):
                    total = total + probs[:, c : c + lanes]
                acc = acc + jnp.dot(probs.astype(BF16), values, preferred_element_type=F32)
                new.append((total, acc))
            return tuple(new)

        state = lax.fori_loop(
            low,
            high,
            value_step,
            tuple(
                (jnp.zeros((span, lanes), F32), jnp.zeros((span, width), F32)) for h in range(heads)
            ),
        )
        result = jnp.zeros((span, width), F32)
        for h in range(heads):
            total = jnp.sum(state[h][0], axis=1, keepdims=True)
            result = jnp.where(head_lanes((span, width), h, head_dim), state[h][1] / total, result)
            log_total = tops[h] + jnp.log(total)
            lse_ref[0, i, h : h + 1, :] = jnp.transpose(jnp.broadcast_to(log_total, (span, 128)))[
                0:1, :
            ]
        out_ref[i, 0] = (result * scale_ref[...]).astype(BF16)
        return carry

    lax.fori_loop(0, blocks, query_block, 0)


def attend(offsets, qkv, scale_lanes, heads, head_dim):
    blocks, rows, _, span, width = qkv.shape
    wide = max(span, min(512, blocks * span))
    grid_spec = pltpu.PrefetchScalarGridSpec(
        num_scalar_prefetch=1,
        grid=(rows,),
        in_specs=[
            pl.BlockSpec((blocks, 1, 3, span, width), lambda r, o: (0, r, 0, 0, 0)),
            pl.BlockSpec((1, width), lambda r, o: (0, 0)),
        ],
        out_specs=[
            pl.BlockSpec((blocks, 1, span, width), lambda r, o: (0, r, 0, 0)),
            pl.BlockSpec((1, blocks, heads, span), lambda r, o: (r, 0, 0, 0)),
        ],
        scratch_shapes=[pltpu.VMEM((heads, blocks * span // wide, span, wide), F32)],
    )
    return pl.pallas_call(
        functools.partial(attend_kernel, heads, head_dim),
        grid_spec=grid_spec,
        out_shape=[
            jax.ShapeDtypeStruct((blocks, rows, span, width), BF16),
            jax.ShapeDtypeStruct((rows, blocks, heads, span), F32),
        ],
        compiler_params=pltpu.CompilerParams(vmem_limit_bytes=VMEM_BYTES),
        name="attend",
    )(offsets, qkv, scale_lanes)


def attend_back_kernel(
    heads,
    head_dim,
    offs_ref,
    qkv_ref,
    grad_ref,
    out_ref,
    inv_ref,
    lse_ref,
    dqkv_ref,
    total_ref,
    q_ref,
    k_ref,
    g_ref,
    delta_ref,
    dq_ref,
):
    blocks, _, _, span, width = qkv_ref.shape
    row = pl.program_id(0)
    score_scale = head_dim ** (-0.5)
    picks = lax.broadcasted_iota(jnp.int32, (8, width), 0)
    lane = lax.broadcasted_iota(jnp.int32, (8, width), 1)
    ones = jnp.where(lane // head_dim == picks, 1.0, 0.0).astype(F32)

    def prepare(i, carry):
        queries = qkv_ref[i, 0, 0] * jnp.asarray(score_scale, BF16)
        keys = qkv_ref[i, 0, 1]
        grads = grad_ref[i, 0]
        for h in range(heads):
            mine = head_lanes((span, width), h, head_dim)
            q_ref[h, i] = jnp.where(mine, queries, 0).astype(BF16)
            k_ref[h, i] = jnp.where(mine, keys, 0).astype(BF16)
            g_ref[h, i] = jnp.where(mine, grads, 0).astype(BF16)
        product = grads.astype(F32) * out_ref[i, 0].astype(F32) * inv_ref[...]
        delta_ref[i] = lax.dot_general(
            ones, product, LAST, precision=lax.Precision.HIGHEST, preferred_element_type=F32
        )
        dq_ref[i] = jnp.zeros((span, width), F32)
        return carry + delta_ref[i]

    total_ref[0] = lax.fori_loop(0, blocks, prepare, jnp.zeros((8, span), F32))

    def key_block(j, carry):
        keys = qkv_ref[j, 0, 1]
        values = qkv_ref[j, 0, 2]
        key_pos = j * span + lax.broadcasted_iota(jnp.int32, (span, 1), 0)
        last = (doc_end(offs_ref, row, (j + 1) * span - 1, blocks * span) - 1) // span + 1

        def query_step(i, state):
            dk, dv = state
            query_pos = i * span + lax.broadcasted_iota(jnp.int32, (1, span), 1)
            query_start = doc_start(offs_ref, row, query_pos)
            allowed = (key_pos >= query_start) & (key_pos <= query_pos)
            dq = dq_ref[i]
            for h in range(heads):
                scores = dot_last(keys, q_ref[h, i])
                scores = jnp.where(allowed, scores - lse_ref[0, i, h : h + 1, :], MASKED)
                probs = jnp.exp(scores)
                d_probs = dot_last(values, g_ref[h, i])
                d_scores = (probs * (d_probs - delta_ref[i, h : h + 1, :])).astype(BF16)
                dv = dv + jnp.dot(probs.astype(BF16), g_ref[h, i], preferred_element_type=F32)
                dk = dk + jnp.dot(d_scores, q_ref[h, i], preferred_element_type=F32)
                dq = dq + dot_first(d_scores, k_ref[h, j])
            dq_ref[i] = dq
            return (dk, dv)

        zero = jnp.zeros((span, width), F32)
        dk, dv = lax.fori_loop(j, last, query_step, (zero, zero))
        dqkv_ref[j, 0, 1] = dk.astype(BF16)
        dqkv_ref[j, 0, 2] = dv.astype(BF16)
        dqkv_ref[j, 0, 0] = (dq_ref[j] * score_scale).astype(BF16)
        return carry

    lax.fori_loop(0, blocks, key_block, 0)


def attend_back(offsets, qkv, grads, scaled, inverse_lanes, lse, heads, head_dim):
    blocks, rows, _, span, width = qkv.shape
    block_spec = pl.BlockSpec((blocks, 1, span, width), lambda r, o: (0, r, 0, 0))
    wide_spec = pl.BlockSpec((blocks, 1, 3, span, width), lambda r, o: (0, r, 0, 0, 0))
    grid_spec = pltpu.PrefetchScalarGridSpec(
        num_scalar_prefetch=1,
        grid=(rows,),
        in_specs=[
            wide_spec,
            block_spec,
            block_spec,
            pl.BlockSpec((1, width), lambda r, o: (0, 0)),
            pl.BlockSpec((1, blocks, heads, span), lambda r, o: (r, 0, 0, 0)),
        ],
        out_specs=[wide_spec, pl.BlockSpec((1, 8, span), lambda r, o: (r, 0, 0))],
        scratch_shapes=[pltpu.VMEM((heads, blocks, span, width), BF16)] * 3
        + [pltpu.VMEM((blocks, 8, span), F32), pltpu.VMEM((blocks, span, width), F32)],
    )
    return pl.pallas_call(
        functools.partial(attend_back_kernel, heads, head_dim),
        grid_spec=grid_spec,
        out_shape=[
            jax.ShapeDtypeStruct(qkv.shape, BF16),
            jax.ShapeDtypeStruct((rows, 8, span), F32),
        ],
        compiler_params=pltpu.CompilerParams(vmem_limit_bytes=VMEM_BYTES),
        name="attend_back",
    )(offsets, qkv, grads, scaled, inverse_lanes, lse)


def exchange(parts):
    return lax.all_to_all(parts, "blk", 0, 0, tiled=True)


def norm_parts(rows_in):
    average = jnp.mean(rows_in, axis=-1, keepdims=True)
    centred = rows_in - average
    spread = lax.rsqrt(jnp.mean(centred * centred, axis=-1, keepdims=True) + EPSILON)
    return centred * spread, spread


def norm_back(hat, spread, gain, grad):
    weighted = grad * gain
    return spread * (
        weighted
        - jnp.mean(weighted, axis=-1, keepdims=True)
        - hat * jnp.mean(weighted * hat, axis=-1, keepdims=True)
    )


def on_device(
    inputs,
    ln_attn,
    w_query,
    w_key,
    w_value,
    w_out,
    head_scale,
    ln_post,
    ln_ffn,
    w_fc1,
    ln_mid,
    w_fc2,
    offsets,
    cotangent,
):
    row_count, span, model_width = inputs.shape
    head_count = head_scale.shape[0]
    head_dim = model_width // head_count
    token_count = row_count * span
    group = lax.axis_size("blk")
    heads = head_count // group
    width = heads * head_dim
    me = lax.axis_index("blk")

    x = inputs.astype(F32).reshape(token_count, model_width)
    x_hat, x_spread = norm_parts(x)
    normed = (x_hat * ln_attn).astype(BF16)

    def project(weight):
        product = jnp.dot(normed, weight, preferred_element_type=F32).astype(BF16)
        return product.reshape(row_count, span, group, width)

    qkv = jnp.stack([project(w_query), project(w_key), project(w_value)], axis=1)
    qkv = exchange(jnp.transpose(qkv, (3, 0, 1, 2, 4)))

    my_scale = lax.dynamic_slice(head_scale, (me * heads,), (heads,))
    scale_lanes = jnp.repeat(my_scale, head_dim).reshape(1, width)
    scaled_mine, lse = attend(offsets, qkv, scale_lanes, heads, head_dim)
    scaled = jnp.transpose(exchange(scaled_mine), (1, 2, 0, 3)).reshape(token_count, model_width)

    d_out = cotangent.reshape(token_count, model_width)
    d_mid = jnp.einsum("td,fd->tf", d_out, w_fc2, preferred_element_type=F32)

    proj = jnp.dot(scaled, w_out, preferred_element_type=F32)
    proj_hat, proj_spread = norm_parts(proj)
    residual = x + proj_hat * ln_post
    res_hat, res_spread = norm_parts(residual)
    ffn_in = (res_hat * ln_ffn).astype(BF16)
    pre = jnp.dot(ffn_in, w_fc1, preferred_element_type=F32)
    phi = 0.5 + 0.5 * lax.erf(pre * (0.5**0.5))
    act = pre * phi
    act_slope = phi + pre * jnp.exp(-0.5 * pre * pre) * 0.3989422804014327
    act_hat, act_spread = norm_parts(act)
    mid = (act_hat * ln_mid).astype(BF16)
    layer_out = (residual + jnp.dot(mid, w_fc2, preferred_element_type=F32)).astype(BF16)

    grad_fc2 = jnp.einsum("tf,td->fd", mid, d_out, preferred_element_type=F32).astype(BF16)
    grad_ln_mid = jnp.sum(d_mid * act_hat, axis=0)
    d_pre = (norm_back(act_hat, act_spread, ln_mid, d_mid) * act_slope).astype(BF16)
    grad_fc1 = jnp.einsum("td,tf->df", ffn_in, d_pre, preferred_element_type=F32).astype(BF16)
    d_ffn = jnp.einsum("tf,df->td", d_pre, w_fc1, preferred_element_type=F32)
    grad_ln_ffn = jnp.sum(d_ffn * res_hat, axis=0)
    d_residual = d_out.astype(F32) + norm_back(res_hat, res_spread, ln_ffn, d_ffn)
    grad_ln_post = jnp.sum(d_residual * proj_hat, axis=0)
    d_proj = norm_back(proj_hat, proj_spread, ln_post, d_residual).astype(BF16)
    grad_out = jnp.einsum("td,te->de", scaled, d_proj, preferred_element_type=F32).astype(BF16)
    d_scaled = jnp.einsum("te,de->td", d_proj, w_out, preferred_element_type=F32)
    d_attn = (d_scaled * jnp.repeat(head_scale, head_dim)).astype(BF16)
    d_attn = jnp.transpose(d_attn.reshape(row_count, span, group, width), (2, 0, 1, 3))
    d_attn = exchange(d_attn)

    dqkv, delta_sums = attend_back(
        offsets, qkv, d_attn, scaled_mine, 1.0 / scale_lanes, lse, heads, head_dim
    )
    my_grad = jnp.sum(delta_sums, axis=(0, 2))[:heads] / my_scale
    grad_scale = lax.dynamic_update_slice(jnp.zeros((head_count,), F32), my_grad, (me * heads,))
    dqkv = exchange(dqkv)
    dqkv = jnp.transpose(dqkv, (2, 1, 3, 0, 4)).reshape(3, token_count, model_width)

    def weight_grad(d_part):
        return jnp.einsum("td,te->de", normed, d_part, preferred_element_type=F32).astype(BF16)

    grads_qkv = [weight_grad(dqkv[n]) for n in range(3)]
    d_normed = sum(
        jnp.einsum("te,de->td", dqkv[n], weight, preferred_element_type=F32)
        for n, weight in enumerate((w_query, w_key, w_value))
    )
    grad_ln_attn = jnp.sum(d_normed * x_hat, axis=0)
    grad_inputs = d_residual + norm_back(x_hat, x_spread, ln_attn, d_normed)

    def reduced(part):
        return lax.psum_scatter(part.astype(BF16), "blk", scatter_dimension=0, tiled=True)

    sums = lax.psum(
        tuple(
            reduced(part)
            for part in (
                grad_ln_attn,
                grads_qkv[0],
                grads_qkv[1],
                grads_qkv[2],
                grad_out,
                grad_ln_post,
                grad_ln_ffn,
                grad_fc1,
                grad_ln_mid,
                grad_fc2,
            )
        ),
        "batch",
    )
    sums = [part.astype(F32) for part in sums]
    grad_scale = lax.psum(grad_scale, ("batch", "blk"))
    return (
        layer_out.reshape(row_count, span, model_width),
        grad_inputs.reshape(row_count, span, model_width),
        sums[0],
        sums[1],
        sums[2],
        sums[3],
        sums[4],
        grad_scale,
        sums[5],
        sums[6],
        sums[7],
        sums[8],
        sums[9],
    )


def solution(mesh):
    rows = P("batch", "blk", None)
    shard = P("blk", None)
    return jax.shard_map(
        on_device,
        mesh=mesh,
        in_specs=(rows,) + (P(),) * 11 + (P("batch", None), rows),
        out_specs=(
            rows,
            rows,
            P("blk"),
            shard,
            shard,
            shard,
            shard,
            P(),
            P("blk"),
            P("blk"),
            shard,
            P("blk"),
            shard,
        ),
        check_vma=False,
    )
```

```python
import functools

import jax
import jax.numpy as jnp
from jax import lax
from jax.experimental import pallas as pl
from jax.experimental.pallas import tpu as pltpu
from jax.sharding import PartitionSpec as P

EPSILON = 1e-05
MASKED = -1e30
VMEM_BYTES = 50 * 1024 * 1024
COST_UNIT = 1.1e9
F32 = jnp.float32
BF16 = jnp.bfloat16
LAST = (((1,), (1,)), ((), ()))
FIRST = (((0,), (0,)), ((), ()))
SMEM = pl.BlockSpec(memory_space=pltpu.SMEM)
VMEM = pl.BlockSpec(memory_space=pltpu.VMEM)


def dot_last(left, right):
    return lax.dot_general(left, right, LAST, preferred_element_type=F32)


def dot_first(left, right):
    return lax.dot_general(left, right, FIRST, preferred_element_type=F32)


def dot(left, right):
    return jnp.dot(left, right, preferred_element_type=F32)


def kernel_params():
    return pltpu.CompilerParams(vmem_limit_bytes=VMEM_BYTES)


def cost(micros):
    return pl.CostEstimate(flops=int(micros * COST_UNIT), bytes_accessed=1024, transcendentals=0)


def exchange(parts):
    return lax.all_to_all(parts, "blk", 0, 0, tiled=True)


def norm_parts(rows_in):
    average = jnp.mean(rows_in, axis=-1, keepdims=True)
    centred = rows_in - average
    spread = lax.rsqrt(jnp.mean(centred * centred, axis=-1, keepdims=True) + EPSILON)
    return centred * spread, spread


def norm_back(hat, spread, gain, grad):
    weighted = grad * gain
    return spread * (
        weighted
        - jnp.mean(weighted, axis=-1, keepdims=True)
        - hat * jnp.mean(weighted * hat, axis=-1, keepdims=True)
    )


def project_kernel(x_ref, gain_ref, wq_ref, wk_ref, wv_ref, normed_ref, out_ref):
    group, _, _, width = out_ref.shape
    hat, _ = norm_parts(x_ref[...].astype(F32))
    normed = (hat * gain_ref[...]).astype(BF16)
    normed_ref[...] = normed
    for n, weight in enumerate((wq_ref, wk_ref, wv_ref)):
        product = dot(normed, weight[...]).astype(BF16)
        for s in range(group):
            out_ref[s, n] = product[:, s * width : (s + 1) * width]


def project(x_row, gain, w_query, w_key, w_value, group):
    span, model = x_row.shape
    return pl.pallas_call(
        project_kernel,
        out_shape=[
            jax.ShapeDtypeStruct((span, model), BF16),
            jax.ShapeDtypeStruct((group, 3, span, model // group), BF16),
        ],
        compiler_params=kernel_params(),
        cost_estimate=cost(5),
        name="project",
    )(x_row, gain, w_query, w_key, w_value)


def doc_start(offs_ref, row, pos):
    start = jnp.zeros_like(pos)
    for d in range(offs_ref.shape[1]):
        first = offs_ref[row, d]
        start = jnp.where(pos >= first, first, start)
    return start


def doc_end(offs_ref, row, pos, length):
    end = jnp.int32(length)
    for d in reversed(range(offs_ref.shape[1])):
        first = offs_ref[row, d]
        end = jnp.where(first > pos, first, end)
    return end


def head_lanes(shape, head, head_dim):
    lane = lax.broadcasted_iota(jnp.int32, shape, 1)
    return (lane >= head * head_dim) & (lane < (head + 1) * head_dim)


def attend_kernel(rows, heads, head_dim, offs_ref, scale_ref, *refs):
    count = len(rows)
    result_ref, lse_ref, score_ref = refs[count:]
    for n, row in enumerate(rows):
        attend_row(
            row,
            heads,
            head_dim,
            offs_ref,
            scale_ref,
            refs[n],
            result_ref.at[:, n],
            lse_ref.at[n],
            score_ref,
        )


def attend_row(
    row, heads, head_dim, offs_ref, scale_ref, held, result_ref, lse_ref, score_ref
):
    blocks, _, span, width = held.shape
    wide = score_ref.shape[-1]
    per = wide // span
    lanes = min(128, wide)
    score_scale = head_dim ** (-0.5)

    def query_block(i, carry):
        first_pos = i * span
        queries = held[i, 0] * jnp.asarray(score_scale, BF16)
        query_head = [
            jnp.where(head_lanes((span, width), h, head_dim), queries, 0).astype(BF16)
            for h in range(heads)
        ]
        query_pos = first_pos + lax.broadcasted_iota(jnp.int32, (span, 1), 0)
        query_start = doc_start(offs_ref, row, query_pos)
        low = doc_start(offs_ref, row, first_pos) // wide
        high = (first_pos + span - 1) // wide + 1

        def score_step(j, tops):
            keys = held[pl.ds(j * per, per), 1].reshape(wide, width)
            key_pos = j * wide + lax.broadcasted_iota(jnp.int32, (span, wide), 1)
            allowed = (key_pos >= query_start) & (key_pos <= query_pos)
            new = []
            for h in range(heads):
                scores = jnp.where(allowed, dot_last(query_head[h], keys), MASKED)
                score_ref[h, j] = scores
                top = tops[h]
                for c in range(0, wide, lanes):
                    top = jnp.maximum(top, scores[:, c : c + lanes])
                new.append(top)
            return tuple(new)

        tops = lax.fori_loop(
            low, high, score_step, tuple(jnp.full((span, lanes), MASKED, F32) for h in range(heads))
        )
        tops = [jnp.max(top, axis=1, keepdims=True) for top in tops]

        def value_step(j, state):
            values = held[pl.ds(j * per, per), 2].reshape(wide, width)
            new = []
            for h in range(heads):
                total, acc = state[h]
                probs = jnp.exp(score_ref[h, j] - tops[h])
                for c in range(0, wide, lanes):
                    total = total + probs[:, c : c + lanes]
                acc = acc + dot(probs.astype(BF16), values)
                new.append((total, acc))
            return tuple(new)

        state = lax.fori_loop(
            low,
            high,
            value_step,
            tuple(
                (jnp.zeros((span, lanes), F32), jnp.zeros((span, width), F32)) for h in range(heads)
            ),
        )
        result = jnp.zeros((span, width), F32)
        for h in range(heads):
            total = jnp.sum(state[h][0], axis=1, keepdims=True)
            result = jnp.where(head_lanes((span, width), h, head_dim), state[h][1] / total, result)
            log_total = tops[h] + jnp.log(total)
            lse_ref[i, h : h + 1, :] = jnp.transpose(jnp.broadcast_to(log_total, (span, 128)))[
                0:1, :
            ]
        result_ref[i] = (result * scale_ref[...]).astype(BF16)
        return carry

    lax.fori_loop(0, blocks, query_block, 0)


def attend(offsets, rows, qkv, scale_lanes, heads, head_dim):
    group, _, span, width = qkv[0].shape
    length = group * span
    wide = max(span, min(512, length))
    return pl.pallas_call(
        functools.partial(attend_kernel, rows, heads, head_dim),
        in_specs=[SMEM, VMEM] + [VMEM] * len(rows),
        out_shape=[
            jax.ShapeDtypeStruct((group, len(rows), span, width), BF16),
            jax.ShapeDtypeStruct((len(rows), group, heads, span), F32),
        ],
        scratch_shapes=[pltpu.VMEM((heads, length // wide, span, wide), F32)],
        compiler_params=kernel_params(),
        cost_estimate=cost(16),
        name="attend",
    )(offsets, scale_lanes, *qkv)


def attend_back_kernel(rows, heads, head_dim, offs_ref, inv_ref, grad_ref, *refs):
    count = len(rows)
    held, out_refs, lse_refs = refs[:count], refs[count : 2 * count], refs[2 * count : 3 * count]
    dqkv_ref, total_ref = refs[3 * count : 3 * count + 2]
    for n, row in enumerate(rows):
        attend_back_row(
            row,
            heads,
            head_dim,
            offs_ref,
            inv_ref,
            lse_refs[n],
            held[n],
            grad_ref.at[:, n],
            out_refs[n],
            dqkv_ref.at[:, n],
            total_ref.at[n],
            *refs[3 * count + 2 :],
        )


def attend_back_row(
    row,
    heads,
    head_dim,
    offs_ref,
    inv_ref,
    lse_ref,
    held,
    grad_ref,
    out_ref,
    dqkv_ref,
    total_ref,
    q_ref,
    k_ref,
    g_ref,
    delta_ref,
    dq_ref,
):
    blocks, _, span, width = held.shape
    score_scale = head_dim ** (-0.5)
    picks = lax.broadcasted_iota(jnp.int32, (8, width), 0)
    lane = lax.broadcasted_iota(jnp.int32, (8, width), 1)
    ones = jnp.where(lane // head_dim == picks, 1.0, 0.0).astype(F32)

    def prepare(i, carry):
        queries = held[i, 0] * jnp.asarray(score_scale, BF16)
        keys = held[i, 1]
        grads = grad_ref[i]
        for h in range(heads):
            mine = head_lanes((span, width), h, head_dim)
            q_ref[h, i] = jnp.where(mine, queries, 0).astype(BF16)
            k_ref[h, i] = jnp.where(mine, keys, 0).astype(BF16)
            g_ref[h, i] = jnp.where(mine, grads, 0).astype(BF16)
        product = grads.astype(F32) * out_ref[i].astype(F32) * inv_ref[...]
        delta_ref[i] = lax.dot_general(
            ones, product, LAST, precision=lax.Precision.HIGHEST, preferred_element_type=F32
        )
        dq_ref[i] = jnp.zeros((span, width), F32)
        return carry + delta_ref[i]

    total_ref[...] = lax.fori_loop(0, blocks, prepare, jnp.zeros((8, span), F32))

    def key_block(j, carry):
        keys = held[j, 1]
        values = held[j, 2]
        key_pos = j * span + lax.broadcasted_iota(jnp.int32, (span, 1), 0)
        last = (doc_end(offs_ref, row, (j + 1) * span - 1, blocks * span) - 1) // span + 1

        def query_step(i, state):
            dk, dv = state
            query_pos = i * span + lax.broadcasted_iota(jnp.int32, (1, span), 1)
            query_start = doc_start(offs_ref, row, query_pos)
            allowed = (key_pos >= query_start) & (key_pos <= query_pos)
            dq = dq_ref[i]
            for h in range(heads):
                scores = dot_last(keys, q_ref[h, i])
                scores = jnp.where(allowed, scores - lse_ref[i, h : h + 1, :], MASKED)
                probs = jnp.exp(scores)
                d_probs = dot_last(values, g_ref[h, i])
                d_scores = (probs * (d_probs - delta_ref[i, h : h + 1, :])).astype(BF16)
                dv = dv + dot(probs.astype(BF16), g_ref[h, i])
                dk = dk + dot(d_scores, q_ref[h, i])
                dq = dq + dot_first(d_scores, k_ref[h, j])
            dq_ref[i] = dq
            return (dk, dv)

        zero = jnp.zeros((span, width), F32)
        dk, dv = lax.fori_loop(j, last, query_step, (zero, zero))
        dqkv_ref[j, 1] = dk.astype(BF16)
        dqkv_ref[j, 2] = dv.astype(BF16)
        dqkv_ref[j, 0] = (dq_ref[j] * score_scale).astype(BF16)
        return carry

    lax.fori_loop(0, blocks, key_block, 0)


def attend_back(offsets, rows, qkv, grads, scaled, inverse_lanes, lse, heads, head_dim):
    group, _, span, width = qkv[0].shape
    count = len(rows)
    return pl.pallas_call(
        functools.partial(attend_back_kernel, rows, heads, head_dim),
        in_specs=[SMEM] + [VMEM] * (2 + 3 * count),
        out_shape=[
            jax.ShapeDtypeStruct((group, count, 3, span, width), BF16),
            jax.ShapeDtypeStruct((count, 8, span), F32),
        ],
        scratch_shapes=[pltpu.VMEM((heads, group, span, width), BF16)] * 3
        + [pltpu.VMEM((group, 8, span), F32), pltpu.VMEM((group, span, width), F32)],
        compiler_params=kernel_params(),
        cost_estimate=cost(26),
        name="attend_back",
    )(offsets, inverse_lanes, grads, *qkv, *scaled, *lse)


def join_grads_kernel(parts, in_ref, out_ref):
    group = in_ref.shape[0]
    for n in range(3):
        whole = jnp.concatenate([in_ref[s, 0, n] for s in range(group)], axis=1)
        piece = whole.shape[1] // parts
        for p in range(parts):
            to = (p * 3 + n) * piece
            out_ref[:, to : to + piece] = whole[:, p * piece : (p + 1) * piece]


def join_grads(block):
    group, _, _, span, width = block.shape
    return pl.pallas_call(
        functools.partial(join_grads_kernel, PARTS),
        out_shape=jax.ShapeDtypeStruct((span, 3 * group * width), BF16),
        compiler_params=kernel_params(),
        cost_estimate=cost(1.5),
        name="join_grads",
    )(block)


FF_STEP = 512


def layer_kernel(
    o_ref,
    x_ref,
    d_out_ref,
    post_ref,
    ffn_ref,
    mid_gain_ref,
    scale_ref,
    w_out_ref,
    d_mid_hbm,
    w_fc1_hbm,
    scaled_ref,
    ffn_in_ref,
    residual_ref,
    mid_ref,
    d_pre_ref,
    d_proj_ref,
    d_residual_ref,
    d_attn_ref,
    g_post_ref,
    g_ffn_ref,
    g_mid_ref,
    d_mid_ref,
    w_fc1_ref,
    act_ref,
    slope_ref,
    sems,
    *,
    row,
):
    group, _, span, width = o_ref.shape
    hidden = act_ref.shape[1]
    steps = [slice(c, c + FF_STEP) for c in range(0, hidden, FF_STEP)]
    weight_copies = [
        pltpu.make_async_copy(w_fc1_hbm.at[:, at], w_fc1_ref.at[:, at], sems.at[c])
        for c, at in enumerate(steps)
    ]
    mid_copy = pltpu.make_async_copy(
        d_mid_hbm.at[row * span : (row + 1) * span, :], d_mid_ref, sems.at[len(steps)]
    )
    for copy in weight_copies:
        copy.start()
    mid_copy.start()

    scaled = jnp.concatenate([o_ref[s, 0] for s in range(group)], axis=1)
    scaled_ref[...] = scaled
    proj_hat, proj_spread = norm_parts(dot(scaled, w_out_ref[...]))
    residual = x_ref[...].astype(F32) + proj_hat * post_ref[...]
    residual_ref[...] = residual
    res_hat, res_spread = norm_parts(residual)
    ffn_in = (res_hat * ffn_ref[...]).astype(BF16)
    ffn_in_ref[...] = ffn_in

    total = jnp.zeros((span, 1), F32)
    for c, at in enumerate(steps):
        weight_copies[c].wait()
        pre = dot(ffn_in, w_fc1_ref[:, at])
        phi = 0.5 + 0.5 * lax.erf(pre * (0.5**0.5))
        act = pre * phi
        act_ref[:, at] = act
        slope_ref[:, at] = phi + pre * jnp.exp(-0.5 * pre * pre) * 0.3989422804014327
        total += jnp.sum(act, axis=1, keepdims=True)
    average = total / hidden
    total = jnp.zeros((span, 1), F32)
    for at in steps:
        centred = act_ref[:, at] - average
        total += jnp.sum(centred * centred, axis=1, keepdims=True)
    spread = lax.rsqrt(total / hidden + EPSILON)

    mid_copy.wait()
    sum_weighted = jnp.zeros((span, 1), F32)
    sum_hat = jnp.zeros((span, 1), F32)
    for at in steps:
        hat = (act_ref[:, at] - average) * spread
        act_ref[:, at] = hat
        gain = mid_gain_ref[:, at]
        mid_ref[:, at] = (hat * gain).astype(BF16)
        grad = d_mid_ref[:, at]
        product = grad * hat
        g_mid_ref[:, at] = jnp.sum(product, axis=0, keepdims=True)
        sum_weighted += jnp.sum(grad * gain, axis=1, keepdims=True)
        sum_hat += jnp.sum(product * gain, axis=1, keepdims=True)
    sum_weighted = sum_weighted / hidden
    sum_hat = sum_hat / hidden
    d_ffn = jnp.zeros(x_ref.shape, F32)
    for at in steps:
        weighted = d_mid_ref[:, at] * mid_gain_ref[:, at]
        d_act = spread * (weighted - sum_weighted - act_ref[:, at] * sum_hat)
        d_pre = (d_act * slope_ref[:, at]).astype(BF16)
        d_pre_ref[:, at] = d_pre
        d_ffn += dot_last(d_pre, w_fc1_ref[:, at])

    g_ffn_ref[...] = jnp.sum(d_ffn * res_hat, axis=0, keepdims=True)
    d_residual = d_out_ref[...].astype(F32) + norm_back(res_hat, res_spread, ffn_ref[...], d_ffn)
    d_residual_ref[...] = d_residual
    g_post_ref[...] = jnp.sum(d_residual * proj_hat, axis=0, keepdims=True)
    d_proj = norm_back(proj_hat, proj_spread, post_ref[...], d_residual).astype(BF16)
    d_proj_ref[...] = d_proj
    d_attn = (dot_last(d_proj, w_out_ref[...]) * scale_ref[...]).astype(BF16)
    for s in range(group):
        d_attn_ref[s, 0] = d_attn[:, s * width : (s + 1) * width]


def layer(row, o_blocks, x_row, d_out_row, gains, w_out, d_mid, w_fc1):
    span, model = x_row.shape
    hidden = w_fc1.shape[1]
    shape = jax.ShapeDtypeStruct
    return pl.pallas_call(
        functools.partial(layer_kernel, row=row),
        in_specs=[VMEM] * 8 + [pl.BlockSpec(memory_space=pl.ANY)] * 2,
        out_shape=[
            shape((span, model), BF16),
            shape((span, model), BF16),
            shape((span, model), F32),
            shape((span, hidden), BF16),
            shape((span, hidden), BF16),
            shape((span, model), BF16),
            shape((span, model), F32),
            shape(o_blocks.shape, BF16),
            shape((1, model), F32),
            shape((1, model), F32),
            shape((1, hidden), F32),
        ],
        scratch_shapes=[
            pltpu.VMEM((span, hidden), F32),
            pltpu.VMEM(w_fc1.shape, BF16),
            pltpu.VMEM((span, hidden), F32),
            pltpu.VMEM((span, hidden), F32),
            pltpu.SemaphoreType.DMA((hidden // FF_STEP + 1,)),
        ],
        compiler_params=kernel_params(),
        cost_estimate=cost(16),
        name="layer",
    )(o_blocks, x_row, d_out_row, *gains, w_out, d_mid, w_fc1)


def layer_out_kernel(*refs):
    count = (len(refs) - 2) // 2
    weight, out_ref = refs[-2], refs[-1]
    for r in range(count):
        out_ref[r] = (refs[r][...] + dot(refs[count + r][...], weight[...])).astype(BF16)


def last_step(residuals, mids, w_fc2):
    return pl.pallas_call(
        layer_out_kernel,
        out_shape=jax.ShapeDtypeStruct((len(mids),) + residuals[0].shape, BF16),
        compiler_params=kernel_params(),
        cost_estimate=cost(13),
        name="layer_out",
    )(*residuals, *mids, w_fc2)


def flip(value, axis, bit):
    size = lax.axis_size(axis)
    return lax.ppermute(value, axis, [(i, i ^ (1 << bit)) for i in range(size)])


def bits(axis):
    return (lax.axis_size(axis) - 1).bit_length()


def add(left, right):
    return (left.astype(F32) + right.astype(F32)).astype(BF16)


def sum_small(value):
    for axis in ("batch", "blk"):
        for bit in range(bits(axis)):
            value = value + flip(value, axis, bit)
    return value


PARTS = 4


def weight_kernel(count, rows, added, part_ref, *refs):
    out_ref = refs[-1]
    extras = refs[2 * count * rows : 2 * count * rows + added]
    at = 0
    for n in range(count):
        lefts = refs[2 * n * rows : (2 * n + 1) * rows]
        rights = refs[(2 * n + 1) * rows : (2 * n + 2) * rows]
        width = rights[0].shape[1]
        total = sum(dot_first(left[...], right[...]) for left, right in zip(lefts, rights))
        for extra in extras:
            total = total + extra[0, :, at : at + width].astype(F32)
        out_ref[0, :, at : at + width] = total.astype(BF16)
        at += width


def weight_part_plain(pairs, part, extras, group):
    pieces = []
    for lefts, rights, kind in pairs:
        left, right = jnp.concatenate(lefts), jnp.concatenate(rights)
        if kind == "columns":
            wide = right.shape[1] // PARTS
            right = lax.dynamic_slice(right, (0, part * wide), (right.shape[0], wide))
            left = left.reshape(left.shape[0], group, -1)
        else:
            left = left.reshape(left.shape[0], group, PARTS, -1)
            left = lax.dynamic_index_in_dim(left, part, 2, keepdims=False)
        pieces.append(jnp.einsum("tsd,te->sde", left, right, preferred_element_type=F32))
    total = jnp.concatenate(pieces, axis=2)
    for extra in extras:
        total = total + extra.astype(F32)
    return total.astype(BF16)


def weight_part(pairs, part, extras, group):
    specs, width = [], 0
    for lefts, rights, kind in pairs:
        span, model = lefts[0].shape
        if kind == "columns":
            high, wide = model // group, rights[0].shape[1] // PARTS
            left_spec = pl.BlockSpec((span, high), lambda s, p: (0, s))
            right_spec = pl.BlockSpec((span, wide), lambda s, p: (0, p[0]))
        else:
            high, wide = model // group // PARTS, rights[0].shape[1]
            left_spec = pl.BlockSpec((span, high), lambda s, p: (0, s * PARTS + p[0]))
            right_spec = pl.BlockSpec((span, wide), lambda s, p: (0, 0))
        specs += [left_spec] * len(lefts) + [right_spec] * len(rights)
        width += wide
    if high % 128:
        return weight_part_plain(pairs, part, extras, group)
    block = pl.BlockSpec((1, high, width), lambda s, p: (s, 0, 0))
    arrays = [array for lefts, rights, _ in pairs for array in (*lefts, *rights)]
    return pl.pallas_call(
        functools.partial(weight_kernel, len(pairs), len(pairs[0][0]), len(extras)),
        grid_spec=pltpu.PrefetchScalarGridSpec(
            num_scalar_prefetch=1,
            grid=(group,),
            in_specs=specs + [block] * len(extras),
            out_specs=block,
        ),
        out_shape=jax.ShapeDtypeStruct((group, high, width), BF16),
        compiler_params=kernel_params(),
        cost_estimate=cost(7.5),
        name="weight_part",
    )(part.astype(jnp.int32).reshape(1), *arrays, *extras)


class WeightSum:
    def __init__(self, order, *pairs):
        self.order, self.pairs = order, pairs
        batch_at = lax.axis_index("batch")
        self.near, self.far = batch_at & 1, (batch_at >> 1) & 1

    def piece(self, near, far, *extras):
        def part_of(part):
            return weight_part(self.pairs, part, extras, lax.axis_size("blk"))

        return self.order(part_of, near * 2 + far)

    def away_far(self):
        self.first = flip(self.piece(1 - self.near, 1 - self.far), "batch", 0)

    def send_far(self):
        self.arrived = flip(self.piece(self.near, 1 - self.far, self.first), "batch", 1)

    def away_near(self):
        self.second = flip(self.piece(1 - self.near, self.far), "batch", 0)

    def keep(self):
        return self.piece(self.near, self.far, self.second, self.arrived)


class Order:
    def __init__(self):
        self.last = ()

    def __call__(self, step, *values):
        self.last = step(*tie(values, self.last))
        return self.last


def tie(values, *after):
    return lax.optimization_barrier((values, after))[0]


def halve(mine, bit):
    at = (lax.axis_index("blk") >> bit) & 1
    halves = mine.reshape((-1, 2) + mine.shape[1:])
    keep = lax.dynamic_index_in_dim(halves, at, 1, keepdims=False)
    send = lax.dynamic_index_in_dim(halves, 1 - at, 1, keepdims=False)
    return add(keep, flip(send, "blk", bit))


def halve_rest(mine, start):
    batch_at = lax.axis_index("batch")
    near, far = batch_at & 1, (batch_at >> 1) & 1
    for bit in range(start, bits("blk")):
        mine = halve(mine, bit)
    mine = mine[0]
    for bit in range(2, bits("batch")):
        mine = add(mine, flip(mine, "batch", bit))
    other = flip(mine, "batch", 1)
    pair = jnp.stack([jnp.where(far == 0, mine, other), jnp.where(far == 0, other, mine)])
    away = flip(pair, "batch", 0)
    first = jnp.where(near == 0, pair, away).astype(F32)
    second = jnp.where(near == 0, away, pair).astype(F32)
    return [first[0], first[1], second[0], second[1]]


def input_grad_kernel(parts, rows, x_ref, gain_ref, wq_ref, wk_ref, wv_ref, *refs):
    out_ref, sum_ref = refs[2 * rows :]
    model = wq_ref.shape[0]
    piece = model // parts
    total = jnp.zeros(sum_ref.shape, F32)
    for r in range(rows):
        d_ref, res_ref = refs[r], refs[rows + r]
        grad = jnp.zeros(res_ref.shape, F32)
        for p in range(parts):
            for n, weight in enumerate((wq_ref, wk_ref, wv_ref)):
                at = (p * 3 + n) * piece
                grad += dot_last(d_ref[:, at : at + piece], weight[:, p * piece : (p + 1) * piece])
        hat, spread = norm_parts(x_ref[r].astype(F32))
        out_ref[r] = res_ref[...] + norm_back(hat, spread, gain_ref[...], grad)
        total += jnp.sum(grad * hat, axis=0, keepdims=True)
    sum_ref[...] = total


def input_grad(x, gain, w_query, w_key, w_value, d_rows, d_residuals):
    return pl.pallas_call(
        functools.partial(input_grad_kernel, PARTS, len(d_rows)),
        out_shape=[
            jax.ShapeDtypeStruct(x.shape, F32),
            jax.ShapeDtypeStruct((1, x.shape[2]), F32),
        ],
        compiler_params=kernel_params(),
        cost_estimate=cost(13),
        name="input_grad",
    )(x, gain, w_query, w_key, w_value, *d_rows, *d_residuals)


def on_device(
    inputs,
    ln_attn,
    w_query,
    w_key,
    w_value,
    w_out,
    head_scale,
    ln_post,
    ln_ffn,
    w_fc1,
    ln_mid,
    w_fc2,
    offsets,
    cotangent,
):
    row_count, span, model = inputs.shape
    head_count = head_scale.shape[0]
    head_dim = model // head_count
    tokens = row_count * span
    group = lax.axis_size("blk")
    heads = head_count // group
    width = heads * head_dim
    my_index = lax.axis_index("blk")
    rows = range(row_count)

    order = Order()
    gain = ln_attn.reshape(1, model)
    normed, qkv = [], []
    for r in rows:

        def project_row(x_row):
            return project(x_row, gain, w_query, w_key, w_value, group)

        normed_row, sent = order(project_row, inputs[r])
        normed.append(normed_row)
        qkv.append(exchange(tie(sent, qkv[-1:])))

    def middle_grad(grad, _):
        return jnp.einsum("td,fd->tf", grad, w_fc2, preferred_element_type=F32)

    d_mid = order(middle_grad, cotangent.reshape(tokens, model), qkv[0])

    my_scale = lax.dynamic_slice(head_scale, (my_index * heads,), (heads,))
    scale_lanes = jnp.repeat(my_scale, head_dim).reshape(1, width)
    scaled_mine, lse = [], []
    for r in rows:

        def attend_one(held):
            return attend(offsets, [r], [held], scale_lanes, heads, head_dim)

        out, log_total = order(attend_one, qkv[r])
        scaled_mine.append(out)
        lse.append(log_total)
    early = exchange(tie(jnp.concatenate(scaled_mine[:-1], axis=1), qkv[-1]))
    late = exchange(tie(scaled_mine[-1], early))

    layer_gains = [
        ln_post.reshape(1, model),
        ln_ffn.reshape(1, model),
        ln_mid.reshape(1, -1),
        jnp.repeat(head_scale, head_dim).reshape(1, model),
    ]
    layers = []
    for r in rows:

        def layer_row(o_blocks):
            return layer(
                r, o_blocks, inputs[r], cotangent[r], layer_gains, w_out, d_mid, w_fc1
            )

        layers.append(order(layer_row, early[:, r : r + 1] if r < row_count - 1 else late))
    (
        scaled,
        ffn_in,
        residual,
        mid,
        d_pre,
        d_proj,
        d_residual,
        d_attn,
        g_post,
        g_ffn,
        g_mid,
    ) = zip(*layers)
    first_heads = exchange(tie(d_attn[0], late))
    rest_heads = exchange(tie(jnp.concatenate(d_attn[1:], axis=1), first_heads))
    d_out = [cotangent[r] for r in rows]

    totals, sent = [], []

    def back(r, row_heads):
        def back_row(held, grads):
            return attend_back(
                offsets,
                [r],
                [held],
                grads,
                [scaled_mine[r].reshape(group, span, width)],
                1.0 / scale_lanes,
                [lse[r].reshape(lse[r].shape[1:])],
                heads,
                head_dim,
            )

        out, total = order(back_row, qkv[r], row_heads)
        totals.append(total)
        sent.append(out)

    sum_fc2 = WeightSum(order, (mid, d_out, "rows"))
    sum_rest = WeightSum(order, (ffn_in, d_pre, "columns"), (scaled, d_proj, "columns"))
    back(0, first_heads)
    grads = [exchange(tie(sent[0], rest_heads))]
    sum_fc2.away_far()
    sum_rest.away_far()
    sum_fc2.send_far()
    sum_rest.send_far()
    for r in rows[1:]:
        back(r, rest_heads[:, r - 1 : r])
        grads.append(exchange(tie(sent[r], grads)))
    sum_fc2.away_near()
    sum_rest.away_near()
    mine_fc2 = halve(sum_fc2.keep(), 0)
    mine_rest = halve(sum_rest.keep(), 0)
    d_rows = [order(join_grads, part) for part in grads]
    sum_qkv = WeightSum(order, (normed, d_rows, "columns"))
    sum_qkv.away_far()
    sum_qkv.away_near()
    sum_qkv.send_far()

    def input_step(x):
        return input_grad(x, gain, w_query, w_key, w_value, d_rows, d_residual)

    grad_inputs, grad_ln_attn = order(input_step, inputs)

    def output_step(weight):
        return last_step(residual, mid, weight)

    layer_out = order(output_step, w_fc2)
    mine_qkv = sum_qkv.keep()
    grads_ffn = halve_rest(tie(jnp.concatenate([mine_fc2, mine_rest], axis=2), d_rows), 1)
    grads_qkv = halve_rest(mine_qkv, 0)
    delta_sum = sum(jnp.sum(total, axis=(0, 2)) for total in totals)
    my_grad = delta_sum[:heads] / my_scale
    scale_part = lax.dynamic_update_slice(
        jnp.zeros((head_count,), F32), my_grad, (my_index * heads,)
    )
    gains = sum_small(
        jnp.concatenate(
            [grad_ln_attn[0], sum(g_post)[0], sum(g_ffn)[0], sum(g_mid)[0], scale_part]
        )
    )
    ends = [0, model, 2 * model, 3 * model, 3 * model + ln_mid.shape[0]]
    ends.append(ends[-1] + head_count)
    gains = [gains[low:high] for low, high in zip(ends[:-1], ends[1:])]

    def shard_of(vector):
        part = vector.shape[0] // group
        return lax.dynamic_slice(vector, (my_index * part,), (part,))

    def whole(parts, start, width, axis=1):
        return jnp.concatenate([part[:, start : start + width] for part in parts], axis=axis)

    piece = model // PARTS
    ff_piece = w_fc1.shape[1] // PARTS
    return (
        layer_out,
        grad_inputs,
        shard_of(gains[0]),
        whole(grads_qkv, 0, piece),
        whole(grads_qkv, piece, piece),
        whole(grads_qkv, 2 * piece, piece),
        whole(grads_ffn, model + ff_piece, piece),
        gains[4],
        shard_of(gains[1]),
        shard_of(gains[2]),
        whole(grads_ffn, model, ff_piece),
        shard_of(gains[3]),
        whole(grads_ffn, 0, model, 0),
    )


def solution(mesh):
    rows = P("batch", "blk", None)
    shard = P("blk", None)
    return jax.shard_map(
        on_device,
        mesh=mesh,
        in_specs=(rows,) + (P(),) * 11 + (P("batch", None), rows),
        out_specs=(
            rows,
            rows,
            P("blk"),
            shard,
            shard,
            shard,
            shard,
            P(),
            P("blk"),
            P("blk"),
            shard,
            P("blk"),
            shard,
        ),
        check_vma=False,
    )
```

```python
import functools

import jax
import jax.numpy as jnp
from jax import lax
from jax.experimental import pallas as pl
from jax.experimental.pallas import tpu as pltpu
from jax.sharding import PartitionSpec as P

EPSILON = 1e-05
MASKED = -1e30
VMEM_BYTES = 50 * 1024 * 1024
F32 = jnp.float32
BF16 = jnp.bfloat16
LAST = (((1,), (1,)), ((), ()))
FIRST = (((0,), (0,)), ((), ()))
SMEM = pl.BlockSpec(memory_space=pltpu.SMEM)
VMEM = pl.BlockSpec(memory_space=pltpu.VMEM)


def dot_last(left, right):
    return lax.dot_general(left, right, LAST, preferred_element_type=F32)


def dot_first(left, right):
    return lax.dot_general(left, right, FIRST, preferred_element_type=F32)


def dot(left, right):
    return jnp.dot(left, right, preferred_element_type=F32)


def kernel_params():
    return pltpu.CompilerParams(vmem_limit_bytes=VMEM_BYTES)


def cost(flops, size):
    return pl.CostEstimate(flops=int(flops), bytes_accessed=int(size), transcendentals=0)


def exchange(parts):
    return lax.all_to_all(parts, "blk", 0, 0, tiled=True)


def norm_parts(rows_in):
    average = jnp.mean(rows_in, axis=-1, keepdims=True)
    centred = rows_in - average
    spread = lax.rsqrt(jnp.mean(centred * centred, axis=-1, keepdims=True) + EPSILON)
    return centred * spread, spread


def norm_back(hat, spread, gain, grad):
    weighted = grad * gain
    return spread * (
        weighted
        - jnp.mean(weighted, axis=-1, keepdims=True)
        - hat * jnp.mean(weighted * hat, axis=-1, keepdims=True)
    )


def project_kernel(
    order_ref, x_ref, gain_ref, wq_hbm, wk_hbm, wv_hbm, normed_ref, out_ref, weight_ref, sems
):
    group, _, _, width = out_ref.shape
    copies = [
        pltpu.make_async_copy(weight, weight_ref.at[n], sems.at[n])
        for n, weight in enumerate((wq_hbm, wk_hbm, wv_hbm))
    ]
    for copy in copies:
        copy.start()
    hat, _ = norm_parts(x_ref[...].astype(F32))
    normed = (hat * gain_ref[...]).astype(BF16)
    normed_ref[...] = normed
    for n in range(3):
        copies[n].wait()
        product = dot(normed, weight_ref[n]).astype(BF16)
        for s in range(group):
            out_ref[s, n] = product[:, s * width : (s + 1) * width]


def project(order, slot, x, gain, w_query, w_key, w_value, group):
    _, span, model = x.shape
    return pl.pallas_call(
        project_kernel,
        grid_spec=pltpu.PrefetchScalarGridSpec(
            num_scalar_prefetch=1,
            grid=(1,),
            in_specs=[pl.BlockSpec((None, span, model), lambda i, o: (o[slot], 0, 0)), VMEM]
            + [pl.BlockSpec(memory_space=pl.ANY)] * 3,
            out_specs=[VMEM] * 2,
            scratch_shapes=[
                pltpu.VMEM((3, model, model), BF16),
                pltpu.SemaphoreType.DMA((3,)),
            ],
        ),
        out_shape=[
            jax.ShapeDtypeStruct((span, model), BF16),
            jax.ShapeDtypeStruct((group, 3, span, model // group), BF16),
        ],
        compiler_params=kernel_params(),
        cost_estimate=cost(0, 1024),
        name="project",
    )(order, x, gain, w_query, w_key, w_value)


def doc_start(offs_ref, row, pos):
    start = jnp.zeros_like(pos)
    for d in range(offs_ref.shape[1]):
        first = offs_ref[row, d]
        start = jnp.where(pos >= first, first, start)
    return start


def doc_end(offs_ref, row, pos, length):
    end = jnp.int32(length)
    for d in reversed(range(offs_ref.shape[1])):
        first = offs_ref[row, d]
        end = jnp.where(first > pos, first, end)
    return end


def head_lanes(shape, head, head_dim):
    lane = lax.broadcasted_iota(jnp.int32, shape, 1)
    return (lane >= head * head_dim) & (lane < (head + 1) * head_dim)


def attend_kernel(rows, heads, head_dim, order_ref, offs_ref, scale_ref, *refs):
    count = len(rows)
    result_ref, lse_ref, score_ref = refs[count:]
    for n, row in enumerate(rows):
        attend_row(
            order_ref[row],
            heads,
            head_dim,
            offs_ref,
            scale_ref,
            refs[n],
            result_ref.at[:, n],
            lse_ref.at[n],
            score_ref,
        )


def attend_row(
    row, heads, head_dim, offs_ref, scale_ref, held, result_ref, lse_ref, score_ref
):
    blocks, _, span, width = held.shape
    wide = score_ref.shape[-1]
    per = wide // span
    lanes = min(128, wide)
    score_scale = head_dim ** (-0.5)

    def query_block(i, carry):
        first_pos = i * span
        queries = held[i, 0] * jnp.asarray(score_scale, BF16)
        query_head = [
            jnp.where(head_lanes((span, width), h, head_dim), queries, 0).astype(BF16)
            for h in range(heads)
        ]
        query_pos = first_pos + lax.broadcasted_iota(jnp.int32, (span, 1), 0)
        query_start = doc_start(offs_ref, row, query_pos)
        low = doc_start(offs_ref, row, first_pos) // wide
        high = (first_pos + span - 1) // wide + 1

        def score_step(j, tops):
            keys = held[pl.ds(j * per, per), 1].reshape(wide, width)
            key_pos = j * wide + lax.broadcasted_iota(jnp.int32, (span, wide), 1)
            allowed = (key_pos >= query_start) & (key_pos <= query_pos)
            new = []
            for h in range(heads):
                scores = jnp.where(allowed, dot_last(query_head[h], keys), MASKED)
                score_ref[h, j] = scores
                top = tops[h]
                for c in range(0, wide, lanes):
                    top = jnp.maximum(top, scores[:, c : c + lanes])
                new.append(top)
            return tuple(new)

        tops = lax.fori_loop(
            low, high, score_step, tuple(jnp.full((span, lanes), MASKED, F32) for h in range(heads))
        )
        tops = [jnp.max(top, axis=1, keepdims=True) for top in tops]

        def value_step(j, state):
            values = held[pl.ds(j * per, per), 2].reshape(wide, width)
            new = []
            for h in range(heads):
                total, acc = state[h]
                probs = jnp.exp(score_ref[h, j] - tops[h])
                for c in range(0, wide, lanes):
                    total = total + probs[:, c : c + lanes]
                acc = acc + dot(probs.astype(BF16), values)
                new.append((total, acc))
            return tuple(new)

        state = lax.fori_loop(
            low,
            high,
            value_step,
            tuple(
                (jnp.zeros((span, lanes), F32), jnp.zeros((span, width), F32)) for h in range(heads)
            ),
        )
        result = jnp.zeros((span, width), F32)
        for h in range(heads):
            total = jnp.sum(state[h][0], axis=1, keepdims=True)
            result = jnp.where(head_lanes((span, width), h, head_dim), state[h][1] / total, result)
            log_total = tops[h] + jnp.log(total)
            lse_ref[i, h : h + 1, :] = jnp.transpose(jnp.broadcast_to(log_total, (span, 128)))[
                0:1, :
            ]
        result_ref[i] = (result * scale_ref[...]).astype(BF16)
        return carry

    lax.fori_loop(0, blocks, query_block, 0)


def attend(order, offsets, rows, qkv, scale_lanes, heads, head_dim):
    group, _, span, width = qkv[0].shape
    length = group * span
    wide = max(span, min(512, length))
    return pl.pallas_call(
        functools.partial(attend_kernel, rows, heads, head_dim),
        in_specs=[SMEM, SMEM, VMEM] + [VMEM] * len(rows),
        out_shape=[
            jax.ShapeDtypeStruct((group, len(rows), span, width), BF16),
            jax.ShapeDtypeStruct((len(rows), group, heads, span), F32),
        ],
        scratch_shapes=[pltpu.VMEM((heads, length // wide, span, wide), F32)],
        compiler_params=kernel_params(),
        cost_estimate=cost(0, 1024),
        name="attend",
    )(order, offsets, scale_lanes, *qkv)


def attend_back_kernel(rows, heads, head_dim, order_ref, offs_ref, inv_ref, grad_ref, *refs):
    count = len(rows)
    held, out_refs, lse_refs = refs[:count], refs[count : 2 * count], refs[2 * count : 3 * count]
    dqkv_ref, total_ref = refs[3 * count : 3 * count + 2]
    for n, row in enumerate(rows):
        attend_back_row(
            order_ref[row],
            heads,
            head_dim,
            offs_ref,
            inv_ref,
            lse_refs[n],
            held[n],
            grad_ref.at[:, n],
            out_refs[n],
            dqkv_ref.at[:, n],
            total_ref.at[n],
            *refs[3 * count + 2 :],
        )


def attend_back_row(
    row,
    heads,
    head_dim,
    offs_ref,
    inv_ref,
    lse_ref,
    held,
    grad_ref,
    out_ref,
    dqkv_ref,
    total_ref,
    q_ref,
    k_ref,
    g_ref,
    delta_ref,
    dq_ref,
):
    blocks, _, span, width = held.shape
    score_scale = head_dim ** (-0.5)
    picks = lax.broadcasted_iota(jnp.int32, (8, width), 0)
    lane = lax.broadcasted_iota(jnp.int32, (8, width), 1)
    ones = jnp.where(lane // head_dim == picks, 1.0, 0.0).astype(F32)

    def prepare(i, carry):
        queries = held[i, 0] * jnp.asarray(score_scale, BF16)
        keys = held[i, 1]
        grads = grad_ref[i]
        for h in range(heads):
            mine = head_lanes((span, width), h, head_dim)
            q_ref[h, i] = jnp.where(mine, queries, 0).astype(BF16)
            k_ref[h, i] = jnp.where(mine, keys, 0).astype(BF16)
            g_ref[h, i] = jnp.where(mine, grads, 0).astype(BF16)
        product = grads.astype(F32) * out_ref[i].astype(F32) * inv_ref[...]
        delta_ref[i] = lax.dot_general(
            ones, product, LAST, precision=lax.Precision.HIGHEST, preferred_element_type=F32
        )
        dq_ref[i] = jnp.zeros((span, width), F32)
        return carry + delta_ref[i]

    total_ref[...] = lax.fori_loop(0, blocks, prepare, jnp.zeros((8, span), F32))

    def key_block(j, carry):
        keys = held[j, 1]
        values = held[j, 2]
        key_pos = j * span + lax.broadcasted_iota(jnp.int32, (span, 1), 0)
        last = (doc_end(offs_ref, row, (j + 1) * span - 1, blocks * span) - 1) // span + 1

        def query_step(i, state):
            dk, dv = state
            query_pos = i * span + lax.broadcasted_iota(jnp.int32, (1, span), 1)
            query_start = doc_start(offs_ref, row, query_pos)
            allowed = (key_pos >= query_start) & (key_pos <= query_pos)
            dq = dq_ref[i]
            for h in range(heads):
                scores = dot_last(keys, q_ref[h, i])
                scores = jnp.where(allowed, scores - lse_ref[i, h : h + 1, :], MASKED)
                probs = jnp.exp(scores)
                d_probs = dot_last(values, g_ref[h, i])
                d_scores = (probs * (d_probs - delta_ref[i, h : h + 1, :])).astype(BF16)
                dv = dv + dot(probs.astype(BF16), g_ref[h, i])
                dk = dk + dot(d_scores, q_ref[h, i])
                dq = dq + dot_first(d_scores, k_ref[h, j])
            dq_ref[i] = dq
            return (dk, dv)

        zero = jnp.zeros((span, width), F32)
        dk, dv = lax.fori_loop(j, last, query_step, (zero, zero))
        dqkv_ref[j, 1] = dk.astype(BF16)
        dqkv_ref[j, 2] = dv.astype(BF16)
        dqkv_ref[j, 0] = (dq_ref[j] * score_scale).astype(BF16)
        return carry

    lax.fori_loop(0, blocks, key_block, 0)


def attend_back(
    order, offsets, rows, qkv, grads, at, scaled, inverse_lanes, lse, heads, head_dim
):
    group, _, span, width = qkv[0].shape
    count = len(rows)
    return pl.pallas_call(
        functools.partial(attend_back_kernel, rows, heads, head_dim),
        grid=(1,),
        in_specs=[SMEM, SMEM, VMEM]
        + [pl.BlockSpec((group, count, span, width), lambda i: (0, at, 0, 0))]
        + [VMEM] * (3 * count),
        out_specs=[VMEM] * 2,
        out_shape=[
            jax.ShapeDtypeStruct((group, count, 3, span, width), BF16),
            jax.ShapeDtypeStruct((count, 8, span), F32),
        ],
        scratch_shapes=[pltpu.VMEM((heads, group, span, width), BF16)] * 3
        + [pltpu.VMEM((group, 8, span), F32), pltpu.VMEM((group, span, width), F32)],
        compiler_params=kernel_params(),
        cost_estimate=cost(0, 1024),
        name="attend_back",
    )(order, offsets, inverse_lanes, grads, *qkv, *scaled, *lse)


def join_grads_kernel(parts, in_ref, out_ref):
    group = in_ref.shape[0]
    for n in range(3):
        whole = jnp.concatenate([in_ref[s, 0, n] for s in range(group)], axis=1)
        piece = whole.shape[1] // parts
        for p in range(parts):
            to = (p * 3 + n) * piece
            out_ref[:, to : to + piece] = whole[:, p * piece : (p + 1) * piece]


def join_grads(block):
    group, _, _, span, width = block.shape
    return pl.pallas_call(
        functools.partial(join_grads_kernel, PARTS),
        out_shape=jax.ShapeDtypeStruct((span, 3 * group * width), BF16),
        compiler_params=kernel_params(),
        cost_estimate=cost(0, 1024),
        name="join_grads",
    )(block)


FF_STEP = 512


def layer_kernel(
    order_ref,
    o_ref,
    x_ref,
    d_out_ref,
    post_ref,
    ffn_ref,
    mid_gain_ref,
    scale_ref,
    w_out_ref,
    d_mid_hbm,
    w_fc1_hbm,
    scaled_ref,
    ffn_in_ref,
    residual_ref,
    mid_ref,
    d_pre_ref,
    d_proj_ref,
    d_residual_ref,
    d_attn_ref,
    g_post_ref,
    g_ffn_ref,
    g_mid_ref,
    d_mid_ref,
    w_fc1_ref,
    act_ref,
    slope_ref,
    sems,
    *,
    slot,
):
    group, _, span, width = o_ref.shape
    hidden = act_ref.shape[1]
    steps = [slice(c, c + FF_STEP) for c in range(0, hidden, FF_STEP)]
    weight_copies = [
        pltpu.make_async_copy(w_fc1_hbm.at[:, at], w_fc1_ref.at[:, at], sems.at[c])
        for c, at in enumerate(steps)
    ]
    mid_copy = pltpu.make_async_copy(
        d_mid_hbm.at[pl.ds(pl.multiple_of(order_ref[slot] * span, span), span), :],
        d_mid_ref,
        sems.at[len(steps)],
    )
    for copy in weight_copies:
        copy.start()
    mid_copy.start()

    scaled = jnp.concatenate([o_ref[s, 0] for s in range(group)], axis=1)
    scaled_ref[...] = scaled
    proj_hat, proj_spread = norm_parts(dot(scaled, w_out_ref[...]))
    residual = x_ref[...].astype(F32) + proj_hat * post_ref[...]
    residual_ref[...] = residual
    res_hat, res_spread = norm_parts(residual)
    ffn_in = (res_hat * ffn_ref[...]).astype(BF16)
    ffn_in_ref[...] = ffn_in

    total = jnp.zeros((span, 1), F32)
    for c, at in enumerate(steps):
        weight_copies[c].wait()
        pre = dot(ffn_in, w_fc1_ref[:, at])
        phi = 0.5 + 0.5 * lax.erf(pre * (0.5**0.5))
        act = pre * phi
        act_ref[:, at] = act
        slope_ref[:, at] = phi + pre * jnp.exp(-0.5 * pre * pre) * 0.3989422804014327
        total += jnp.sum(act, axis=1, keepdims=True)
    average = total / hidden
    total = jnp.zeros((span, 1), F32)
    for at in steps:
        centred = act_ref[:, at] - average
        total += jnp.sum(centred * centred, axis=1, keepdims=True)
    spread = lax.rsqrt(total / hidden + EPSILON)

    mid_copy.wait()
    sum_weighted = jnp.zeros((span, 1), F32)
    sum_hat = jnp.zeros((span, 1), F32)
    for at in steps:
        hat = (act_ref[:, at] - average) * spread
        act_ref[:, at] = hat
        gain = mid_gain_ref[:, at]
        mid_ref[:, at] = (hat * gain).astype(BF16)
        grad = d_mid_ref[:, at]
        product = grad * hat
        g_mid_ref[:, at] = jnp.sum(product, axis=0, keepdims=True)
        sum_weighted += jnp.sum(grad * gain, axis=1, keepdims=True)
        sum_hat += jnp.sum(product * gain, axis=1, keepdims=True)
    sum_weighted = sum_weighted / hidden
    sum_hat = sum_hat / hidden
    d_ffn = jnp.zeros(x_ref.shape, F32)
    for at in steps:
        weighted = d_mid_ref[:, at] * mid_gain_ref[:, at]
        d_act = spread * (weighted - sum_weighted - act_ref[:, at] * sum_hat)
        d_pre = (d_act * slope_ref[:, at]).astype(BF16)
        d_pre_ref[:, at] = d_pre
        d_ffn += dot_last(d_pre, w_fc1_ref[:, at])

    g_ffn_ref[...] = jnp.sum(d_ffn * res_hat, axis=0, keepdims=True)
    d_residual = d_out_ref[...].astype(F32) + norm_back(res_hat, res_spread, ffn_ref[...], d_ffn)
    d_residual_ref[...] = d_residual
    g_post_ref[...] = jnp.sum(d_residual * proj_hat, axis=0, keepdims=True)
    d_proj = norm_back(proj_hat, proj_spread, post_ref[...], d_residual).astype(BF16)
    d_proj_ref[...] = d_proj
    d_attn = (dot_last(d_proj, w_out_ref[...]) * scale_ref[...]).astype(BF16)
    for s in range(group):
        d_attn_ref[s, 0] = d_attn[:, s * width : (s + 1) * width]


def layer(order, slot, o_blocks, at, x, d_out, gains, w_out, d_mid, w_fc1):
    group, _, span, width = o_blocks.shape
    model = x.shape[2]
    hidden = w_fc1.shape[1]
    shape = jax.ShapeDtypeStruct
    return pl.pallas_call(
        functools.partial(layer_kernel, slot=slot),
        grid_spec=pltpu.PrefetchScalarGridSpec(
            num_scalar_prefetch=1,
            grid=(1,),
            in_specs=[pl.BlockSpec((group, 1, span, width), lambda i, o: (0, at, 0, 0))]
            + [pl.BlockSpec((None, span, model), lambda i, o: (o[slot], 0, 0))] * 2
            + [VMEM] * 5
            + [pl.BlockSpec(memory_space=pl.ANY)] * 2,
            out_specs=[VMEM] * 11,
            scratch_shapes=[
                pltpu.VMEM((span, hidden), F32),
                pltpu.VMEM(w_fc1.shape, BF16),
                pltpu.VMEM((span, hidden), F32),
                pltpu.VMEM((span, hidden), F32),
                pltpu.SemaphoreType.DMA((hidden // FF_STEP + 1,)),
            ],
        ),
        out_shape=[
            shape((span, model), BF16),
            shape((span, model), BF16),
            shape((span, model), F32),
            shape((span, hidden), BF16),
            shape((span, hidden), BF16),
            shape((span, model), BF16),
            shape((span, model), F32),
            shape((group, 1, span, width), BF16),
            shape((1, model), F32),
            shape((1, model), F32),
            shape((1, hidden), F32),
        ],
        compiler_params=kernel_params(),
        cost_estimate=cost(0, 1024),
        name="layer",
    )(order, o_blocks, x, d_out, *gains, w_out, d_mid, w_fc1)


def layer_out_kernel(order_ref, *refs):
    count = (len(refs) - 2) // 2
    weight, out_ref = refs[-2], refs[-1]
    for r in range(count):
        out_ref[order_ref[r]] = (refs[r][...] + dot(refs[count + r][...], weight[...])).astype(BF16)


def last_step(order, residuals, mids, w_fc2):
    return pl.pallas_call(
        layer_out_kernel,
        in_specs=[SMEM] + [VMEM] * (2 * len(mids) + 1),
        out_shape=jax.ShapeDtypeStruct((len(mids),) + residuals[0].shape, BF16),
        compiler_params=kernel_params(),
        cost_estimate=cost(0, 1024),
        name="layer_out",
    )(order, *residuals, *mids, w_fc2)


def flip(value, axis, bit):
    size = lax.axis_size(axis)
    return lax.ppermute(value, axis, [(i, i ^ (1 << bit)) for i in range(size)])


def bits(axis):
    return (lax.axis_size(axis) - 1).bit_length()


PARTS = 4


def weight_kernel(count, rows, added, shards, part_ref, *refs):
    out_ref = refs[-1]
    high = out_ref.shape[1]
    per = rows * (shards + 1)
    extras = refs[per * count : per * count + added]
    at = 0
    for n in range(count):
        mine = refs[n * per : (n + 1) * per]
        rights = mine[rows * shards :]
        width = rights[0].shape[1]
        total = 0.0
        for r in range(rows):
            left = [ref[...] for ref in mine[r * shards : (r + 1) * shards]]
            left = jnp.concatenate(left, axis=1) if shards > 1 else left[0]
            total += dot_first(left, rights[r][...])
        for i in range(shards):
            piece = total[i * high : (i + 1) * high]
            for extra in extras:
                piece = piece + extra[i, :, at : at + width].astype(F32)
            out_ref[i, :, at : at + width] = piece.astype(BF16)
        at += width


def weight_part_plain(pairs, part, extras, group):
    pieces = []
    for lefts, rights, kind in pairs:
        left, right = jnp.concatenate(lefts), jnp.concatenate(rights)
        if kind == "columns":
            wide = right.shape[1] // PARTS
            right = lax.dynamic_slice(right, (0, part * wide), (right.shape[0], wide))
            left = left.reshape(left.shape[0], group, -1)
        else:
            left = left.reshape(left.shape[0], group, PARTS, -1)
            left = lax.dynamic_index_in_dim(left, part, 2, keepdims=False)
        pieces.append(jnp.einsum("tsd,te->sde", left, right, preferred_element_type=F32))
    total = jnp.concatenate(pieces, axis=2)
    for extra in extras:
        total = total + extra.astype(F32)
    return total.astype(BF16)


def weight_part(pairs, part, extras, group):
    shards = 2
    specs, arrays, width = [], [], 0
    for lefts, rights, kind in pairs:
        span, model = lefts[0].shape
        stride = 1 if kind == "columns" else PARTS
        high = model // group // stride
        wide = rights[0].shape[1] // (PARTS if kind == "columns" else 1)
        for left in lefts:
            for i in range(shards):

                def left_at(g, p, i=i, stride=stride):
                    return (0, (g * shards + i) * stride + (p[0] if stride > 1 else 0))

                specs.append(pl.BlockSpec((span, high), left_at))
                arrays.append(left)
        for right in rights:

            def right_at(g, p, stride=stride):
                return (0, p[0] if stride == 1 else 0)

            specs.append(pl.BlockSpec((span, wide), right_at))
            arrays.append(right)
        width += wide
    if high % 128:
        return weight_part_plain(pairs, part, extras, group)
    block = pl.BlockSpec((shards, high, width), lambda g, p: (g, 0, 0))
    return pl.pallas_call(
        functools.partial(weight_kernel, len(pairs), len(pairs[0][0]), len(extras), shards),
        grid_spec=pltpu.PrefetchScalarGridSpec(
            num_scalar_prefetch=1,
            grid=(group // shards,),
            in_specs=specs + [block] * len(extras),
            out_specs=block,
        ),
        out_shape=jax.ShapeDtypeStruct((group, high, width), BF16),
        compiler_params=kernel_params(),
        cost_estimate=cost(0, 1024),
        name="weight_part",
    )(part.astype(jnp.int32).reshape(1), *arrays, *extras)


class WeightSum:
    def __init__(self, *pairs):
        self.pairs = pairs
        batch_at = lax.axis_index("batch")
        self.near, self.far = batch_at & 1, (batch_at >> 1) & 1

    def piece(self, order, near, far, *extras):
        def part_of(part):
            return weight_part(self.pairs, part, extras, lax.axis_size("blk"))

        return order(part_of, near * 2 + far)

    def away_far(self, order):
        return self.piece(order, 1 - self.near, 1 - self.far)

    def send_far(self, order, away):
        return self.piece(order, self.near, 1 - self.far, away)

    def away_near(self, order):
        return self.piece(order, 1 - self.near, self.far)

    def keep(self, order, away, arrived):
        return self.piece(order, self.near, self.far, away, arrived)


def over_near(sent):
    return flip(sent, "batch", 0)


def over_far(sent):
    return flip(sent, "batch", 1)


class Order:
    def __init__(self):
        self.last = ()

    def __call__(self, step, *values):
        self.last = step(*tie(values, self.last))
        return self.last


def window(always, step):
    def nothing():
        return jax.tree.map(lambda leaf: jnp.zeros(leaf.shape, leaf.dtype), jax.eval_shape(step))

    return lax.cond(always, step, nothing)


def tie(values, *after):
    return lax.optimization_barrier((values, after))[0]


def combine_kernel(plan, at_ref, *refs):
    ins = sum(2 if added else 1 for added, _ in plan)
    into, out_of = list(refs[:ins]), list(refs[ins:])
    for n, (added, cut) in enumerate(plan):
        terms = [into.pop(0) for _ in range(2 if added else 1)]

        def total(i):
            if len(terms) == 1:
                return terms[0][i]
            return (terms[0][i].astype(F32) + terms[1][i].astype(F32)).astype(BF16)

        if cut:
            keep, send = out_of.pop(0), out_of.pop(0)
            for j in range(keep.shape[0]):
                keep[j] = total(2 * j + at_ref[n])
                send[j] = total(2 * j + 1 - at_ref[n])
        else:
            whole = out_of.pop(0)
            for j in range(whole.shape[0]):
                whole[j] = total(j)


class Tree:
    def __init__(self, mine):
        self.steps = [("blk", bit) for bit in range(bits("blk"))]
        self.steps += [("batch", bit) for bit in range(2, bits("batch"))]
        self.steps += [("far", 1), ("near", 0)]
        self.kept, self.sends, self.arrived = mine, None, None

    def start(self):
        kind, bit = self.steps[0]
        return [flip(send, "blk" if kind == "blk" else "batch", bit) for send in self.sends]

    def end(self, arrived):
        self.last = self.steps.pop(0)[0]
        self.arrived = arrived


def combine(trees):
    me = lax.axis_index("blk")
    plan, ins, shapes, at, cutting = [], [], [], [], []
    for tree in trees:
        if tree.sends is not None and tree.last == "far":
            tree.sends = [tree.kept, tree.arrived[0]]
            continue
        added = tree.sends is not None
        kind, bit = tree.steps[0]
        cut = kind == "blk"
        plan.append((added, cut))
        ins += [tree.kept] + (list(tree.arrived) if added else [])
        count, *rest = tree.kept.shape
        shape = jax.ShapeDtypeStruct((count // 2 if cut else count, *rest), BF16)
        shapes += [shape] * (2 if cut else 1)
        at.append((me >> bit) & 1 if cut else me * 0)
        cutting.append(tree)
    if not plan:
        return
    outs = list(
        pl.pallas_call(
            functools.partial(combine_kernel, plan),
            in_specs=[SMEM] + [VMEM] * len(ins),
            out_shape=shapes,
            compiler_params=kernel_params(),
            cost_estimate=cost(0, 1024),
            name="combine",
        )(jnp.stack(at).astype(jnp.int32), *ins)
    )
    for tree, (_, cut) in zip(cutting, plan):
        tree.kept = outs.pop(0)
        tree.sends = [outs.pop(0)] if cut else [tree.kept]


def place_kernel(layout, part_ref, *refs):
    ins, outs = list(refs[: 4 * len(layout)]), list(refs[4 * len(layout) :])
    near, far = part_ref[0], part_ref[1]
    order = [near * 2 + far, near * 2 + 1 - far, (1 - near) * 2 + far, (1 - near) * 2 + 1 - far]
    for spans in layout:
        pieces = [ins.pop(0) for _ in range(4)]
        for start, width, kind in spans:
            out = outs.pop(0)
            for part, piece in zip(order, pieces):
                value = piece[0, :, start : start + width].astype(F32)
                if kind == "columns":
                    out[:, pl.ds(pl.multiple_of(part * width, 128), width)] = value
                else:
                    high = value.shape[0]
                    out[pl.ds(pl.multiple_of(part * high, 8), high), :] = value


def place(trees, layout):
    batch_at = lax.axis_index("batch")
    parts = jnp.stack([batch_at & 1, (batch_at >> 1) & 1]).astype(jnp.int32)
    ins, shapes = [], []
    for tree, spans in zip(trees, layout):
        ins += [*tree.sends, *tree.arrived]
        high = tree.kept.shape[1]
        for _, width, kind in spans:
            shape = (high, PARTS * width) if kind == "columns" else (PARTS * high, width)
            shapes.append(jax.ShapeDtypeStruct(shape, F32))
    return pl.pallas_call(
        functools.partial(place_kernel, layout),
        in_specs=[SMEM] + [VMEM] * len(ins),
        out_shape=shapes,
        compiler_params=kernel_params(),
        cost_estimate=cost(0, 1024),
        name="place",
    )(parts, *ins)


class SmallSum:
    def __init__(self, mine):
        self.mine = mine
        self.steps = [("batch", bit) for bit in range(bits("batch"))]
        self.steps += [("blk", bit) for bit in range(bits("blk"))]

    def start(self):
        return flip(self.mine, *self.steps[0])

    def end(self, arrived):
        self.steps.pop(0)
        self.mine = self.mine + arrived


def input_grad_kernel(parts, rows, order_ref, x_ref, gain_ref, wq_ref, wk_ref, wv_ref, *refs):
    out_ref, sum_ref = refs[2 * rows :]
    model = wq_ref.shape[0]
    piece = model // parts
    total = jnp.zeros(sum_ref.shape, F32)
    for r in range(rows):
        d_ref, res_ref = refs[r], refs[rows + r]
        grad = jnp.zeros(res_ref.shape, F32)
        for p in range(parts):
            for n, weight in enumerate((wq_ref, wk_ref, wv_ref)):
                at = (p * 3 + n) * piece
                grad += dot_last(d_ref[:, at : at + piece], weight[:, p * piece : (p + 1) * piece])
        row = order_ref[r]
        hat, spread = norm_parts(x_ref[row].astype(F32))
        out_ref[row] = res_ref[...] + norm_back(hat, spread, gain_ref[...], grad)
        total += jnp.sum(grad * hat, axis=0, keepdims=True)
    sum_ref[...] = total


def input_grad(order, x, gain, w_query, w_key, w_value, d_rows, d_residuals):
    return pl.pallas_call(
        functools.partial(input_grad_kernel, PARTS, len(d_rows)),
        in_specs=[SMEM] + [VMEM] * (5 + 2 * len(d_rows)),
        out_shape=[
            jax.ShapeDtypeStruct(x.shape, F32),
            jax.ShapeDtypeStruct((1, x.shape[2]), F32),
        ],
        compiler_params=kernel_params(),
        cost_estimate=cost(0, 1024),
        name="input_grad",
    )(order, x, gain, w_query, w_key, w_value, *d_rows, *d_residuals)


def on_device(
    inputs,
    ln_attn,
    w_query,
    w_key,
    w_value,
    w_out,
    head_scale,
    ln_post,
    ln_ffn,
    w_fc1,
    ln_mid,
    w_fc2,
    offsets,
    cotangent,
):
    row_count, span, model = inputs.shape
    head_count = head_scale.shape[0]
    head_dim = model // head_count
    tokens = row_count * span
    group = lax.axis_size("blk")
    heads = head_count // group
    width = heads * head_dim
    my_index = lax.axis_index("blk")
    rows = range(row_count)

    always = offsets[0, 0] == 0
    ends = jnp.concatenate(
        [offsets[:, 1:], jnp.full((row_count, 1), span * group, offsets.dtype)], axis=1
    )
    work = jnp.sum((ends - offsets) ** 2, axis=1)
    index = jnp.arange(row_count, dtype=jnp.int32)
    before = (work[None, :] > work[:, None]) | (
        (work[None, :] == work[:, None]) & (index[None, :] < index[:, None])
    )
    rank = jnp.sum(before.astype(jnp.int32), axis=1)
    by_work = jnp.sum(jnp.where(rank[None, :] == index[:, None], index[None, :], 0), axis=1)
    gain = ln_attn.reshape(1, model)
    last = row_count - 1
    my_scale = lax.dynamic_slice(head_scale, (my_index * heads,), (heads,))
    scale_lanes = jnp.repeat(my_scale, head_dim).reshape(1, width)
    layer_gains = [
        ln_post.reshape(1, model),
        ln_ffn.reshape(1, model),
        ln_mid.reshape(1, -1),
        jnp.repeat(head_scale, head_dim).reshape(1, model),
    ]

    def project_row(r, x):
        return project(by_work, r, x, gain, w_query, w_key, w_value, group)

    def attend_one(r, held):
        return attend(by_work, offsets, [r], [held], scale_lanes, heads, head_dim)

    def layer_row(r, o_blocks):
        at = r if r < last else 0
        return layer(by_work, r, o_blocks, at, inputs, cotangent, layer_gains, w_out, d_mid, w_fc1)

    def back(order, r, row_heads, at=0):
        def back_row(held):
            return attend_back(
                by_work,
                offsets,
                [r],
                [held],
                row_heads,
                at,
                [scaled_mine[r].reshape(group, span, width)],
                1.0 / scale_lanes,
                [lse[r].reshape(lse[r].shape[1:])],
                heads,
                head_dim,
            )

        return order(back_row, qkv[r])

    def first_window():
        order = Order()
        return exchange(sent), [
            order(functools.partial(project_row, r), inputs) for r in rows[1:]
        ]

    normed_first, sent = project_row(0, inputs)
    held, projected = window(always, first_window)
    qkv = [held]
    normed = [normed_first] + [part[0] for part in projected]
    scaled_mine, lse = [], []
    for r in rows[1:]:

        def next_window():
            order = Order()
            extra = ()
            if r == 1:
                extra = jnp.einsum(
                    "td,fd->tf",
                    cotangent.reshape(tokens, model),
                    w_fc2,
                    preferred_element_type=F32,
                )
            return exchange(projected[r - 1][1]), attend_one(r - 1, qkv[r - 1]), extra

        held, (out, log_total), extra = window(always, next_window)
        d_mid = extra if r == 1 else d_mid
        qkv.append(held)
        scaled_mine.append(out)
        lse.append(log_total)

    def early_window():
        return (
            exchange(jnp.concatenate(scaled_mine, axis=1)),
            attend_one(last, qkv[last]),
        )

    early, (out, log_total) = window(always, early_window)
    scaled_mine.append(out)
    lse.append(log_total)

    def late_window():
        return exchange(scaled_mine[last]), layer_row(0, early)

    late, layer_first = window(always, late_window)

    def layer_window():
        order = Order()
        first = exchange(layer_first[7])
        rest = []
        for r in rows[1:]:

            def one(o_blocks):
                return layer_row(r, o_blocks)

            rest.append(order(one, early if r < last else late))
        return first, rest

    first_heads, rest = window(always, layer_window)
    (
        scaled,
        ffn_in,
        residual,
        mid,
        d_pre,
        d_proj,
        d_residual,
        d_attn,
        g_post,
        g_ffn,
        g_mid,
    ) = zip(layer_first, *rest)
    d_out = [lax.dynamic_index_in_dim(cotangent, by_work[r], keepdims=False) for r in rows]
    sum_one = WeightSum((mid, d_out, "rows"))
    sum_two = WeightSum((ffn_in, d_pre, "columns"))
    sum_three = WeightSum((scaled, d_proj, "columns"))
    order = Order()
    away = over_near(sum_one.away_far(order))
    away_two = sum_two.away_far(order)
    sent_one = sum_one.send_far(order, away)

    def back_first():
        order = Order()
        arrived = over_far(sent_one)
        heads_in = exchange(jnp.concatenate(d_attn[1:], axis=1))
        away = over_near(away_two)
        near = sum_one.away_near(order)
        out = back(order, 0, first_heads)
        return arrived, heads_in, out, near, sum_two.send_far(order, away)

    far_one, rest_heads, (sent, total), near_one, sent_two = window(always, back_first)
    totals = [total]

    def back_second():
        order = Order()
        arrived = over_far(sent_two), over_near(near_one)
        grad = exchange(sent)
        out = back(order, 1, rest_heads, 0)
        return grad, out, arrived, sum_two.away_near(order), sum_three.away_far(order)

    grad, (sent, total), arrived, near_two, away_three = window(always, back_second)
    far_two, near_one = arrived
    totals.append(total)
    grads = [grad]
    order = Order()
    away_three = over_near(away_three)
    tree_one = Tree(sum_one.keep(order, near_one, far_one))
    combine([tree_one])
    sent_three = sum_three.send_far(order, away_three)
    for r in rows[2:]:

        def back_next():
            order = Order()
            moved, near = (), ()
            if r == 2:
                moved = tree_one.start(), over_far(sent_three), over_near(near_two)
            grad = exchange(sent)
            out = back(order, r, rest_heads, r - 1)
            if r == 2:
                near = sum_three.away_near(order)
            return grad, moved, near, out

        grad, moved, near, (sent, total) = window(always, back_next)
        totals.append(total)
        grads.append(grad)
        if r == 2:
            moved, far_three, near_two = moved
            tree_one.end(moved)
            near_three = near
    tree_two = Tree(sum_two.keep(Order(), near_two, far_two))
    combine([tree_one, tree_two])

    def back_last():
        order = Order()
        moved = tree_one.start(), tree_two.start(), over_near(near_three)
        grad = exchange(sent)
        joined = [order(join_grads, part) for part in grads]

        def output_step(weight):
            return last_step(by_work, residual, mid, weight)

        return grad, moved, joined, order(output_step, w_fc2)

    grad, moved, d_rows, layer_out = window(always, back_last)
    tree_one.end(moved[0])
    tree_two.end(moved[1])
    near_three = moved[2]
    order = Order()
    d_rows = d_rows + [order(join_grads, grad)]
    sum_qkv = WeightSum((normed, d_rows, "columns"))
    away_qkv = over_near(sum_qkv.away_far(order))
    near_qkv = sum_qkv.away_near(order)
    tree_three = Tree(sum_three.keep(order, near_three, far_three))
    combine([tree_one, tree_two, tree_three])
    sent_qkv = sum_qkv.send_far(order, away_qkv)

    def advance(trees, extra=lambda: ()):
        def step():
            return [tree.start() for tree in trees], extra()

        moved, out = window(always, step)
        for tree, arrived in zip(trees, moved):
            tree.end(arrived)
        return out

    def beside():
        order = Order()
        arrived = over_far(sent_qkv)
        near = over_near(near_qkv)

        def input_step(x):
            return input_grad(by_work, x, gain, w_query, w_key, w_value, d_rows, d_residual)

        return arrived, near, order(input_step, inputs)

    far_qkv, near_qkv, (grad_inputs, grad_ln_attn) = advance(
        [tree_one, tree_two, tree_three], beside
    )
    tree_qkv = Tree(sum_qkv.keep(order, near_qkv, far_qkv))
    delta_sum = sum(jnp.sum(total, axis=(0, 2)) for total in totals)
    my_grad = delta_sum[:heads] / my_scale
    scale_part = lax.dynamic_update_slice(
        jnp.zeros((head_count,), F32), my_grad, (my_index * heads,)
    )
    small = SmallSum(
        jnp.concatenate(
            [grad_ln_attn[0], sum(g_post)[0], sum(g_ffn)[0], sum(g_mid)[0], scale_part]
        )
    )
    piece = model // PARTS
    ff_piece = w_fc1.shape[1] // PARTS
    trees = [tree_qkv, tree_three, tree_two, tree_one]
    placed = None
    while any(tree.steps for tree in trees + [small]):
        combine([tree for tree in trees if tree.steps])

        def place_early():
            if tree_two.steps or tree_one.steps or placed is not None:
                return ()
            return place(
                [tree_one, tree_two], [[(0, model, "rows")], [(0, ff_piece, "columns")]]
            )

        early_out = advance([tree for tree in trees + [small] if tree.steps], place_early)
        placed = early_out or placed
    if placed is None:
        placed = place([tree_one, tree_two], [[(0, model, "rows")], [(0, ff_piece, "columns")]])
    grad_fc2, grad_fc1 = placed
    *grads_qkv, grad_out = place(
        [tree_qkv, tree_three],
        [[(n * piece, piece, "columns") for n in range(3)], [(0, piece, "columns")]],
    )
    gains = small.mine
    ends = [0, model, 2 * model, 3 * model, 3 * model + ln_mid.shape[0]]
    ends.append(ends[-1] + head_count)
    gains = [gains[low:high] for low, high in zip(ends[:-1], ends[1:])]

    def shard_of(vector):
        part = vector.shape[0] // group
        return lax.dynamic_slice(vector, (my_index * part,), (part,))

    return (
        layer_out,
        grad_inputs,
        shard_of(gains[0]),
        grads_qkv[0],
        grads_qkv[1],
        grads_qkv[2],
        grad_out,
        gains[4],
        shard_of(gains[1]),
        shard_of(gains[2]),
        grad_fc1,
        shard_of(gains[3]),
        grad_fc2,
    )


def solution(mesh):
    rows = P("batch", "blk", None)
    shard = P("blk", None)
    return jax.shard_map(
        on_device,
        mesh=mesh,
        in_specs=(rows,) + (P(),) * 11 + (P("batch", None), rows),
        out_specs=(
            rows,
            rows,
            P("blk"),
            shard,
            shard,
            shard,
            shard,
            P(),
            P("blk"),
            P("blk"),
            shard,
            P("blk"),
            shard,
        ),
        check_vma=False,
    )
```

```python
import functools

import jax
import jax.numpy as jnp
from jax import lax
from jax.experimental import pallas as pl
from jax.experimental.pallas import tpu as pltpu
from jax.sharding import PartitionSpec as P

EPSILON = 1e-05
MASKED = -1e30
VMEM_BYTES = 50 * 1024 * 1024
F32 = jnp.float32
BF16 = jnp.bfloat16
LAST = (((1,), (1,)), ((), ()))
FIRST = (((0,), (0,)), ((), ()))
SMEM = pl.BlockSpec(memory_space=pltpu.SMEM)
VMEM = pl.BlockSpec(memory_space=pltpu.VMEM)


def dot_last(left, right):
    return lax.dot_general(left, right, LAST, preferred_element_type=F32)


def dot_first(left, right):
    return lax.dot_general(left, right, FIRST, preferred_element_type=F32)


def dot(left, right):
    return jnp.dot(left, right, preferred_element_type=F32)


def kernel_params():
    return pltpu.CompilerParams(vmem_limit_bytes=VMEM_BYTES)


def cost(flops, size):
    return pl.CostEstimate(flops=int(flops), bytes_accessed=int(size), transcendentals=0)


def exchange(parts):
    return lax.all_to_all(parts, "blk", 0, 0, tiled=True)


def norm_parts(rows_in):
    average = jnp.mean(rows_in, axis=-1, keepdims=True)
    centred = rows_in - average
    spread = lax.rsqrt(jnp.mean(centred * centred, axis=-1, keepdims=True) + EPSILON)
    return centred * spread, spread


def norm_back(hat, spread, gain, grad):
    weighted = grad * gain
    return spread * (
        weighted
        - jnp.mean(weighted, axis=-1, keepdims=True)
        - hat * jnp.mean(weighted * hat, axis=-1, keepdims=True)
    )


def rows_by_work(offs_ref, length):
    rows, docs = offs_ref.shape
    work = []
    for r in range(rows):
        total = jnp.int32(0)
        for d in range(docs):
            end = offs_ref[r, d + 1] if d + 1 < docs else length
            total += (end - offs_ref[r, d]) * (end - offs_ref[r, d])
        work.append(total)
    ranks = []
    for r in range(rows):
        rank = jnp.int32(0)
        for other in range(rows):
            if other < r:
                rank += (work[other] >= work[r]).astype(jnp.int32)
            elif other > r:
                rank += (work[other] > work[r]).astype(jnp.int32)
        ranks.append(rank)
    return [
        sum(jnp.where(ranks[r] == slot, jnp.int32(r), jnp.int32(0)) for r in range(rows))
        for slot in range(rows)
    ]


def project_kernel(
    slot,
    offs_ref,
    gain_ref,
    x_hbm,
    wq_hbm,
    wk_hbm,
    wv_hbm,
    normed_ref,
    out_ref,
    order_ref,
    x_ref,
    weight_ref,
    sems,
):
    group, _, span, width = out_ref.shape
    order = rows_by_work(offs_ref, group * span)
    copy_x = pltpu.make_async_copy(x_hbm.at[order[slot]], x_ref, sems.at[3])
    copy_x.start()
    copies = [
        pltpu.make_async_copy(weight, weight_ref.at[n], sems.at[n])
        for n, weight in enumerate((wq_hbm, wk_hbm, wv_hbm))
    ]
    for copy in copies:
        copy.start()
    for r, row in enumerate(order):
        order_ref[r] = row
    copy_x.wait()
    hat, _ = norm_parts(x_ref[...].astype(F32))
    normed = (hat * gain_ref[...]).astype(BF16)
    normed_ref[...] = normed
    for n in range(3):
        copies[n].wait()
        product = dot(normed, weight_ref[n]).astype(BF16)
        for s in range(group):
            out_ref[s, n] = product[:, s * width : (s + 1) * width]


def project(offsets, slot, x, gain, w_query, w_key, w_value, group):
    rows, span, model = x.shape
    return pl.pallas_call(
        functools.partial(project_kernel, slot),
        in_specs=[SMEM, VMEM] + [pl.BlockSpec(memory_space=pl.ANY)] * 4,
        out_specs=[VMEM, VMEM, SMEM],
        scratch_shapes=[
            pltpu.VMEM((span, model), BF16),
            pltpu.VMEM((3, model, model), BF16),
            pltpu.SemaphoreType.DMA((4,)),
        ],
        out_shape=[
            jax.ShapeDtypeStruct((span, model), BF16),
            jax.ShapeDtypeStruct((group, 3, span, model // group), BF16),
            jax.ShapeDtypeStruct((rows,), jnp.int32),
        ],
        compiler_params=kernel_params(),
        cost_estimate=cost(0, 1024),
        name="project",
    )(offsets, gain, x, w_query, w_key, w_value)


def doc_start(offs_ref, row, pos):
    start = jnp.zeros_like(pos)
    for d in range(offs_ref.shape[1]):
        first = offs_ref[row, d]
        start = jnp.where(pos >= first, first, start)
    return start


def doc_end(offs_ref, row, pos, length):
    end = jnp.int32(length)
    for d in reversed(range(offs_ref.shape[1])):
        first = offs_ref[row, d]
        end = jnp.where(first > pos, first, end)
    return end


def head_lanes(shape, head, head_dim):
    lane = lax.broadcasted_iota(jnp.int32, shape, 1)
    return (lane >= head * head_dim) & (lane < (head + 1) * head_dim)


def attend_kernel(rows, heads, head_dim, order_ref, offs_ref, scale_ref, *refs):
    count = len(rows)
    result_ref, lse_ref, score_ref = refs[count:]
    for n, row in enumerate(rows):
        attend_row(
            order_ref[row],
            heads,
            head_dim,
            offs_ref,
            scale_ref,
            refs[n],
            result_ref.at[:, n],
            lse_ref.at[n],
            score_ref,
        )


def attend_row(
    row, heads, head_dim, offs_ref, scale_ref, held, result_ref, lse_ref, score_ref
):
    blocks, _, span, width = held.shape
    wide = score_ref.shape[-1]
    per = wide // span
    lanes = min(128, wide)
    score_scale = head_dim ** (-0.5)

    def query_block(i, carry):
        first_pos = i * span
        queries = held[i, 0] * jnp.asarray(score_scale, BF16)
        query_head = [
            jnp.where(head_lanes((span, width), h, head_dim), queries, 0).astype(BF16)
            for h in range(heads)
        ]
        query_pos = first_pos + lax.broadcasted_iota(jnp.int32, (span, 1), 0)
        query_start = doc_start(offs_ref, row, query_pos)
        low = doc_start(offs_ref, row, first_pos) // wide
        high = (first_pos + span - 1) // wide + 1

        def score_step(j, tops):
            keys = held[pl.ds(j * per, per), 1].reshape(wide, width)
            key_pos = j * wide + lax.broadcasted_iota(jnp.int32, (span, wide), 1)
            allowed = (key_pos >= query_start) & (key_pos <= query_pos)
            new = []
            for h in range(heads):
                scores = jnp.where(allowed, dot_last(query_head[h], keys), MASKED)
                score_ref[h, j] = scores
                top = tops[h]
                for c in range(0, wide, lanes):
                    top = jnp.maximum(top, scores[:, c : c + lanes])
                new.append(top)
            return tuple(new)

        tops = lax.fori_loop(
            low, high, score_step, tuple(jnp.full((span, lanes), MASKED, F32) for h in range(heads))
        )
        tops = [jnp.max(top, axis=1, keepdims=True) for top in tops]

        def value_step(j, state):
            values = held[pl.ds(j * per, per), 2].reshape(wide, width)
            new = []
            for h in range(heads):
                total, acc = state[h]
                probs = jnp.exp(score_ref[h, j] - tops[h])
                for c in range(0, wide, lanes):
                    total = total + probs[:, c : c + lanes]
                acc = acc + dot(probs.astype(BF16), values)
                new.append((total, acc))
            return tuple(new)

        state = lax.fori_loop(
            low,
            high,
            value_step,
            tuple(
                (jnp.zeros((span, lanes), F32), jnp.zeros((span, width), F32)) for h in range(heads)
            ),
        )
        result = jnp.zeros((span, width), F32)
        for h in range(heads):
            total = jnp.sum(state[h][0], axis=1, keepdims=True)
            result = jnp.where(head_lanes((span, width), h, head_dim), state[h][1] / total, result)
            log_total = tops[h] + jnp.log(total)
            lse_ref[i, h : h + 1, :] = jnp.transpose(jnp.broadcast_to(log_total, (span, 128)))[
                0:1, :
            ]
        result_ref[i] = (result * scale_ref[...]).astype(BF16)
        return carry

    lax.fori_loop(0, blocks, query_block, 0)


def attend(order, offsets, rows, qkv, scale_lanes, heads, head_dim):
    group, _, span, width = qkv[0].shape
    length = group * span
    wide = max(span, min(512, length))
    return pl.pallas_call(
        functools.partial(attend_kernel, rows, heads, head_dim),
        in_specs=[SMEM, SMEM, VMEM] + [VMEM] * len(rows),
        out_shape=[
            jax.ShapeDtypeStruct((group, len(rows), span, width), BF16),
            jax.ShapeDtypeStruct((len(rows), group, heads, span), F32),
        ],
        scratch_shapes=[pltpu.VMEM((heads, length // wide, span, wide), F32)],
        compiler_params=kernel_params(),
        cost_estimate=cost(0, 1024),
        name="attend",
    )(order, offsets, scale_lanes, *qkv)


def attend_back_kernel(rows, heads, head_dim, order_ref, offs_ref, inv_ref, grad_ref, *refs):
    count = len(rows)
    held, out_refs, lse_refs = refs[:count], refs[count : 2 * count], refs[2 * count : 3 * count]
    dqkv_ref, total_ref = refs[3 * count : 3 * count + 2]
    for n, row in enumerate(rows):
        attend_back_row(
            order_ref[row],
            heads,
            head_dim,
            offs_ref,
            inv_ref,
            lse_refs[n],
            held[n],
            grad_ref.at[:, n],
            out_refs[n],
            dqkv_ref.at[:, n],
            total_ref.at[n],
            *refs[3 * count + 2 :],
        )


def attend_back_row(
    row,
    heads,
    head_dim,
    offs_ref,
    inv_ref,
    lse_ref,
    held,
    grad_ref,
    out_ref,
    dqkv_ref,
    total_ref,
    q_ref,
    k_ref,
    g_ref,
    delta_ref,
    dq_ref,
):
    blocks, _, span, width = held.shape
    score_scale = head_dim ** (-0.5)
    picks = lax.broadcasted_iota(jnp.int32, (8, width), 0)
    lane = lax.broadcasted_iota(jnp.int32, (8, width), 1)
    ones = jnp.where(lane // head_dim == picks, 1.0, 0.0).astype(F32)

    def prepare(i, carry):
        queries = held[i, 0] * jnp.asarray(score_scale, BF16)
        keys = held[i, 1]
        grads = grad_ref[i]
        for h in range(heads):
            mine = head_lanes((span, width), h, head_dim)
            q_ref[h, i] = jnp.where(mine, queries, 0).astype(BF16)
            k_ref[h, i] = jnp.where(mine, keys, 0).astype(BF16)
            g_ref[h, i] = jnp.where(mine, grads, 0).astype(BF16)
        product = grads.astype(F32) * out_ref[i].astype(F32) * inv_ref[...]
        delta_ref[i] = lax.dot_general(
            ones, product, LAST, precision=lax.Precision.HIGHEST, preferred_element_type=F32
        )
        dq_ref[i] = jnp.zeros((span, width), F32)
        return carry + delta_ref[i]

    total_ref[...] = lax.fori_loop(0, blocks, prepare, jnp.zeros((8, span), F32))

    def key_block(j, carry):
        keys = held[j, 1]
        values = held[j, 2]
        key_pos = j * span + lax.broadcasted_iota(jnp.int32, (span, 1), 0)
        last = (doc_end(offs_ref, row, (j + 1) * span - 1, blocks * span) - 1) // span + 1

        def query_step(i, state):
            dk, dv = state
            query_pos = i * span + lax.broadcasted_iota(jnp.int32, (1, span), 1)
            query_start = doc_start(offs_ref, row, query_pos)
            allowed = (key_pos >= query_start) & (key_pos <= query_pos)
            dq = dq_ref[i]
            for h in range(heads):
                scores = dot_last(keys, q_ref[h, i])
                scores = jnp.where(allowed, scores - lse_ref[i, h : h + 1, :], MASKED)
                probs = jnp.exp(scores)
                d_probs = dot_last(values, g_ref[h, i])
                d_scores = (probs * (d_probs - delta_ref[i, h : h + 1, :])).astype(BF16)
                dv = dv + dot(probs.astype(BF16), g_ref[h, i])
                dk = dk + dot(d_scores, q_ref[h, i])
                dq = dq + dot_first(d_scores, k_ref[h, j])
            dq_ref[i] = dq
            return (dk, dv)

        zero = jnp.zeros((span, width), F32)
        dk, dv = lax.fori_loop(j, last, query_step, (zero, zero))
        dqkv_ref[j, 1] = dk.astype(BF16)
        dqkv_ref[j, 2] = dv.astype(BF16)
        dqkv_ref[j, 0] = (dq_ref[j] * score_scale).astype(BF16)
        return carry

    lax.fori_loop(0, blocks, key_block, 0)


def attend_back(
    order, offsets, rows, qkv, grads, at, scaled, inverse_lanes, lse, heads, head_dim
):
    group, _, span, width = qkv[0].shape
    count = len(rows)
    return pl.pallas_call(
        functools.partial(attend_back_kernel, rows, heads, head_dim),
        grid=(1,),
        in_specs=[SMEM, SMEM, VMEM]
        + [pl.BlockSpec((group, count, span, width), lambda i: (0, at, 0, 0))]
        + [VMEM] * (3 * count),
        out_specs=[VMEM] * 2,
        out_shape=[
            jax.ShapeDtypeStruct((group, count, 3, span, width), BF16),
            jax.ShapeDtypeStruct((count, 8, span), F32),
        ],
        scratch_shapes=[pltpu.VMEM((heads, group, span, width), BF16)] * 3
        + [pltpu.VMEM((group, 8, span), F32), pltpu.VMEM((group, span, width), F32)],
        compiler_params=kernel_params(),
        cost_estimate=cost(0, 1024),
        name="attend_back",
    )(order, offsets, inverse_lanes, grads, *qkv, *scaled, *lse)


def join_grads_kernel(parts, in_ref, out_ref, value_ref):
    group = in_ref.shape[0]
    for n in range(3):
        whole = jnp.concatenate([in_ref[s, 0, n] for s in range(group)], axis=1)
        piece = whole.shape[1] // parts
        if n == 2:
            value_ref[...] = whole
            continue
        for p in range(parts):
            to = (p * 2 + n) * piece
            out_ref[:, to : to + piece] = whole[:, p * piece : (p + 1) * piece]


def join_grads(block):
    group, _, _, span, width = block.shape
    return pl.pallas_call(
        functools.partial(join_grads_kernel, PARTS),
        out_shape=[
            jax.ShapeDtypeStruct((span, 2 * group * width), BF16),
            jax.ShapeDtypeStruct((span, group * width), BF16),
        ],
        compiler_params=kernel_params(),
        cost_estimate=cost(0, 1024),
        name="join_grads",
    )(block)


FF_STEP = 512


def layer_kernel(
    order_ref,
    o_ref,
    x_ref,
    d_out_ref,
    post_ref,
    ffn_ref,
    mid_gain_ref,
    scale_ref,
    w_out_ref,
    d_mid_hbm,
    w_fc1_hbm,
    scaled_ref,
    ffn_in_ref,
    residual_ref,
    mid_ref,
    d_pre_ref,
    d_proj_ref,
    d_residual_ref,
    d_attn_ref,
    g_post_ref,
    g_ffn_ref,
    g_mid_ref,
    d_mid_ref,
    w_fc1_ref,
    act_ref,
    slope_ref,
    sems,
    *,
    slot,
):
    group, _, span, width = o_ref.shape
    hidden = act_ref.shape[1]
    steps = [slice(c, c + FF_STEP) for c in range(0, hidden, FF_STEP)]
    weight_copies = [
        pltpu.make_async_copy(w_fc1_hbm.at[:, at], w_fc1_ref.at[:, at], sems.at[c])
        for c, at in enumerate(steps)
    ]
    mid_copy = pltpu.make_async_copy(
        d_mid_hbm.at[pl.ds(pl.multiple_of(order_ref[slot] * span, span), span), :],
        d_mid_ref,
        sems.at[len(steps)],
    )
    for copy in weight_copies:
        copy.start()
    mid_copy.start()

    scaled = jnp.concatenate([o_ref[s, 0] for s in range(group)], axis=1)
    scaled_ref[...] = scaled
    proj_hat, proj_spread = norm_parts(dot(scaled, w_out_ref[...]))
    residual = x_ref[...].astype(F32) + proj_hat * post_ref[...]
    residual_ref[...] = residual
    res_hat, res_spread = norm_parts(residual)
    ffn_in = (res_hat * ffn_ref[...]).astype(BF16)
    ffn_in_ref[...] = ffn_in

    total = jnp.zeros((span, 1), F32)
    for c, at in enumerate(steps):
        weight_copies[c].wait()
        pre = dot(ffn_in, w_fc1_ref[:, at])
        phi = 0.5 + 0.5 * lax.erf(pre * (0.5**0.5))
        act = pre * phi
        act_ref[:, at] = act
        slope_ref[:, at] = phi + pre * jnp.exp(-0.5 * pre * pre) * 0.3989422804014327
        total += jnp.sum(act, axis=1, keepdims=True)
    average = total / hidden
    total = jnp.zeros((span, 1), F32)
    for at in steps:
        centred = act_ref[:, at] - average
        total += jnp.sum(centred * centred, axis=1, keepdims=True)
    spread = lax.rsqrt(total / hidden + EPSILON)

    mid_copy.wait()
    sum_weighted = jnp.zeros((span, 1), F32)
    sum_hat = jnp.zeros((span, 1), F32)
    for at in steps:
        hat = (act_ref[:, at] - average) * spread
        act_ref[:, at] = hat
        gain = mid_gain_ref[:, at]
        mid_ref[:, at] = (hat * gain).astype(BF16)
        grad = d_mid_ref[:, at]
        product = grad * hat
        g_mid_ref[:, at] = jnp.sum(product, axis=0, keepdims=True)
        sum_weighted += jnp.sum(grad * gain, axis=1, keepdims=True)
        sum_hat += jnp.sum(product * gain, axis=1, keepdims=True)
    sum_weighted = sum_weighted / hidden
    sum_hat = sum_hat / hidden
    d_ffn = jnp.zeros(x_ref.shape, F32)
    for at in steps:
        weighted = d_mid_ref[:, at] * mid_gain_ref[:, at]
        d_act = spread * (weighted - sum_weighted - act_ref[:, at] * sum_hat)
        d_pre = (d_act * slope_ref[:, at]).astype(BF16)
        d_pre_ref[:, at] = d_pre
        d_ffn += dot_last(d_pre, w_fc1_ref[:, at])

    g_ffn_ref[...] = jnp.sum(d_ffn * res_hat, axis=0, keepdims=True)
    d_residual = d_out_ref[...].astype(F32) + norm_back(res_hat, res_spread, ffn_ref[...], d_ffn)
    d_residual_ref[...] = d_residual
    g_post_ref[...] = jnp.sum(d_residual * proj_hat, axis=0, keepdims=True)
    d_proj = norm_back(proj_hat, proj_spread, post_ref[...], d_residual).astype(BF16)
    d_proj_ref[...] = d_proj
    d_attn = (dot_last(d_proj, w_out_ref[...]) * scale_ref[...]).astype(BF16)
    for s in range(group):
        d_attn_ref[s, 0] = d_attn[:, s * width : (s + 1) * width]


def layer(order, slot, o_blocks, at, x, d_out, gains, w_out, d_mid, w_fc1):
    group, _, span, width = o_blocks.shape
    model = x.shape[2]
    hidden = w_fc1.shape[1]
    shape = jax.ShapeDtypeStruct
    return pl.pallas_call(
        functools.partial(layer_kernel, slot=slot),
        grid_spec=pltpu.PrefetchScalarGridSpec(
            num_scalar_prefetch=1,
            grid=(1,),
            in_specs=[pl.BlockSpec((group, 1, span, width), lambda i, o: (0, at, 0, 0))]
            + [pl.BlockSpec((None, span, model), lambda i, o: (o[slot], 0, 0))] * 2
            + [VMEM] * 5
            + [pl.BlockSpec(memory_space=pl.ANY)] * 2,
            out_specs=[VMEM] * 11,
            scratch_shapes=[
                pltpu.VMEM((span, hidden), F32),
                pltpu.VMEM(w_fc1.shape, BF16),
                pltpu.VMEM((span, hidden), F32),
                pltpu.VMEM((span, hidden), F32),
                pltpu.SemaphoreType.DMA((hidden // FF_STEP + 1,)),
            ],
        ),
        out_shape=[
            shape((span, model), BF16),
            shape((span, model), BF16),
            shape((span, model), F32),
            shape((span, hidden), BF16),
            shape((span, hidden), BF16),
            shape((span, model), BF16),
            shape((span, model), F32),
            shape((group, 1, span, width), BF16),
            shape((1, model), F32),
            shape((1, model), F32),
            shape((1, hidden), F32),
        ],
        compiler_params=kernel_params(),
        cost_estimate=cost(0, 1024),
        name="layer",
    )(order, o_blocks, x, d_out, *gains, w_out, d_mid, w_fc1)


def layer_out_kernel(order_ref, *refs):
    count = (len(refs) - 2) // 2
    weight, out_ref = refs[-2], refs[-1]
    for r in range(count):
        out_ref[order_ref[r]] = (refs[r][...] + dot(refs[count + r][...], weight[...])).astype(BF16)


def last_step(order, residuals, mids, w_fc2):
    return pl.pallas_call(
        layer_out_kernel,
        in_specs=[SMEM] + [VMEM] * (2 * len(mids) + 1),
        out_shape=jax.ShapeDtypeStruct((len(mids),) + residuals[0].shape, BF16),
        compiler_params=kernel_params(),
        cost_estimate=cost(0, 1024),
        name="layer_out",
    )(order, *residuals, *mids, w_fc2)


def flip(value, axis, bit):
    size = lax.axis_size(axis)
    return lax.ppermute(value, axis, [(i, i ^ (1 << bit)) for i in range(size)])


def bits(axis):
    return (lax.axis_size(axis) - 1).bit_length()


PARTS = 4


def weight_kernel(count, rows, added, shards, part_ref, *refs):
    out_ref = refs[-1]
    high = out_ref.shape[1]
    per = rows * (shards + 1)
    extras = refs[per * count : per * count + added]
    at = 0
    for n in range(count):
        mine = refs[n * per : (n + 1) * per]
        rights = mine[rows * shards :]
        width = rights[0].shape[1]
        total = 0.0
        for r in range(rows):
            left = [ref[...] for ref in mine[r * shards : (r + 1) * shards]]
            left = jnp.concatenate(left, axis=1) if shards > 1 else left[0]
            total += dot_first(left, rights[r][...])
        for i in range(shards):
            piece = total[i * high : (i + 1) * high]
            for extra in extras:
                piece = piece + extra[i, :, at : at + width].astype(F32)
            out_ref[i, :, at : at + width] = piece.astype(BF16)
        at += width


def weight_part_plain(pairs, part, parts, extras, group):
    pieces = []
    for lefts, rights, kind in pairs:
        left, right = jnp.concatenate(lefts), jnp.concatenate(rights)
        if kind == "columns":
            wide = right.shape[1] // parts
            right = lax.dynamic_slice(right, (0, part * wide), (right.shape[0], wide))
            left = left.reshape(left.shape[0], group, -1)
        else:
            left = left.reshape(left.shape[0], group, parts, -1)
            left = lax.dynamic_index_in_dim(left, part, 2, keepdims=False)
        pieces.append(jnp.einsum("tsd,te->sde", left, right, preferred_element_type=F32))
    total = jnp.concatenate(pieces, axis=2)
    for extra in extras:
        total = total + extra.astype(F32)
    return total.astype(BF16)


def weight_part(pairs, part, parts, extras, group):
    shards = 2
    specs, arrays, width = [], [], 0
    for lefts, rights, kind in pairs:
        span, model = lefts[0].shape
        stride = 1 if kind == "columns" else parts
        high = model // group // stride
        wide = rights[0].shape[1] // (parts if kind == "columns" else 1)
        for left in lefts:
            for i in range(shards):

                def left_at(g, p, i=i, stride=stride):
                    return (0, (g * shards + i) * stride + (p[0] if stride > 1 else 0))

                specs.append(pl.BlockSpec((span, high), left_at))
                arrays.append(left)
        for right in rights:

            def right_at(g, p, stride=stride):
                return (0, p[0] if stride == 1 else 0)

            specs.append(pl.BlockSpec((span, wide), right_at))
            arrays.append(right)
        width += wide
    if high % 128:
        return weight_part_plain(pairs, part, parts, extras, group)
    block = pl.BlockSpec((shards, high, width), lambda g, p: (g, 0, 0))
    return pl.pallas_call(
        functools.partial(weight_kernel, len(pairs), len(pairs[0][0]), len(extras), shards),
        grid_spec=pltpu.PrefetchScalarGridSpec(
            num_scalar_prefetch=1,
            grid=(group // shards,),
            in_specs=specs + [block] * len(extras),
            out_specs=block,
        ),
        out_shape=jax.ShapeDtypeStruct((group, high, width), BF16),
        compiler_params=kernel_params(),
        cost_estimate=cost(0, 1024),
        name="weight_part",
    )(part.astype(jnp.int32).reshape(1), *arrays, *extras)


class WeightSum:
    def __init__(self, *pairs):
        self.pairs = pairs
        batch_at = lax.axis_index("batch")
        self.near, self.far = batch_at & 1, (batch_at >> 1) & 1

    def piece(self, order, near, far, *extras):
        def part_of(part):
            return weight_part(self.pairs, part, PARTS, extras, lax.axis_size("blk"))

        return order(part_of, near * 2 + far)

    def half(self, order, near, *extras):
        def part_of(part):
            return weight_part(self.pairs, part, 2, extras, lax.axis_size("blk"))

        return order(part_of, near)

    def away_far(self, order):
        return self.piece(order, 1 - self.near, 1 - self.far)

    def send_far(self, order, away):
        return self.piece(order, self.near, 1 - self.far, away)

    def away_near(self, order):
        return self.piece(order, 1 - self.near, self.far)

    def keep(self, order, away, arrived):
        return self.piece(order, self.near, self.far, away, arrived)


def over_near(sent):
    return flip(sent, "batch", 0)


def over_far(sent):
    return flip(sent, "batch", 1)


class Order:
    def __init__(self):
        self.last = ()

    def __call__(self, step, *values):
        self.last = step(*tie(values, self.last))
        return self.last


def window(always, step):
    def nothing():
        return jax.tree.map(lambda leaf: jnp.zeros(leaf.shape, leaf.dtype), jax.eval_shape(step))

    return lax.cond(always, step, nothing)


def tie(values, *after):
    return lax.optimization_barrier((values, after))[0]


def combine_kernel(plan, at_ref, *refs):
    ins = sum(max(beside, 2) if kind != "first" else beside for kind, beside, _ in plan)
    into, out_of = list(refs[:ins]), list(refs[ins:])
    for n, (kind, beside, cut) in enumerate(plan):
        terms = [into.pop(0) for _ in range(beside if kind == "first" else 2)]
        if kind == "stack":
            out = out_of.pop(0)
            out[0], out[1] = terms[0][0], terms[1][0]
            continue

        def put(ref, j, i):
            if kind == "add":
                ref[j] = (terms[0][i].astype(F32) + terms[1][i].astype(F32)).astype(BF16)
                return
            at = 0
            for term in terms:
                ref[j, :, at : at + term.shape[2]] = term[i]
                at += term.shape[2]

        if cut:
            keep, send = out_of.pop(0), out_of.pop(0)
            for j in range(keep.shape[0]):
                put(keep, j, 2 * j + at_ref[n])
                put(send, j, 2 * j + 1 - at_ref[n])
        else:
            whole = out_of.pop(0)
            for j in range(whole.shape[0]):
                put(whole, j, j)


class Tree:
    def __init__(self, *mine, halved=2):
        self.steps = [("blk", bit) for bit in range(bits("blk"))]
        self.steps += [("batch", bit) for bit in range(halved, bits("batch"))]
        self.steps += [("far", 1), ("near", 0)][2 - halved :]
        self.terms, self.last = list(mine), "first"

    def start(self):
        kind, bit = self.steps[0]
        return flip(self.send, "blk" if kind == "blk" else "batch", bit)

    def end(self, arrived):
        self.last = self.steps.pop(0)[0]
        self.terms = [self.kept, arrived]


def combine(trees):
    me = lax.axis_index("blk")
    plan, ins, shapes, at = [], [], [], []
    for tree in trees:
        kind, bit = tree.steps[0]
        cut = kind == "blk"
        state = {"first": "first", "far": "stack"}.get(tree.last, "add")
        plan.append((state, len(tree.terms), cut))
        ins += tree.terms
        count, high, wide = tree.terms[0].shape
        if state == "first":
            wide = sum(term.shape[2] for term in tree.terms)
        count = count // 2 if cut else 2 if state == "stack" else count
        shapes += [jax.ShapeDtypeStruct((count, high, wide), BF16)] * (2 if cut else 1)
        at.append((me >> bit) & 1 if cut else me * 0)
    outs = list(
        pl.pallas_call(
            functools.partial(combine_kernel, plan),
            in_specs=[SMEM] + [VMEM] * len(ins),
            out_shape=shapes,
            compiler_params=kernel_params(),
            cost_estimate=cost(0, 1024),
            name="combine",
        )(jnp.stack(at).astype(jnp.int32), *ins)
    )
    for tree, (_, _, cut) in zip(trees, plan):
        tree.kept = outs.pop(0)
        tree.send = outs.pop(0) if cut else tree.kept


def place_kernel(layout, part_ref, *refs):
    ins, outs = list(refs[: 2 * len(layout)]), list(refs[2 * len(layout) :])
    near, far = part_ref[0], part_ref[1]
    order = [near * 2 + far, near * 2 + 1 - far, (1 - near) * 2 + far, (1 - near) * 2 + 1 - far]
    for spans in layout:
        both = [ins.pop(0), ins.pop(0)]
        count = 2 * both[0].shape[0]
        for start, width, kind in spans:
            out = outs.pop(0)
            for n, part in enumerate(order if count == 4 else [near, 1 - near]):
                value = both[n * 2 // count][n % (count // 2), :, start : start + width]
                value = value.astype(F32)
                if kind == "columns":
                    out[:, pl.ds(pl.multiple_of(part * width, 128), width)] = value
                else:
                    high = value.shape[0]
                    out[pl.ds(pl.multiple_of(part * high, 8), high), :] = value


def place(trees, layout):
    batch_at = lax.axis_index("batch")
    parts = jnp.stack([batch_at & 1, (batch_at >> 1) & 1]).astype(jnp.int32)
    ins, shapes = [], []
    for tree, spans in zip(trees, layout):
        ins += tree.terms
        count, high = 2 * tree.kept.shape[0], tree.kept.shape[1]
        for _, width, kind in spans:
            shape = (high, count * width) if kind == "columns" else (count * high, width)
            shapes.append(jax.ShapeDtypeStruct(shape, F32))
    return pl.pallas_call(
        functools.partial(place_kernel, layout),
        in_specs=[SMEM] + [VMEM] * len(ins),
        out_shape=shapes,
        compiler_params=kernel_params(),
        cost_estimate=cost(0, 1024),
        name="place",
    )(parts, *ins)


class SmallSum:
    def __init__(self, mine):
        self.mine = mine
        self.steps = [("batch", bit) for bit in range(bits("batch"))]
        self.steps += [("blk", bit) for bit in range(bits("blk"))]

    def start(self):
        return flip(self.mine, *self.steps[0])

    def end(self, arrived):
        self.steps.pop(0)
        self.mine = self.mine + arrived


def input_grad_kernel(parts, rows, order_ref, x_ref, gain_ref, wq_ref, wk_ref, wv_ref, *refs):
    out_ref, sum_ref = refs[3 * rows :]
    model = wq_ref.shape[0]
    piece = model // parts
    total = jnp.zeros(sum_ref.shape, F32)
    for r in range(rows):
        d_ref, value_ref, res_ref = refs[r], refs[rows + r], refs[2 * rows + r]
        grad = dot_last(value_ref[...], wv_ref[...])
        for p in range(parts):
            for n, weight in enumerate((wq_ref, wk_ref)):
                at = (p * 2 + n) * piece
                grad += dot_last(d_ref[:, at : at + piece], weight[:, p * piece : (p + 1) * piece])
        row = order_ref[r]
        hat, spread = norm_parts(x_ref[row].astype(F32))
        out_ref[row] = res_ref[...] + norm_back(hat, spread, gain_ref[...], grad)
        total += jnp.sum(grad * hat, axis=0, keepdims=True)
    sum_ref[...] = total


def input_grad(order, x, gain, w_query, w_key, w_value, d_rows, d_values, d_residuals):
    return pl.pallas_call(
        functools.partial(input_grad_kernel, PARTS, len(d_rows)),
        in_specs=[SMEM] + [VMEM] * (5 + 3 * len(d_rows)),
        out_shape=[
            jax.ShapeDtypeStruct(x.shape, F32),
            jax.ShapeDtypeStruct((1, x.shape[2]), F32),
        ],
        compiler_params=kernel_params(),
        cost_estimate=cost(0, 1024),
        name="input_grad",
    )(order, x, gain, w_query, w_key, w_value, *d_rows, *d_values, *d_residuals)


def on_device(
    inputs,
    ln_attn,
    w_query,
    w_key,
    w_value,
    w_out,
    head_scale,
    ln_post,
    ln_ffn,
    w_fc1,
    ln_mid,
    w_fc2,
    offsets,
    cotangent,
):
    row_count, span, model = inputs.shape
    head_count = head_scale.shape[0]
    head_dim = model // head_count
    tokens = row_count * span
    group = lax.axis_size("blk")
    heads = head_count // group
    width = heads * head_dim
    my_index = lax.axis_index("blk")
    rows = range(row_count)

    always = offsets[0, 0] == 0
    gain = ln_attn.reshape(1, model)
    last = row_count - 1
    my_scale = lax.dynamic_slice(head_scale, (my_index * heads,), (heads,))
    scale_lanes = jnp.repeat(my_scale, head_dim).reshape(1, width)
    layer_gains = [
        ln_post.reshape(1, model),
        ln_ffn.reshape(1, model),
        ln_mid.reshape(1, -1),
        jnp.repeat(head_scale, head_dim).reshape(1, model),
    ]

    def project_row(r, x):
        return project(offsets, r, x, gain, w_query, w_key, w_value, group)

    def attend_one(r, held):
        return attend(by_work, offsets, [r], [held], scale_lanes, heads, head_dim)

    def layer_row(r, o_blocks):
        at = r if r < last else 0
        return layer(by_work, r, o_blocks, at, inputs, cotangent, layer_gains, w_out, d_mid, w_fc1)

    def back(order, r, row_heads, at=0):
        def back_row(held):
            return attend_back(
                by_work,
                offsets,
                [r],
                [held],
                row_heads,
                at,
                [scaled_mine[r].reshape(group, span, width)],
                1.0 / scale_lanes,
                [lse[r].reshape(lse[r].shape[1:])],
                heads,
                head_dim,
            )

        return order(back_row, qkv[r])

    def first_window():
        order = Order()
        return exchange(sent), [
            order(functools.partial(project_row, r), inputs) for r in rows[1:]
        ]

    normed_first, sent, by_work = project_row(0, inputs)
    held, projected = window(always, first_window)
    qkv = [held]
    normed = [normed_first] + [part[0] for part in projected]
    scaled_mine, lse = [], []
    for r in rows[1:]:

        def next_window():
            order = Order()
            extra = ()
            if r == 1:
                extra = jnp.einsum(
                    "td,fd->tf",
                    cotangent.reshape(tokens, model),
                    w_fc2,
                    preferred_element_type=F32,
                )
            return exchange(projected[r - 1][1]), attend_one(r - 1, qkv[r - 1]), extra

        held, (out, log_total), extra = window(always, next_window)
        d_mid = extra if r == 1 else d_mid
        qkv.append(held)
        scaled_mine.append(out)
        lse.append(log_total)

    def early_window():
        return (
            exchange(jnp.concatenate(scaled_mine, axis=1)),
            attend_one(last, qkv[last]),
        )

    early, (out, log_total) = window(always, early_window)
    scaled_mine.append(out)
    lse.append(log_total)

    def late_window():
        return exchange(scaled_mine[last]), layer_row(0, early)

    late, layer_first = window(always, late_window)

    def layer_window():
        order = Order()
        first = exchange(layer_first[7])
        rest = []
        for r in rows[1:]:

            def one(o_blocks):
                return layer_row(r, o_blocks)

            rest.append(order(one, early if r < last else late))
        return first, rest

    first_heads, rest = window(always, layer_window)
    (
        scaled,
        ffn_in,
        residual,
        mid,
        d_pre,
        d_proj,
        d_residual,
        d_attn,
        g_post,
        g_ffn,
        g_mid,
    ) = zip(layer_first, *rest)
    d_out = [lax.dynamic_index_in_dim(cotangent, by_work[r], keepdims=False) for r in rows]
    sum_one = WeightSum((mid, d_out, "rows"))
    sum_two = WeightSum((ffn_in, d_pre, "columns"))
    sum_three = WeightSum((scaled, d_proj, "columns"))
    order = Order()
    away = over_near(sum_one.away_far(order))
    away_two = sum_two.away_far(order)
    sent_one = sum_one.send_far(order, away)

    def back_first():
        order = Order()
        arrived = over_far(sent_one)
        heads_in = exchange(jnp.concatenate(d_attn[1:], axis=1))
        away = over_near(away_two)
        out = back(order, 0, first_heads)
        return arrived, heads_in, out, sum_two.send_far(order, away)

    far_one, rest_heads, (sent, total), sent_two = window(always, back_first)
    totals = [total]

    def back_second():
        order = Order()
        arrived = over_far(sent_two)
        grad = exchange(sent)
        away = over_near(sum_one.away_near(order))
        out = back(order, 1, rest_heads, 0)
        near = sum_two.away_near(order), sum_three.half(order, 1 - sum_three.near)
        return grad, out, arrived, near, sum_one.keep(order, away, far_one)

    grad, (sent, total), far_two, near, mine_one = window(always, back_second)
    near_two, away_three = near
    totals.append(total)
    grads = [grad]
    tree_one = Tree(mine_one)
    combine([tree_one])
    for r in rows[2:]:

        def back_next():
            order = Order()
            moved, over, out_of = (), (), ()
            if r == 2:
                moved = tree_one.start()
                over = over_near(near_two), over_near(away_three)
            grad = exchange(sent)
            out = back(order, r, rest_heads, r - 1)
            if r == 2:
                mine = sum_two.keep(order, over[0], far_two)
                out_of = mine, sum_three.half(order, sum_three.near, over[1])
            return grad, moved, out_of, out

        grad, moved, out_of, (sent, total) = window(always, back_next)
        totals.append(total)
        grads.append(grad)
        if r == 2:
            tree_one.end(moved)
            mine_two, mine_three = out_of
    tree_two = Tree(mine_two)
    combine([tree_one, tree_two])

    def back_last():
        order = Order()
        moved = tree_one.start(), tree_two.start()
        grad = exchange(sent)
        joined = [order(join_grads, part) for part in grads]

        def output_step(weight):
            return last_step(by_work, residual, mid, weight)

        return grad, moved, joined, order(output_step, w_fc2)

    grad, moved, joined, layer_out = window(always, back_last)
    tree_one.end(moved[0])
    tree_two.end(moved[1])
    order = Order()
    joined = joined + [order(join_grads, grad)]
    d_rows, d_values = zip(*joined)
    sum_qk = WeightSum((normed, d_rows, "columns"))
    sum_v = WeightSum((normed, d_values, "columns"))
    away_qk = over_near(sum_qk.away_far(order))
    away_v = over_near(sum_v.half(order, 1 - sum_v.near))
    sent_qk = sum_qk.send_far(order, away_qk)
    tree_v = Tree(sum_v.half(order, sum_v.near, away_v), mine_three, halved=1)
    combine([tree_one, tree_two, tree_v])

    def advance(trees, extra=lambda: ()):
        def step():
            return [tree.start() for tree in trees], extra()

        moved, out = window(always, step)
        for tree, arrived in zip(trees, moved):
            tree.end(arrived)
        return out

    def beside():
        order = Order()
        arrived = over_far(sent_qk)
        near = over_near(sum_qk.away_near(order))

        def input_step(x):
            return input_grad(
                by_work, x, gain, w_query, w_key, w_value, d_rows, d_values, d_residual
            )

        return arrived, near, order(input_step, inputs)

    far_qk, near_qk, (grad_inputs, grad_ln_attn) = advance(
        [tree_one, tree_two, tree_v], beside
    )
    tree_qk = Tree(sum_qk.keep(order, near_qk, far_qk))
    delta_sum = sum(jnp.sum(total, axis=(0, 2)) for total in totals)
    my_grad = delta_sum[:heads] / my_scale
    scale_part = lax.dynamic_update_slice(
        jnp.zeros((head_count,), F32), my_grad, (my_index * heads,)
    )
    small = SmallSum(
        jnp.concatenate(
            [grad_ln_attn[0], sum(g_post)[0], sum(g_ffn)[0], sum(g_mid)[0], scale_part]
        )
    )
    piece = model // PARTS
    ff_piece = w_fc1.shape[1] // PARTS
    trees = [tree_qk, tree_v, tree_two, tree_one]
    placed = None
    while any(tree.steps for tree in trees + [small]):
        combine([tree for tree in trees if tree.steps])

        def place_early():
            if tree_two.steps or tree_one.steps or placed is not None:
                return ()
            return place(
                [tree_one, tree_two], [[(0, model, "rows")], [(0, ff_piece, "columns")]]
            )

        early_out = advance([tree for tree in trees + [small] if tree.steps], place_early)
        placed = early_out or placed
    if placed is None:
        placed = place([tree_one, tree_two], [[(0, model, "rows")], [(0, ff_piece, "columns")]])
    grad_fc2, grad_fc1 = placed
    *grads_qkv, value, grad_out = place(
        [tree_qk, tree_v],
        [
            [(n * piece, piece, "columns") for n in range(2)],
            [(n * 2 * piece, 2 * piece, "columns") for n in range(2)],
        ],
    )
    grads_qkv.append(value)
    gains = small.mine
    ends = [0, model, 2 * model, 3 * model, 3 * model + ln_mid.shape[0]]
    ends.append(ends[-1] + head_count)
    gains = [gains[low:high] for low, high in zip(ends[:-1], ends[1:])]

    def shard_of(vector):
        part = vector.shape[0] // group
        return lax.dynamic_slice(vector, (my_index * part,), (part,))

    return (
        layer_out,
        grad_inputs,
        shard_of(gains[0]),
        grads_qkv[0],
        grads_qkv[1],
        grads_qkv[2],
        grad_out,
        gains[4],
        shard_of(gains[1]),
        shard_of(gains[2]),
        grad_fc1,
        shard_of(gains[3]),
        grad_fc2,
    )


def solution(mesh):
    rows = P("batch", "blk", None)
    shard = P("blk", None)
    return jax.shard_map(
        on_device,
        mesh=mesh,
        in_specs=(rows,) + (P(),) * 11 + (P("batch", None), rows),
        out_specs=(
            rows,
            rows,
            P("blk"),
            shard,
            shard,
            shard,
            shard,
            P(),
            P("blk"),
            P("blk"),
            shard,
            P("blk"),
            shard,
        ),
        check_vma=False,
    )
```

```python
import functools

import jax
import jax.numpy as jnp
from jax import lax
from jax.experimental import pallas as pl
from jax.experimental.pallas import tpu as pltpu
from jax.sharding import PartitionSpec as P

EPSILON = 1e-05
MASKED = -1e30
VMEM_BYTES = 50 * 1024 * 1024
F32 = jnp.float32
BF16 = jnp.bfloat16
LAST = (((1,), (1,)), ((), ()))
FIRST = (((0,), (0,)), ((), ()))
SMEM = pl.BlockSpec(memory_space=pltpu.SMEM)
VMEM = pl.BlockSpec(memory_space=pltpu.VMEM)


def dot_last(left, right):
    return lax.dot_general(left, right, LAST, preferred_element_type=F32)


def dot_first(left, right):
    return lax.dot_general(left, right, FIRST, preferred_element_type=F32)


def dot(left, right):
    return jnp.dot(left, right, preferred_element_type=F32)


def kernel_params():
    return pltpu.CompilerParams(vmem_limit_bytes=VMEM_BYTES)


def cost(flops, size):
    return pl.CostEstimate(flops=int(flops), bytes_accessed=int(size), transcendentals=0)


def exchange(parts):
    return lax.all_to_all(parts, "blk", 0, 0, tiled=True)


def norm_parts(rows_in):
    average = jnp.mean(rows_in, axis=-1, keepdims=True)
    centred = rows_in - average
    spread = lax.rsqrt(jnp.mean(centred * centred, axis=-1, keepdims=True) + EPSILON)
    return centred * spread, spread


def norm_back(hat, spread, gain, grad):
    weighted = grad * gain
    return spread * (
        weighted
        - jnp.mean(weighted, axis=-1, keepdims=True)
        - hat * jnp.mean(weighted * hat, axis=-1, keepdims=True)
    )


def rows_by_work(offs_ref, length):
    rows, docs = offs_ref.shape
    work = []
    for r in range(rows):
        total = jnp.int32(0)
        for d in range(docs):
            end = offs_ref[r, d + 1] if d + 1 < docs else length
            total += (end - offs_ref[r, d]) * (end - offs_ref[r, d])
        work.append(total)
    ranks = []
    for r in range(rows):
        rank = jnp.int32(0)
        for other in range(rows):
            if other < r:
                rank += (work[other] >= work[r]).astype(jnp.int32)
            elif other > r:
                rank += (work[other] > work[r]).astype(jnp.int32)
        ranks.append(rank)
    return [
        sum(jnp.where(ranks[r] == slot, jnp.int32(r), jnp.int32(0)) for r in range(rows))
        for slot in range(rows)
    ]


def project_kernel(
    slot,
    offs_ref,
    gain_ref,
    x_hbm,
    wq_hbm,
    wk_hbm,
    wv_hbm,
    normed_ref,
    out_ref,
    order_ref,
    x_ref,
    weight_ref,
    sems,
):
    group, _, span, width = out_ref.shape
    order = rows_by_work(offs_ref, group * span)
    copy_x = pltpu.make_async_copy(x_hbm.at[order[slot]], x_ref, sems.at[3])
    copy_x.start()
    copies = [
        pltpu.make_async_copy(weight, weight_ref.at[n], sems.at[n])
        for n, weight in enumerate((wq_hbm, wk_hbm, wv_hbm))
    ]
    for copy in copies:
        copy.start()
    for r, row in enumerate(order):
        order_ref[r] = row
    copy_x.wait()
    hat, _ = norm_parts(x_ref[...].astype(F32))
    normed = (hat * gain_ref[...]).astype(BF16)
    normed_ref[...] = normed
    for n in range(3):
        copies[n].wait()
        product = dot(normed, weight_ref[n]).astype(BF16)
        for s in range(group):
            out_ref[s, n] = product[:, s * width : (s + 1) * width]


def project(offsets, slot, x, gain, w_query, w_key, w_value, group):
    rows, span, model = x.shape
    return pl.pallas_call(
        functools.partial(project_kernel, slot),
        in_specs=[SMEM, VMEM] + [pl.BlockSpec(memory_space=pl.ANY)] * 4,
        out_specs=[VMEM, VMEM, SMEM],
        scratch_shapes=[
            pltpu.VMEM((span, model), BF16),
            pltpu.VMEM((3, model, model), BF16),
            pltpu.SemaphoreType.DMA((4,)),
        ],
        out_shape=[
            jax.ShapeDtypeStruct((span, model), BF16),
            jax.ShapeDtypeStruct((group, 3, span, model // group), BF16),
            jax.ShapeDtypeStruct((rows,), jnp.int32),
        ],
        compiler_params=kernel_params(),
        cost_estimate=cost(0, 1024),
        name="project",
    )(offsets, gain, x, w_query, w_key, w_value)


def doc_start(offs_ref, row, pos):
    start = jnp.zeros_like(pos)
    for d in range(offs_ref.shape[1]):
        first = offs_ref[row, d]
        start = jnp.where(pos >= first, first, start)
    return start


def doc_end(offs_ref, row, pos, length):
    end = jnp.int32(length)
    for d in reversed(range(offs_ref.shape[1])):
        first = offs_ref[row, d]
        end = jnp.where(first > pos, first, end)
    return end


def head_lanes(shape, head, head_dim):
    lane = lax.broadcasted_iota(jnp.int32, shape, 1)
    return (lane >= head * head_dim) & (lane < (head + 1) * head_dim)


def attend_kernel(rows, heads, head_dim, order_ref, offs_ref, scale_ref, *refs):
    count = len(rows)
    result_ref, lse_ref, score_ref = refs[count:]
    for n, row in enumerate(rows):
        attend_row(
            order_ref[row],
            heads,
            head_dim,
            offs_ref,
            scale_ref,
            refs[n],
            result_ref.at[:, n],
            lse_ref.at[n],
            score_ref,
        )


def attend_row(
    row, heads, head_dim, offs_ref, scale_ref, held, result_ref, lse_ref, score_ref
):
    blocks, _, span, width = held.shape
    wide = score_ref.shape[-1]
    per = wide // span
    lanes = min(128, wide)
    score_scale = head_dim ** (-0.5)

    def query_block(i, carry):
        first_pos = i * span
        queries = held[i, 0] * jnp.asarray(score_scale, BF16)
        query_head = [
            jnp.where(head_lanes((span, width), h, head_dim), queries, 0).astype(BF16)
            for h in range(heads)
        ]
        query_pos = first_pos + lax.broadcasted_iota(jnp.int32, (span, 1), 0)
        query_start = doc_start(offs_ref, row, query_pos)
        low = doc_start(offs_ref, row, first_pos) // wide
        high = (first_pos + span - 1) // wide + 1

        def score_step(j, tops):
            keys = held[pl.ds(j * per, per), 1].reshape(wide, width)
            key_pos = j * wide + lax.broadcasted_iota(jnp.int32, (span, wide), 1)
            allowed = (key_pos >= query_start) & (key_pos <= query_pos)
            new = []
            for h in range(heads):
                scores = jnp.where(allowed, dot_last(query_head[h], keys), MASKED)
                score_ref[h, j] = scores
                top = tops[h]
                for c in range(0, wide, lanes):
                    top = jnp.maximum(top, scores[:, c : c + lanes])
                new.append(top)
            return tuple(new)

        tops = lax.fori_loop(
            low, high, score_step, tuple(jnp.full((span, lanes), MASKED, F32) for h in range(heads))
        )
        tops = [jnp.max(top, axis=1, keepdims=True) for top in tops]

        def value_step(j, state):
            values = held[pl.ds(j * per, per), 2].reshape(wide, width)
            new = []
            for h in range(heads):
                total, acc = state[h]
                probs = jnp.exp(score_ref[h, j] - tops[h])
                for c in range(0, wide, lanes):
                    total = total + probs[:, c : c + lanes]
                acc = acc + dot(probs.astype(BF16), values)
                new.append((total, acc))
            return tuple(new)

        state = lax.fori_loop(
            low,
            high,
            value_step,
            tuple(
                (jnp.zeros((span, lanes), F32), jnp.zeros((span, width), F32)) for h in range(heads)
            ),
        )
        result = jnp.zeros((span, width), F32)
        for h in range(heads):
            total = jnp.sum(state[h][0], axis=1, keepdims=True)
            result = jnp.where(head_lanes((span, width), h, head_dim), state[h][1] / total, result)
            log_total = tops[h] + jnp.log(total)
            lse_ref[i, h : h + 1, :] = jnp.transpose(jnp.broadcast_to(log_total, (span, 128)))[
                0:1, :
            ]
        result_ref[i] = (result * scale_ref[...]).astype(BF16)
        return carry

    lax.fori_loop(0, blocks, query_block, 0)


def attend(order, offsets, rows, qkv, scale_lanes, heads, head_dim):
    group, _, span, width = qkv[0].shape
    length = group * span
    wide = max(span, min(512, length))
    return pl.pallas_call(
        functools.partial(attend_kernel, rows, heads, head_dim),
        in_specs=[SMEM, SMEM, VMEM] + [VMEM] * len(rows),
        out_shape=[
            jax.ShapeDtypeStruct((group, len(rows), span, width), BF16),
            jax.ShapeDtypeStruct((len(rows), group, heads, span), F32),
        ],
        scratch_shapes=[pltpu.VMEM((heads, length // wide, span, wide), F32)],
        compiler_params=kernel_params(),
        cost_estimate=cost(0, 1024),
        name="attend",
    )(order, offsets, scale_lanes, *qkv)


def attend_back_kernel(rows, heads, head_dim, order_ref, offs_ref, inv_ref, grad_ref, *refs):
    count = len(rows)
    held, out_refs, lse_refs = refs[:count], refs[count : 2 * count], refs[2 * count : 3 * count]
    dqkv_ref, total_ref = refs[3 * count : 3 * count + 2]
    for n, row in enumerate(rows):
        attend_back_row(
            order_ref[row],
            heads,
            head_dim,
            offs_ref,
            inv_ref,
            lse_refs[n],
            held[n],
            grad_ref.at[:, n],
            out_refs[n],
            dqkv_ref.at[:, n],
            total_ref.at[n],
            *refs[3 * count + 2 :],
        )


def attend_back_row(
    row,
    heads,
    head_dim,
    offs_ref,
    inv_ref,
    lse_ref,
    held,
    grad_ref,
    out_ref,
    dqkv_ref,
    total_ref,
    q_ref,
    k_ref,
    g_ref,
    delta_ref,
    dq_ref,
):
    blocks, _, span, width = held.shape
    score_scale = head_dim ** (-0.5)
    picks = lax.broadcasted_iota(jnp.int32, (8, width), 0)
    lane = lax.broadcasted_iota(jnp.int32, (8, width), 1)
    ones = jnp.where(lane // head_dim == picks, 1.0, 0.0).astype(F32)

    def prepare(i, carry):
        queries = held[i, 0] * jnp.asarray(score_scale, BF16)
        keys = held[i, 1]
        grads = grad_ref[i]
        for h in range(heads):
            mine = head_lanes((span, width), h, head_dim)
            q_ref[h, i] = jnp.where(mine, queries, 0).astype(BF16)
            k_ref[h, i] = jnp.where(mine, keys, 0).astype(BF16)
            g_ref[h, i] = jnp.where(mine, grads, 0).astype(BF16)
        product = grads.astype(F32) * out_ref[i].astype(F32) * inv_ref[...]
        delta_ref[i] = lax.dot_general(
            ones, product, LAST, precision=lax.Precision.HIGHEST, preferred_element_type=F32
        )
        dq_ref[i] = jnp.zeros((span, width), F32)
        return carry + delta_ref[i]

    total_ref[...] = lax.fori_loop(0, blocks, prepare, jnp.zeros((8, span), F32))

    def key_block(j, carry):
        keys = held[j, 1]
        values = held[j, 2]
        key_pos = j * span + lax.broadcasted_iota(jnp.int32, (span, 1), 0)
        last = (doc_end(offs_ref, row, (j + 1) * span - 1, blocks * span) - 1) // span + 1

        def query_step(i, state):
            dk, dv = state
            query_pos = i * span + lax.broadcasted_iota(jnp.int32, (1, span), 1)
            query_start = doc_start(offs_ref, row, query_pos)
            allowed = (key_pos >= query_start) & (key_pos <= query_pos)
            dq = dq_ref[i]
            for h in range(heads):
                scores = dot_last(keys, q_ref[h, i])
                scores = jnp.where(allowed, scores - lse_ref[i, h : h + 1, :], MASKED)
                probs = jnp.exp(scores)
                d_probs = dot_last(values, g_ref[h, i])
                d_scores = (probs * (d_probs - delta_ref[i, h : h + 1, :])).astype(BF16)
                dv = dv + dot(probs.astype(BF16), g_ref[h, i])
                dk = dk + dot(d_scores, q_ref[h, i])
                dq = dq + dot_first(d_scores, k_ref[h, j])
            dq_ref[i] = dq
            return (dk, dv)

        zero = jnp.zeros((span, width), F32)
        dk, dv = lax.fori_loop(j, last, query_step, (zero, zero))
        dqkv_ref[j, 1] = dk.astype(BF16)
        dqkv_ref[j, 2] = dv.astype(BF16)
        dqkv_ref[j, 0] = (dq_ref[j] * score_scale).astype(BF16)
        return carry

    lax.fori_loop(0, blocks, key_block, 0)


def attend_back(
    order, offsets, rows, qkv, grads, at, scaled, inverse_lanes, lse, heads, head_dim
):
    group, _, span, width = qkv[0].shape
    count = len(rows)
    return pl.pallas_call(
        functools.partial(attend_back_kernel, rows, heads, head_dim),
        grid=(1,),
        in_specs=[SMEM, SMEM, VMEM]
        + [pl.BlockSpec((group, count, span, width), lambda i: (0, at, 0, 0))]
        + [VMEM] * (3 * count),
        out_specs=[VMEM] * 2,
        out_shape=[
            jax.ShapeDtypeStruct((group, count, 3, span, width), BF16),
            jax.ShapeDtypeStruct((count, 8, span), F32),
        ],
        scratch_shapes=[pltpu.VMEM((heads, group, span, width), BF16)] * 3
        + [pltpu.VMEM((group, 8, span), F32), pltpu.VMEM((group, span, width), F32)],
        compiler_params=kernel_params(),
        cost_estimate=cost(0, 1024),
        name="attend_back",
    )(order, offsets, inverse_lanes, grads, *qkv, *scaled, *lse)


def join_grads_kernel(parts, in_ref, out_ref, value_ref):
    group = in_ref.shape[0]
    for n in range(3):
        whole = jnp.concatenate([in_ref[s, 0, n] for s in range(group)], axis=1)
        piece = whole.shape[1] // parts
        if n == 2:
            value_ref[...] = whole
            continue
        for p in range(parts):
            to = (p * 2 + n) * piece
            out_ref[:, to : to + piece] = whole[:, p * piece : (p + 1) * piece]


def join_grads(block):
    group, _, _, span, width = block.shape
    return pl.pallas_call(
        functools.partial(join_grads_kernel, PARTS),
        out_shape=[
            jax.ShapeDtypeStruct((span, 2 * group * width), BF16),
            jax.ShapeDtypeStruct((span, group * width), BF16),
        ],
        compiler_params=kernel_params(),
        cost_estimate=cost(0, 1024),
        name="join_grads",
    )(block)


FF_STEP = 1024


def layer_kernel(
    order_ref,
    o_ref,
    x_ref,
    d_out_ref,
    post_ref,
    ffn_ref,
    mid_gain_ref,
    scale_ref,
    w_out_ref,
    d_mid_hbm,
    w_fc1_hbm,
    scaled_ref,
    ffn_in_ref,
    residual_ref,
    mid_ref,
    d_pre_ref,
    d_proj_ref,
    d_residual_ref,
    d_attn_ref,
    g_post_ref,
    g_ffn_ref,
    g_mid_ref,
    d_mid_ref,
    w_fc1_ref,
    act_ref,
    slope_ref,
    sems,
    *,
    slot,
):
    group, _, span, width = o_ref.shape
    hidden = act_ref.shape[1]
    steps = [slice(c, c + FF_STEP) for c in range(0, hidden, FF_STEP)]
    weight_copies = [
        pltpu.make_async_copy(w_fc1_hbm.at[:, at], w_fc1_ref.at[:, at], sems.at[c])
        for c, at in enumerate(steps)
    ]
    mid_copy = pltpu.make_async_copy(
        d_mid_hbm.at[pl.ds(pl.multiple_of(order_ref[slot] * span, span), span), :],
        d_mid_ref,
        sems.at[len(steps)],
    )
    for copy in weight_copies:
        copy.start()
    mid_copy.start()

    scaled = jnp.concatenate([o_ref[s, 0] for s in range(group)], axis=1)
    scaled_ref[...] = scaled
    proj_hat, proj_spread = norm_parts(dot(scaled, w_out_ref[...]))
    residual = x_ref[...].astype(F32) + proj_hat * post_ref[...]
    residual_ref[...] = residual
    res_hat, res_spread = norm_parts(residual)
    ffn_in = (res_hat * ffn_ref[...]).astype(BF16)
    ffn_in_ref[...] = ffn_in

    total = jnp.zeros((span, 1), F32)
    for c, at in enumerate(steps):
        weight_copies[c].wait()
        pre = dot(ffn_in, w_fc1_ref[:, at])
        phi = 0.5 + 0.5 * lax.erf(pre * (0.5**0.5))
        act = pre * phi
        act_ref[:, at] = act
        slope_ref[:, at] = phi + pre * jnp.exp(-0.5 * pre * pre) * 0.3989422804014327
        total += jnp.sum(act, axis=1, keepdims=True)
    average = total / hidden
    total = jnp.zeros((span, 1), F32)
    for at in steps:
        centred = act_ref[:, at] - average
        total += jnp.sum(centred * centred, axis=1, keepdims=True)
    spread = lax.rsqrt(total / hidden + EPSILON)

    mid_copy.wait()
    sum_weighted = jnp.zeros((span, 1), F32)
    sum_hat = jnp.zeros((span, 1), F32)
    for at in steps:
        hat = (act_ref[:, at] - average) * spread
        act_ref[:, at] = hat
        gain = mid_gain_ref[:, at]
        mid_ref[:, at] = (hat * gain).astype(BF16)
        grad = d_mid_ref[:, at]
        product = grad * hat
        g_mid_ref[:, at] = jnp.sum(product, axis=0, keepdims=True)
        sum_weighted += jnp.sum(grad * gain, axis=1, keepdims=True)
        sum_hat += jnp.sum(product * gain, axis=1, keepdims=True)
    sum_weighted = sum_weighted / hidden
    sum_hat = sum_hat / hidden
    d_ffn = jnp.zeros(x_ref.shape, F32)
    for at in steps:
        weighted = d_mid_ref[:, at] * mid_gain_ref[:, at]
        d_act = spread * (weighted - sum_weighted - act_ref[:, at] * sum_hat)
        d_pre = (d_act * slope_ref[:, at]).astype(BF16)
        d_pre_ref[:, at] = d_pre
        d_ffn += dot_last(d_pre, w_fc1_ref[:, at])

    g_ffn_ref[...] = jnp.sum(d_ffn * res_hat, axis=0, keepdims=True)
    d_residual = d_out_ref[...].astype(F32) + norm_back(res_hat, res_spread, ffn_ref[...], d_ffn)
    d_residual_ref[...] = d_residual
    g_post_ref[...] = jnp.sum(d_residual * proj_hat, axis=0, keepdims=True)
    d_proj = norm_back(proj_hat, proj_spread, post_ref[...], d_residual).astype(BF16)
    d_proj_ref[...] = d_proj
    d_attn = (dot_last(d_proj, w_out_ref[...]) * scale_ref[...]).astype(BF16)
    for s in range(group):
        d_attn_ref[s, 0] = d_attn[:, s * width : (s + 1) * width]


def layer(order, slot, o_blocks, at, x, d_out, gains, w_out, d_mid, w_fc1):
    group, _, span, width = o_blocks.shape
    model = x.shape[2]
    hidden = w_fc1.shape[1]
    shape = jax.ShapeDtypeStruct
    return pl.pallas_call(
        functools.partial(layer_kernel, slot=slot),
        grid_spec=pltpu.PrefetchScalarGridSpec(
            num_scalar_prefetch=1,
            grid=(1,),
            in_specs=[pl.BlockSpec((group, 1, span, width), lambda i, o: (0, at, 0, 0))]
            + [pl.BlockSpec((None, span, model), lambda i, o: (o[slot], 0, 0))] * 2
            + [VMEM] * 5
            + [pl.BlockSpec(memory_space=pl.ANY)] * 2,
            out_specs=[VMEM] * 11,
            scratch_shapes=[
                pltpu.VMEM((span, hidden), F32),
                pltpu.VMEM(w_fc1.shape, BF16),
                pltpu.VMEM((span, hidden), F32),
                pltpu.VMEM((span, hidden), F32),
                pltpu.SemaphoreType.DMA((hidden // FF_STEP + 1,)),
            ],
        ),
        out_shape=[
            shape((span, model), BF16),
            shape((span, model), BF16),
            shape((span, model), F32),
            shape((span, hidden), BF16),
            shape((span, hidden), BF16),
            shape((span, model), BF16),
            shape((span, model), F32),
            shape((group, 1, span, width), BF16),
            shape((1, model), F32),
            shape((1, model), F32),
            shape((1, hidden), F32),
        ],
        compiler_params=kernel_params(),
        cost_estimate=cost(0, 1024),
        name="layer",
    )(order, o_blocks, x, d_out, *gains, w_out, d_mid, w_fc1)


def layer_out_kernel(order_ref, *refs):
    count = (len(refs) - 2) // 2
    weight, out_ref = refs[-2], refs[-1]
    for r in range(count):
        out_ref[order_ref[r]] = (refs[r][...] + dot(refs[count + r][...], weight[...])).astype(BF16)


def last_step(order, residuals, mids, w_fc2):
    return pl.pallas_call(
        layer_out_kernel,
        in_specs=[SMEM] + [VMEM] * (2 * len(mids) + 1),
        out_shape=jax.ShapeDtypeStruct((len(mids),) + residuals[0].shape, BF16),
        compiler_params=kernel_params(),
        cost_estimate=cost(0, 1024),
        name="layer_out",
    )(order, *residuals, *mids, w_fc2)


def flip(value, axis, bit):
    size = lax.axis_size(axis)
    return lax.ppermute(value, axis, [(i, i ^ (1 << bit)) for i in range(size)])


def bits(axis):
    return (lax.axis_size(axis) - 1).bit_length()


PARTS = 4


def weight_kernel(count, rows, added, shards, part_ref, *refs):
    out_ref = refs[-1]
    high = out_ref.shape[1]
    per = rows * (shards + 1)
    extras = refs[per * count : per * count + added]
    at = 0
    for n in range(count):
        mine = refs[n * per : (n + 1) * per]
        rights = mine[rows * shards :]
        width = rights[0].shape[1]
        total = 0.0
        for r in range(rows):
            left = [ref[...] for ref in mine[r * shards : (r + 1) * shards]]
            left = jnp.concatenate(left, axis=1) if shards > 1 else left[0]
            total += dot_first(left, rights[r][...])
        for i in range(shards):
            piece = total[i * high : (i + 1) * high]
            for extra in extras:
                piece = piece + extra[i, :, at : at + width].astype(F32)
            out_ref[i, :, at : at + width] = piece.astype(BF16)
        at += width


def weight_part_plain(pairs, part, parts, extras, group):
    pieces = []
    for lefts, rights, kind in pairs:
        left, right = jnp.concatenate(lefts), jnp.concatenate(rights)
        if kind == "columns":
            wide = right.shape[1] // parts
            right = lax.dynamic_slice(right, (0, part * wide), (right.shape[0], wide))
            left = left.reshape(left.shape[0], group, -1)
        else:
            left = left.reshape(left.shape[0], group, parts, -1)
            left = lax.dynamic_index_in_dim(left, part, 2, keepdims=False)
        pieces.append(jnp.einsum("tsd,te->sde", left, right, preferred_element_type=F32))
    total = jnp.concatenate(pieces, axis=2)
    for extra in extras:
        total = total + extra.astype(F32)
    return total.astype(BF16)


def weight_part(pairs, part, parts, extras, group):
    shards = 2
    specs, arrays, width = [], [], 0
    for lefts, rights, kind in pairs:
        span, model = lefts[0].shape
        stride = 1 if kind == "columns" else parts
        high = model // group // stride
        wide = rights[0].shape[1] // (parts if kind == "columns" else 1)
        for left in lefts:
            for i in range(shards):

                def left_at(g, p, i=i, stride=stride):
                    return (0, (g * shards + i) * stride + (p[0] if stride > 1 else 0))

                specs.append(pl.BlockSpec((span, high), left_at))
                arrays.append(left)
        for right in rights:

            def right_at(g, p, stride=stride):
                return (0, p[0] if stride == 1 else 0)

            specs.append(pl.BlockSpec((span, wide), right_at))
            arrays.append(right)
        width += wide
    if high % 128:
        return weight_part_plain(pairs, part, parts, extras, group)
    block = pl.BlockSpec((shards, high, width), lambda g, p: (g, 0, 0))
    return pl.pallas_call(
        functools.partial(weight_kernel, len(pairs), len(pairs[0][0]), len(extras), shards),
        grid_spec=pltpu.PrefetchScalarGridSpec(
            num_scalar_prefetch=1,
            grid=(group // shards,),
            in_specs=specs + [block] * len(extras),
            out_specs=block,
        ),
        out_shape=jax.ShapeDtypeStruct((group, high, width), BF16),
        compiler_params=kernel_params(),
        cost_estimate=cost(0, 1024),
        name="weight_part",
    )(part.astype(jnp.int32).reshape(1), *arrays, *extras)


class WeightSum:
    def __init__(self, *pairs):
        self.pairs = pairs
        batch_at = lax.axis_index("batch")
        self.near, self.far = batch_at & 1, (batch_at >> 1) & 1

    def piece(self, order, near, far, *extras):
        def part_of(part):
            return weight_part(self.pairs, part, PARTS, extras, lax.axis_size("blk"))

        return order(part_of, near * 2 + far)

    def half(self, order, near, *extras):
        def part_of(part):
            return weight_part(self.pairs, part, 2, extras, lax.axis_size("blk"))

        return order(part_of, near)

    def away_far(self, order):
        return self.piece(order, 1 - self.near, 1 - self.far)

    def send_far(self, order, away):
        return self.piece(order, self.near, 1 - self.far, away)

    def away_near(self, order):
        return self.piece(order, 1 - self.near, self.far)

    def keep(self, order, away, arrived):
        return self.piece(order, self.near, self.far, away, arrived)


def over_near(sent):
    return flip(sent, "batch", 0)


def over_far(sent):
    return flip(sent, "batch", 1)


class Order:
    def __init__(self):
        self.last = ()

    def __call__(self, step, *values):
        self.last = step(*tie(values, self.last))
        return self.last


def window(always, step):
    def nothing():
        return jax.tree.map(lambda leaf: jnp.zeros(leaf.shape, leaf.dtype), jax.eval_shape(step))

    return lax.cond(always, step, nothing)


def tie(values, *after):
    return lax.optimization_barrier((values, after))[0]


def combine_kernel(plan, at_ref, *refs):
    ins = sum(count for _, count, _ in plan)
    into, out_of = list(refs[:ins]), list(refs[ins:])
    for n, (kind, count, cut) in enumerate(plan):
        terms = [into.pop(0) for _ in range(count)]
        if kind == "small":
            out_of.pop(0)[...] = sum(term[...] for term in terms)
            continue
        if kind == "stack":
            out = out_of.pop(0)
            out[0], out[1] = terms[0][0], terms[1][0]
            continue

        def put(ref, j, i):
            if kind == "add":
                ref[j] = (terms[0][i].astype(F32) + terms[1][i].astype(F32)).astype(BF16)
                return
            at = 0
            for term in terms:
                ref[j, :, at : at + term.shape[2]] = term[i]
                at += term.shape[2]

        if cut:
            keep, send = out_of.pop(0), out_of.pop(0)
            for j in range(keep.shape[0]):
                put(keep, j, 2 * j + at_ref[n])
                put(send, j, 2 * j + 1 - at_ref[n])
        else:
            whole = out_of.pop(0)
            for j in range(whole.shape[0]):
                put(whole, j, j)


class Tree:
    def __init__(self, *mine, halved=2):
        self.steps = [("blk", bit) for bit in range(bits("blk"))]
        self.steps += [("batch", bit) for bit in range(halved, bits("batch"))]
        self.steps += [("far", 1), ("near", 0)][2 - halved :]
        self.terms, self.last = list(mine), "first"

    def start(self):
        kind, bit = self.steps[0]
        return flip(self.send, "blk" if kind == "blk" else "batch", bit)

    def end(self, arrived):
        self.last = self.steps.pop(0)[0]
        self.terms = [self.kept, arrived]


def combine(trees):
    me = lax.axis_index("blk")
    plan, ins, shapes, at = [], [], [], []
    for tree in trees:
        kind, bit = tree.steps[0]
        cut = kind == "blk" and tree.last != "small"
        if tree.last == "small":
            plan.append(("small", len(tree.terms), False))
            ins += tree.terms
            shapes.append(jax.ShapeDtypeStruct(tree.terms[0].shape, F32))
            at.append(me * 0)
            continue
        state = {"first": "first", "far": "stack"}.get(tree.last, "add")
        plan.append((state, len(tree.terms), cut))
        ins += tree.terms
        count, high, wide = tree.terms[0].shape
        if state == "first":
            wide = sum(term.shape[2] for term in tree.terms)
        count = count // 2 if cut else 2 if state == "stack" else count
        shapes += [jax.ShapeDtypeStruct((count, high, wide), BF16)] * (2 if cut else 1)
        at.append((me >> bit) & 1 if cut else me * 0)
    outs = list(
        pl.pallas_call(
            functools.partial(combine_kernel, plan),
            in_specs=[SMEM] + [VMEM] * len(ins),
            out_shape=shapes,
            compiler_params=kernel_params(),
            cost_estimate=cost(0, 1024),
            name="combine",
        )(jnp.stack(at).astype(jnp.int32), *ins)
    )
    for tree, (_, _, cut) in zip(trees, plan):
        tree.kept = outs.pop(0)
        tree.send = outs.pop(0) if cut else tree.kept


def place_kernel(layout, lines, part_ref, *refs):
    count = 2 * len(layout) + (2 if lines else 0)
    ins, outs = list(refs[:count]), list(refs[count:])
    if lines:
        one, other = ins[-2:]
        for (start, size, cut), out in zip(lines, outs[-len(lines) :]):
            at = pl.ds(start, size)
            if cut:
                at = pl.ds(pl.multiple_of(start + part_ref[2] * size, 128), size)
            out[...] = one[:, at] + other[:, at]
    near, far = part_ref[0], part_ref[1]
    order = [near * 2 + far, near * 2 + 1 - far, (1 - near) * 2 + far, (1 - near) * 2 + 1 - far]
    for spans in layout:
        both = [ins.pop(0), ins.pop(0)]
        count = 2 * both[0].shape[0]
        for start, width, kind in spans:
            out = outs.pop(0)
            for n, part in enumerate(order if count == 4 else [near, 1 - near]):
                value = both[n * 2 // count][n % (count // 2), :, start : start + width]
                value = value.astype(F32)
                if kind == "columns":
                    out[:, pl.ds(pl.multiple_of(part * width, 128), width)] = value
                else:
                    high = value.shape[0]
                    out[pl.ds(pl.multiple_of(part * high, 8), high), :] = value


def place(trees, layout, small=None, lines=()):
    batch_at = lax.axis_index("batch")
    parts = jnp.stack([batch_at & 1, (batch_at >> 1) & 1, lax.axis_index("blk")])
    parts = parts.astype(jnp.int32)
    ins, shapes = [], []
    for tree, spans in zip(trees, layout):
        ins += tree.terms
        count, high = 2 * tree.kept.shape[0], tree.kept.shape[1]
        for _, width, kind in spans:
            shape = (high, count * width) if kind == "columns" else (count * high, width)
            shapes.append(jax.ShapeDtypeStruct(shape, F32))
    if lines:
        ins += small.terms
        shapes += [jax.ShapeDtypeStruct((1, size), F32) for _, size, _ in lines]
    return pl.pallas_call(
        functools.partial(place_kernel, layout, lines),
        in_specs=[SMEM] + [VMEM] * len(ins),
        out_shape=shapes,
        compiler_params=kernel_params(),
        cost_estimate=cost(0, 1024),
        name="place",
    )(parts, *ins)


class SmallSum:
    def __init__(self, mine):
        self.steps = [("batch", bit) for bit in range(bits("batch"))]
        self.steps += [("blk", bit) for bit in range(bits("blk"))]
        self.terms, self.last = [mine], "small"

    def start(self):
        return flip(self.send, *self.steps[0])

    def end(self, arrived):
        self.steps.pop(0)
        self.terms = [self.kept, arrived]


def input_grad_kernel(parts, rows, order_ref, x_ref, gain_ref, wq_ref, wk_ref, wv_ref, *refs):
    out_ref, sum_ref = refs[3 * rows :]
    model = wq_ref.shape[0]
    piece = model // parts
    total = jnp.zeros(sum_ref.shape, F32)
    for r in range(rows):
        d_ref, value_ref, res_ref = refs[r], refs[rows + r], refs[2 * rows + r]
        grad = dot_last(value_ref[...], wv_ref[...])
        for p in range(parts):
            for n, weight in enumerate((wq_ref, wk_ref)):
                at = (p * 2 + n) * piece
                grad += dot_last(d_ref[:, at : at + piece], weight[:, p * piece : (p + 1) * piece])
        row = order_ref[r]
        hat, spread = norm_parts(x_ref[row].astype(F32))
        out_ref[row] = res_ref[...] + norm_back(hat, spread, gain_ref[...], grad)
        total += jnp.sum(grad * hat, axis=0, keepdims=True)
    sum_ref[...] = total


def input_grad(order, x, gain, w_query, w_key, w_value, d_rows, d_values, d_residuals):
    return pl.pallas_call(
        functools.partial(input_grad_kernel, PARTS, len(d_rows)),
        in_specs=[SMEM] + [VMEM] * (5 + 3 * len(d_rows)),
        out_shape=[
            jax.ShapeDtypeStruct(x.shape, F32),
            jax.ShapeDtypeStruct((1, x.shape[2]), F32),
        ],
        compiler_params=kernel_params(),
        cost_estimate=cost(0, 1024),
        name="input_grad",
    )(order, x, gain, w_query, w_key, w_value, *d_rows, *d_values, *d_residuals)


def on_device(
    inputs,
    ln_attn,
    w_query,
    w_key,
    w_value,
    w_out,
    head_scale,
    ln_post,
    ln_ffn,
    w_fc1,
    ln_mid,
    w_fc2,
    offsets,
    cotangent,
):
    row_count, span, model = inputs.shape
    head_count = head_scale.shape[0]
    head_dim = model // head_count
    tokens = row_count * span
    group = lax.axis_size("blk")
    heads = head_count // group
    width = heads * head_dim
    my_index = lax.axis_index("blk")
    rows = range(row_count)

    always = offsets[0, 0] == 0
    gain = ln_attn.reshape(1, model)
    last = row_count - 1
    my_scale = lax.dynamic_slice(head_scale, (my_index * heads,), (heads,))
    scale_lanes = jnp.repeat(my_scale, head_dim).reshape(1, width)
    layer_gains = [
        ln_post.reshape(1, model),
        ln_ffn.reshape(1, model),
        ln_mid.reshape(1, -1),
        jnp.repeat(head_scale, head_dim).reshape(1, model),
    ]

    def project_row(r, x):
        return project(offsets, r, x, gain, w_query, w_key, w_value, group)

    def attend_one(r, held):
        return attend(by_work, offsets, [r], [held], scale_lanes, heads, head_dim)

    def layer_row(r, o_blocks):
        at = r if r < last else 0
        return layer(by_work, r, o_blocks, at, inputs, cotangent, layer_gains, w_out, d_mid, w_fc1)

    def back(order, r, row_heads, at=0):
        def back_row(held):
            return attend_back(
                by_work,
                offsets,
                [r],
                [held],
                row_heads,
                at,
                [scaled_mine[r].reshape(group, span, width)],
                1.0 / scale_lanes,
                [lse[r].reshape(lse[r].shape[1:])],
                heads,
                head_dim,
            )

        return order(back_row, qkv[r])

    def first_window():
        order = Order()
        return exchange(sent), [
            order(functools.partial(project_row, r), inputs) for r in rows[1:]
        ]

    normed_first, sent, by_work = project_row(0, inputs)
    held, projected = first_window()
    qkv = [held]
    normed = [normed_first] + [part[0] for part in projected]
    scaled_mine, lse = [], []
    for r in rows[1:]:

        def next_window():
            order = Order()
            extra = ()
            if r == 1:
                extra = jnp.einsum(
                    "td,fd->tf",
                    cotangent.reshape(tokens, model),
                    w_fc2,
                    preferred_element_type=F32,
                )
            return exchange(projected[r - 1][1]), attend_one(r - 1, qkv[r - 1]), extra

        held, (out, log_total), extra = window(always, next_window)
        d_mid = extra if r == 1 else d_mid
        qkv.append(held)
        scaled_mine.append(out)
        lse.append(log_total)

    def early_window():
        return (
            exchange(jnp.concatenate(scaled_mine, axis=1)),
            attend_one(last, qkv[last]),
        )

    early, (out, log_total) = window(always, early_window)
    scaled_mine.append(out)
    lse.append(log_total)

    def late_window():
        return exchange(scaled_mine[last]), layer_row(0, early)

    late, layer_first = window(always, late_window)

    def layer_window():
        order = Order()
        first = exchange(layer_first[7])
        rest = []
        for r in rows[1:]:

            def one(o_blocks):
                return layer_row(r, o_blocks)

            rest.append(order(one, early if r < last else late))
        return first, rest

    first_heads, rest = window(always, layer_window)
    (
        scaled,
        ffn_in,
        residual,
        mid,
        d_pre,
        d_proj,
        d_residual,
        d_attn,
        g_post,
        g_ffn,
        g_mid,
    ) = zip(layer_first, *rest)
    d_out = [lax.dynamic_index_in_dim(cotangent, by_work[r], keepdims=False) for r in rows]
    sum_one = WeightSum((mid, d_out, "rows"))
    sum_two = WeightSum((ffn_in, d_pre, "columns"))
    sum_three = WeightSum((scaled, d_proj, "columns"))
    order = Order()
    away = over_near(sum_one.away_far(order))
    away_two = sum_two.away_far(order)
    sent_one = sum_one.send_far(order, away)

    def back_first():
        order = Order()
        arrived = over_far(sent_one)
        heads_in = exchange(jnp.concatenate(d_attn[1:], axis=1))
        away = over_near(away_two)
        out = back(order, 0, first_heads)
        return arrived, heads_in, out, sum_two.send_far(order, away)

    far_one, rest_heads, (sent, total), sent_two = window(always, back_first)
    totals = [total]

    def back_second():
        order = Order()
        arrived = over_far(sent_two)
        grad = exchange(sent)
        away = over_near(sum_one.away_near(order))
        out = back(order, 1, rest_heads, 0)
        near = sum_two.away_near(order), sum_three.half(order, 1 - sum_three.near)
        return grad, out, arrived, near, sum_one.keep(order, away, far_one)

    grad, (sent, total), far_two, near, mine_one = window(always, back_second)
    near_two, away_three = near
    totals.append(total)
    grads = [grad]
    tree_one = Tree(mine_one)
    combine([tree_one])
    for r in rows[2:]:

        def back_next():
            order = Order()
            moved, over, out_of = (), (), ()
            if r == 2:
                moved = tree_one.start()
                over = over_near(near_two), over_near(away_three)
            grad = exchange(sent)
            out = back(order, r, rest_heads, r - 1)
            if r == 2:
                mine = sum_two.keep(order, over[0], far_two)
                out_of = mine, sum_three.half(order, sum_three.near, over[1])
            return grad, moved, out_of, out

        grad, moved, out_of, (sent, total) = window(always, back_next)
        totals.append(total)
        grads.append(grad)
        if r == 2:
            tree_one.end(moved)
            mine_two, mine_three = out_of
    tree_two = Tree(mine_two)
    combine([tree_one, tree_two])

    def back_last():
        order = Order()
        moved = tree_one.start(), tree_two.start()
        grad = exchange(sent)
        joined = [order(join_grads, part) for part in grads]

        def output_step(weight):
            return last_step(by_work, residual, mid, weight)

        return grad, moved, joined, order(output_step, w_fc2)

    grad, moved, joined, layer_out = window(always, back_last)
    tree_one.end(moved[0])
    tree_two.end(moved[1])
    order = Order()
    joined = joined + [order(join_grads, grad)]
    d_rows, d_values = zip(*joined)
    sum_qk = WeightSum((normed, d_rows, "columns"))
    sum_v = WeightSum((normed, d_values, "columns"))
    away_qk = over_near(sum_qk.away_far(order))
    away_v = over_near(sum_v.half(order, 1 - sum_v.near))
    sent_qk = sum_qk.send_far(order, away_qk)
    tree_v = Tree(sum_v.half(order, sum_v.near, away_v), mine_three, halved=1)
    combine([tree_one, tree_two, tree_v])

    def advance(trees, extra=lambda: ()):
        def step():
            return [tree.start() for tree in trees], extra()

        moved, out = window(always, step)
        for tree, arrived in zip(trees, moved):
            tree.end(arrived)
        return out

    def beside():
        order = Order()
        arrived = over_far(sent_qk)
        near = over_near(sum_qk.away_near(order))

        def input_step(x):
            return input_grad(
                by_work, x, gain, w_query, w_key, w_value, d_rows, d_values, d_residual
            )

        return arrived, near, order(input_step, inputs)

    far_qk, near_qk, (grad_inputs, grad_ln_attn) = advance(
        [tree_one, tree_two, tree_v], beside
    )
    tree_qk = Tree(sum_qk.keep(order, near_qk, far_qk))
    delta_sum = sum(jnp.sum(total, axis=(0, 2)) for total in totals)
    my_grad = delta_sum[:heads] / my_scale
    scale_part = lax.dynamic_update_slice(
        jnp.zeros((head_count,), F32), my_grad, (my_index * heads,)
    )
    small = SmallSum(
        jnp.concatenate(
            [grad_ln_attn[0], sum(g_post)[0], sum(g_ffn)[0], sum(g_mid)[0], scale_part]
        ).reshape(1, -1)
    )
    piece = model // PARTS
    ff_piece = w_fc1.shape[1] // PARTS
    trees = [tree_qk, tree_v, tree_two, tree_one]
    placed = None
    while any(tree.steps for tree in trees + [small]):
        combine([tree for tree in trees + [small] if tree.steps])

        def place_early():
            if tree_two.steps or tree_one.steps or placed is not None:
                return ()
            return place(
                [tree_one, tree_two], [[(0, model, "rows")], [(0, ff_piece, "columns")]]
            )

        early_out = advance([tree for tree in trees + [small] if tree.steps], place_early)
        placed = early_out or placed
    if placed is None:
        placed = place([tree_one, tree_two], [[(0, model, "rows")], [(0, ff_piece, "columns")]])
    grad_fc2, grad_fc1 = placed
    lines = [(0, model), (model, model), (2 * model, model), (3 * model, ln_mid.shape[0])]
    ends = lines[-1][0] + lines[-1][1]
    layout = [
        [(n * piece, piece, "columns") for n in range(2)],
        [(n * 2 * piece, 2 * piece, "columns") for n in range(2)],
    ]
    if model // group % 128:
        grad_query, grad_key, grad_value, grad_out = place([tree_qk, tree_v], layout)
        total = sum(small.terms)[0]
        gains = [
            lax.dynamic_slice(total, (start + my_index * (size // group),), (size // group,))
            for start, size in lines
        ]
        gains.append(total[ends:])
    else:
        lines = [(start, size // group, True) for start, size in lines]
        lines.append((ends, head_count, False))
        grad_query, grad_key, grad_value, grad_out, *gains = place(
            [tree_qk, tree_v], layout, small, lines
        )
        gains = [line[0] for line in gains]
    return (
        layer_out,
        grad_inputs,
        gains[0],
        grad_query,
        grad_key,
        grad_value,
        grad_out,
        gains[4],
        gains[1],
        gains[2],
        grad_fc1,
        gains[3],
        grad_fc2,
    )


def solution(mesh):
    rows = P("batch", "blk", None)
    shard = P("blk", None)
    return jax.shard_map(
        on_device,
        mesh=mesh,
        in_specs=(rows,) + (P(),) * 11 + (P("batch", None), rows),
        out_specs=(
            rows,
            rows,
            P("blk"),
            shard,
            shard,
            shard,
            shard,
            P(),
            P("blk"),
            P("blk"),
            shard,
            P("blk"),
            shard,
        ),
        check_vma=False,
    )
```

```python
import functools

import jax
import jax.numpy as jnp
from jax import lax
from jax.experimental import pallas as pl
from jax.experimental.pallas import tpu as pltpu
from jax.sharding import PartitionSpec as P

EPSILON = 1e-05
MASKED = -1e30
VMEM_BYTES = 50 * 1024 * 1024
F32 = jnp.float32
BF16 = jnp.bfloat16
LAST = (((1,), (1,)), ((), ()))
FIRST = (((0,), (0,)), ((), ()))
SMEM = pl.BlockSpec(memory_space=pltpu.SMEM)
VMEM = pl.BlockSpec(memory_space=pltpu.VMEM)


def dot_last(left, right):
    return lax.dot_general(left, right, LAST, preferred_element_type=F32)


def dot_first(left, right):
    return lax.dot_general(left, right, FIRST, preferred_element_type=F32)


def dot(left, right):
    return jnp.dot(left, right, preferred_element_type=F32)


def kernel_params():
    return pltpu.CompilerParams(vmem_limit_bytes=VMEM_BYTES)


def cost(flops, size):
    return pl.CostEstimate(flops=int(flops), bytes_accessed=int(size), transcendentals=0)


def exchange(parts):
    return lax.all_to_all(parts, "blk", 0, 0, tiled=True)


def norm_parts(rows_in):
    average = jnp.mean(rows_in, axis=-1, keepdims=True)
    centred = rows_in - average
    spread = lax.rsqrt(jnp.mean(centred * centred, axis=-1, keepdims=True) + EPSILON)
    return centred * spread, spread


def norm_back(hat, spread, gain, grad):
    weighted = grad * gain
    return spread * (
        weighted
        - jnp.mean(weighted, axis=-1, keepdims=True)
        - hat * jnp.mean(weighted * hat, axis=-1, keepdims=True)
    )


def rows_by_work(offs_ref, length):
    rows, docs = offs_ref.shape
    work = []
    for r in range(rows):
        total = jnp.int32(0)
        for d in range(docs):
            end = offs_ref[r, d + 1] if d + 1 < docs else length
            total += (end - offs_ref[r, d]) * (end - offs_ref[r, d])
        work.append(total)
    ranks = []
    for r in range(rows):
        rank = jnp.int32(0)
        for other in range(rows):
            if other < r:
                rank += (work[other] >= work[r]).astype(jnp.int32)
            elif other > r:
                rank += (work[other] > work[r]).astype(jnp.int32)
        ranks.append(rank)
    return [
        sum(jnp.where(ranks[r] == slot, jnp.int32(r), jnp.int32(0)) for r in range(rows))
        for slot in range(rows)
    ]


def project_kernel(
    slot,
    offs_ref,
    gain_ref,
    x_hbm,
    wq_hbm,
    wk_hbm,
    wv_hbm,
    normed_ref,
    out_ref,
    order_ref,
    x_ref,
    weight_ref,
    sems,
):
    group, _, span, width = out_ref.shape
    order = rows_by_work(offs_ref, group * span)
    copy_x = pltpu.make_async_copy(x_hbm.at[order[slot]], x_ref, sems.at[3])
    copy_x.start()
    copies = [
        pltpu.make_async_copy(weight, weight_ref.at[n], sems.at[n])
        for n, weight in enumerate((wq_hbm, wk_hbm, wv_hbm))
    ]
    for copy in copies:
        copy.start()
    for r, row in enumerate(order):
        order_ref[r] = row
    copy_x.wait()
    hat, _ = norm_parts(x_ref[...].astype(F32))
    normed = (hat * gain_ref[...]).astype(BF16)
    normed_ref[...] = normed
    for n in range(3):
        copies[n].wait()
        product = dot(normed, weight_ref[n]).astype(BF16)
        for s in range(group):
            out_ref[s, n] = product[:, s * width : (s + 1) * width]


def project(offsets, slot, x, gain, w_query, w_key, w_value, group):
    rows, span, model = x.shape
    return pl.pallas_call(
        functools.partial(project_kernel, slot),
        in_specs=[SMEM, VMEM] + [pl.BlockSpec(memory_space=pl.ANY)] * 4,
        out_specs=[VMEM, VMEM, SMEM],
        scratch_shapes=[
            pltpu.VMEM((span, model), BF16),
            pltpu.VMEM((3, model, model), BF16),
            pltpu.SemaphoreType.DMA((4,)),
        ],
        out_shape=[
            jax.ShapeDtypeStruct((span, model), BF16),
            jax.ShapeDtypeStruct((group, 3, span, model // group), BF16),
            jax.ShapeDtypeStruct((rows,), jnp.int32),
        ],
        compiler_params=kernel_params(),
        cost_estimate=cost(0, 1024),
        name="project",
    )(offsets, gain, x, w_query, w_key, w_value)


def doc_start(offs_ref, row, pos):
    start = jnp.zeros_like(pos)
    for d in range(offs_ref.shape[1]):
        first = offs_ref[row, d]
        start = jnp.where(pos >= first, first, start)
    return start


def doc_end(offs_ref, row, pos, length):
    end = jnp.int32(length)
    for d in reversed(range(offs_ref.shape[1])):
        first = offs_ref[row, d]
        end = jnp.where(first > pos, first, end)
    return end


def head_lanes(shape, head, head_dim):
    lane = lax.broadcasted_iota(jnp.int32, shape, 1)
    return (lane >= head * head_dim) & (lane < (head + 1) * head_dim)


def attend_kernel(slot, heads, head_dim, order_ref, offs_ref, scale_ref, held, *refs):
    result_ref, lse_ref, score_ref = refs[-3:]
    attend_row(
        order_ref[slot], heads, head_dim, offs_ref, scale_ref, held, result_ref, lse_ref, score_ref
    )


def attend_row(
    row, heads, head_dim, offs_ref, scale_ref, held, result_ref, lse_ref, score_ref
):
    blocks, _, span, width = held.shape
    wide = score_ref.shape[-1]
    per = wide // span
    lanes = min(128, wide)
    score_scale = head_dim ** (-0.5)

    def query_block(i, carry):
        first_pos = i * span
        queries = held[i, 0] * jnp.asarray(score_scale, BF16)
        query_head = [
            jnp.where(head_lanes((span, width), h, head_dim), queries, 0).astype(BF16)
            for h in range(heads)
        ]
        query_pos = first_pos + lax.broadcasted_iota(jnp.int32, (span, 1), 0)
        query_start = doc_start(offs_ref, row, query_pos)
        low = doc_start(offs_ref, row, first_pos) // wide
        high = (first_pos + span - 1) // wide + 1

        def score_step(j, tops):
            keys = held[pl.ds(j * per, per), 1].reshape(wide, width)
            key_pos = j * wide + lax.broadcasted_iota(jnp.int32, (span, wide), 1)
            allowed = (key_pos >= query_start) & (key_pos <= query_pos)
            new = []
            for h in range(heads):
                scores = jnp.where(allowed, dot_last(query_head[h], keys), MASKED)
                score_ref[h, j] = scores
                top = tops[h]
                for c in range(0, wide, lanes):
                    top = jnp.maximum(top, scores[:, c : c + lanes])
                new.append(top)
            return tuple(new)

        tops = lax.fori_loop(
            low, high, score_step, tuple(jnp.full((span, lanes), MASKED, F32) for h in range(heads))
        )
        tops = [jnp.max(top, axis=1, keepdims=True) for top in tops]

        def value_step(j, state):
            values = held[pl.ds(j * per, per), 2].reshape(wide, width)
            new = []
            for h in range(heads):
                total, acc = state[h]
                probs = jnp.exp(score_ref[h, j] - tops[h])
                for c in range(0, wide, lanes):
                    total = total + probs[:, c : c + lanes]
                acc = acc + dot(probs.astype(BF16), values)
                new.append((total, acc))
            return tuple(new)

        state = lax.fori_loop(
            low,
            high,
            value_step,
            tuple(
                (jnp.zeros((span, lanes), F32), jnp.zeros((span, width), F32)) for h in range(heads)
            ),
        )
        result = jnp.zeros((span, width), F32)
        for h in range(heads):
            total = jnp.sum(state[h][0], axis=1, keepdims=True)
            result = jnp.where(head_lanes((span, width), h, head_dim), state[h][1] / total, result)
            log_total = tops[h] + jnp.log(total)
            lse_ref[i, h : h + 1, :] = jnp.transpose(jnp.broadcast_to(log_total, (span, 128)))[
                0:1, :
            ]
        result_ref[i] = (result * scale_ref[...]).astype(BF16)
        return carry

    lax.fori_loop(0, blocks, query_block, 0)


def attend(order, offsets, slot, qkv, scale_lanes, heads, head_dim, at=0, count=1, into=None):
    group, _, span, width = qkv.shape
    length = group * span
    wide = max(span, min(512, length))
    held = [] if into is None else [into]
    return pl.pallas_call(
        functools.partial(attend_kernel, slot, heads, head_dim),
        grid=(1,),
        in_specs=[SMEM, SMEM, VMEM, VMEM] + [pl.BlockSpec(memory_space=pl.ANY)] * len(held),
        out_specs=[pl.BlockSpec((group, None, span, width), lambda i: (0, at, 0, 0)), VMEM],
        out_shape=[
            jax.ShapeDtypeStruct((group, count, span, width), BF16),
            jax.ShapeDtypeStruct((group, heads, span), F32),
        ],
        scratch_shapes=[pltpu.VMEM((heads, length // wide, span, wide), F32)],
        input_output_aliases={4: 0} if held else {},
        compiler_params=kernel_params(),
        cost_estimate=cost(0, 1024),
        name="attend",
    )(order, offsets, scale_lanes, qkv, *held)


def attend_back_kernel(slot, heads, head_dim, order_ref, offs_ref, *refs):
    attend_back_row(order_ref[slot], heads, head_dim, offs_ref, *refs)


def attend_back_row(
    row,
    heads,
    head_dim,
    offs_ref,
    inv_ref,
    lse_ref,
    held,
    grad_ref,
    out_ref,
    dqkv_ref,
    total_ref,
    q_ref,
    k_ref,
    g_ref,
    delta_ref,
    dq_ref,
):
    blocks, _, span, width = held.shape
    score_scale = head_dim ** (-0.5)
    picks = lax.broadcasted_iota(jnp.int32, (8, width), 0)
    lane = lax.broadcasted_iota(jnp.int32, (8, width), 1)
    ones = jnp.where(lane // head_dim == picks, 1.0, 0.0).astype(F32)

    def prepare(i, carry):
        queries = held[i, 0] * jnp.asarray(score_scale, BF16)
        keys = held[i, 1]
        grads = grad_ref[i]
        for h in range(heads):
            mine = head_lanes((span, width), h, head_dim)
            q_ref[h, i] = jnp.where(mine, queries, 0).astype(BF16)
            k_ref[h, i] = jnp.where(mine, keys, 0).astype(BF16)
            g_ref[h, i] = jnp.where(mine, grads, 0).astype(BF16)
        product = grads.astype(F32) * out_ref[i].astype(F32) * inv_ref[...]
        delta_ref[i] = lax.dot_general(
            ones, product, LAST, precision=lax.Precision.HIGHEST, preferred_element_type=F32
        )
        dq_ref[i] = jnp.zeros((span, width), F32)
        return carry + delta_ref[i]

    total_ref[...] = lax.fori_loop(0, blocks, prepare, jnp.zeros((8, span), F32))

    def key_block(j, carry):
        keys = held[j, 1]
        values = held[j, 2]
        key_pos = j * span + lax.broadcasted_iota(jnp.int32, (span, 1), 0)
        last = (doc_end(offs_ref, row, (j + 1) * span - 1, blocks * span) - 1) // span + 1

        def query_step(i, state):
            dk, dv = state
            query_pos = i * span + lax.broadcasted_iota(jnp.int32, (1, span), 1)
            query_start = doc_start(offs_ref, row, query_pos)
            allowed = (key_pos >= query_start) & (key_pos <= query_pos)
            dq = dq_ref[i]
            for h in range(heads):
                scores = dot_last(keys, q_ref[h, i])
                scores = jnp.where(allowed, scores - lse_ref[i, h : h + 1, :], MASKED)
                probs = jnp.exp(scores)
                d_probs = dot_last(values, g_ref[h, i])
                d_scores = (probs * (d_probs - delta_ref[i, h : h + 1, :])).astype(BF16)
                dv = dv + dot(probs.astype(BF16), g_ref[h, i])
                dk = dk + dot(d_scores, q_ref[h, i])
                dq = dq + dot_first(d_scores, k_ref[h, j])
            dq_ref[i] = dq
            return (dk, dv)

        zero = jnp.zeros((span, width), F32)
        dk, dv = lax.fori_loop(j, last, query_step, (zero, zero))
        dqkv_ref[j, 1] = dk.astype(BF16)
        dqkv_ref[j, 2] = dv.astype(BF16)
        dqkv_ref[j, 0] = (dq_ref[j] * score_scale).astype(BF16)
        return carry

    lax.fori_loop(0, blocks, key_block, 0)


def attend_back(
    order, offsets, slot, qkv, grads, grads_at, scaled, scaled_at, inverse_lanes, lse, heads, head_dim
):
    group, _, span, width = qkv.shape

    def block_spec(at):
        return pl.BlockSpec((group, None, span, width), lambda i: (0, at, 0, 0))

    return pl.pallas_call(
        functools.partial(attend_back_kernel, slot, heads, head_dim),
        grid=(1,),
        in_specs=[SMEM, SMEM, VMEM, VMEM, VMEM, block_spec(grads_at), block_spec(scaled_at)],
        out_specs=[pl.BlockSpec((group, None, 3, span, width), lambda i: (0, 0, 0, 0, 0)), VMEM],
        out_shape=[
            jax.ShapeDtypeStruct((group, 1, 3, span, width), BF16),
            jax.ShapeDtypeStruct((8, span), F32),
        ],
        scratch_shapes=[pltpu.VMEM((heads, group, span, width), BF16)] * 3
        + [pltpu.VMEM((group, 8, span), F32), pltpu.VMEM((group, span, width), F32)],
        compiler_params=kernel_params(),
        cost_estimate=cost(0, 1024),
        name="attend_back",
    )(order, offsets, inverse_lanes, lse, qkv, grads, scaled)


def join_grads_kernel(parts, in_ref, out_ref, value_ref):
    group = in_ref.shape[0]
    for n in range(3):
        whole = jnp.concatenate([in_ref[s, 0, n] for s in range(group)], axis=1)
        piece = whole.shape[1] // parts
        if n == 2:
            value_ref[...] = whole
            continue
        for p in range(parts):
            to = (p * 2 + n) * piece
            out_ref[:, to : to + piece] = whole[:, p * piece : (p + 1) * piece]


def join_grads(block):
    group, _, _, span, width = block.shape
    return pl.pallas_call(
        functools.partial(join_grads_kernel, PARTS),
        out_shape=[
            jax.ShapeDtypeStruct((span, 2 * group * width), BF16),
            jax.ShapeDtypeStruct((span, group * width), BF16),
        ],
        compiler_params=kernel_params(),
        cost_estimate=cost(0, 1024),
        name="join_grads",
    )(block)


FF_STEP = 1024
LAYER_VMEM = 62 * 1024 * 1024


def layer_kernel(
    slots,
    order_ref,
    post_ref,
    ffn_ref,
    mid_gain_ref,
    scale_ref,
    w_out_ref,
    x_hbm,
    d_out_hbm,
    d_mid_hbm,
    w_fc1_hbm,
    *refs,
):
    count = len(slots)
    o_refs = refs[:count]
    (
        scaled_ref,
        ffn_in_ref,
        residual_ref,
        mid_ref,
        d_pre_ref,
        d_proj_ref,
        d_residual_ref,
        d_attn_ref,
        g_post_ref,
        g_ffn_ref,
        g_mid_ref,
        x_ref,
        d_out_ref,
        d_mid_ref,
        w_fc1_ref,
        act_ref,
        slope_ref,
        sems,
        row_sems,
    ) = refs[count:]
    group, _, span, width = o_refs[0].shape
    tokens, hidden = act_ref.shape
    step = FF_STEP // count
    steps = [slice(c, c + step) for c in range(0, hidden, step)]
    weight_copies = [
        pltpu.make_async_copy(
            w_fc1_hbm.at[:, c : c + FF_STEP], w_fc1_ref.at[:, c : c + FF_STEP], sems.at[n]
        )
        for n, c in enumerate(range(0, hidden, FF_STEP))
    ]
    x_copies, mid_copies = [], []
    for n, slot in enumerate(slots):
        row = order_ref[slot]
        to = slice(n * span, (n + 1) * span)
        x_copies.append(pltpu.make_async_copy(x_hbm.at[row], x_ref.at[to], row_sems.at[0, n]))
        x_copies.append(
            pltpu.make_async_copy(d_out_hbm.at[row], d_out_ref.at[to], row_sems.at[1, n])
        )
        rows = pl.ds(pl.multiple_of(row * span, span), span)
        mid_copies.append(
            pltpu.make_async_copy(d_mid_hbm.at[rows], d_mid_ref.at[to], row_sems.at[2, n])
        )
    for copy in x_copies + weight_copies + mid_copies:
        copy.start()

    for n in range(count):
        for s in range(group):
            scaled_ref[n * span : (n + 1) * span, s * width : (s + 1) * width] = o_refs[n][s, 0]
    proj_hat, proj_spread = norm_parts(dot(scaled_ref[...], w_out_ref[...]))
    for copy in x_copies:
        copy.wait()
    residual = x_ref[...].astype(F32) + proj_hat * post_ref[...]
    residual_ref[...] = residual
    res_hat, res_spread = norm_parts(residual)
    ffn_in = (res_hat * ffn_ref[...]).astype(BF16)
    ffn_in_ref[...] = ffn_in

    total = jnp.zeros((tokens, 1), F32)
    for n, at in enumerate(steps):
        if n % count == 0:
            weight_copies[n // count].wait()
        pre = dot(ffn_in, w_fc1_ref[:, at])
        phi = 0.5 + 0.5 * lax.erf(pre * (0.5**0.5))
        act = pre * phi
        act_ref[:, at] = act
        slope = phi + pre * jnp.exp(-0.5 * pre * pre) * 0.3989422804014327
        slope_ref[:, at] = slope.astype(slope_ref.dtype)
        total += jnp.sum(act, axis=1, keepdims=True)
    average = total / hidden
    total = jnp.zeros((tokens, 1), F32)
    for at in steps:
        centred = act_ref[:, at] - average
        total += jnp.sum(centred * centred, axis=1, keepdims=True)
    spread = lax.rsqrt(total / hidden + EPSILON)

    for copy in mid_copies:
        copy.wait()
    sum_weighted = jnp.zeros((tokens, 1), F32)
    sum_hat = jnp.zeros((tokens, 1), F32)
    for at in steps:
        hat = (act_ref[:, at] - average) * spread
        act_ref[:, at] = hat
        gain = mid_gain_ref[:, at]
        mid_ref[:, at] = (hat * gain).astype(BF16)
        grad = d_mid_ref[:, at]
        product = grad * hat
        g_mid_ref[:, at] = jnp.sum(product, axis=0, keepdims=True)
        sum_weighted += jnp.sum(grad * gain, axis=1, keepdims=True)
        sum_hat += jnp.sum(product * gain, axis=1, keepdims=True)
    sum_weighted = sum_weighted / hidden
    sum_hat = sum_hat / hidden
    d_ffn = jnp.zeros(x_ref.shape, F32)
    for at in steps:
        weighted = d_mid_ref[:, at] * mid_gain_ref[:, at]
        d_act = spread * (weighted - sum_weighted - act_ref[:, at] * sum_hat)
        d_pre = (d_act * slope_ref[:, at].astype(F32)).astype(BF16)
        d_pre_ref[:, at] = d_pre
        d_ffn += dot_last(d_pre, w_fc1_ref[:, at])

    g_ffn_ref[...] = jnp.sum(d_ffn * res_hat, axis=0, keepdims=True)
    d_residual = d_out_ref[...].astype(F32) + norm_back(res_hat, res_spread, ffn_ref[...], d_ffn)
    d_residual_ref[...] = d_residual
    g_post_ref[...] = jnp.sum(d_residual * proj_hat, axis=0, keepdims=True)
    d_proj = norm_back(proj_hat, proj_spread, post_ref[...], d_residual).astype(BF16)
    d_proj_ref[...] = d_proj
    d_attn = (dot_last(d_proj, w_out_ref[...]) * scale_ref[...]).astype(BF16)
    for n in range(count):
        for s in range(group):
            d_attn_ref[s, n] = d_attn[n * span : (n + 1) * span, s * width : (s + 1) * width]


def layer(order, slots, blocks, x, d_out, gains, w_out, d_mid, w_fc1):
    group, _, span, width = blocks[0][0].shape
    model, hidden = w_fc1.shape
    tokens = len(slots) * span
    shape = jax.ShapeDtypeStruct

    def block_spec(at):
        return pl.BlockSpec((group, 1, span, width), lambda i, o: (0, at, 0, 0))

    return pl.pallas_call(
        functools.partial(layer_kernel, slots),
        grid_spec=pltpu.PrefetchScalarGridSpec(
            num_scalar_prefetch=1,
            grid=(1,),
            in_specs=[VMEM] * 5
            + [pl.BlockSpec(memory_space=pl.ANY)] * 4
            + [block_spec(at) for _, at in blocks],
            out_specs=[VMEM] * 11,
            scratch_shapes=[
                pltpu.VMEM((tokens, model), BF16),
                pltpu.VMEM((tokens, model), BF16),
                pltpu.VMEM((tokens, hidden), d_mid.dtype),
                pltpu.VMEM(w_fc1.shape, BF16),
                pltpu.VMEM((tokens, hidden), F32),
                pltpu.VMEM((tokens, hidden), F32 if len(slots) == 1 else BF16),
                pltpu.SemaphoreType.DMA((hidden // FF_STEP,)),
                pltpu.SemaphoreType.DMA((3, len(slots))),
            ],
        ),
        out_shape=[
            shape((tokens, model), BF16),
            shape((tokens, model), BF16),
            shape((tokens, model), F32),
            shape((tokens, hidden), BF16),
            shape((tokens, hidden), BF16),
            shape((tokens, model), BF16),
            shape((tokens, model), F32),
            shape((group, len(slots), span, width), BF16),
            shape((1, model), F32),
            shape((1, model), F32),
            shape((1, hidden), F32),
        ],
        compiler_params=pltpu.CompilerParams(vmem_limit_bytes=LAYER_VMEM),
        cost_estimate=cost(0, 1024),
        name="layer",
    )(order, *gains, w_out, x, d_out, d_mid, w_fc1, *[block for block, _ in blocks])


def layer_out_kernel(order_ref, *refs):
    count = (len(refs) - 2) // 2
    weight, out_ref = refs[-2], refs[-1]
    span, slot = out_ref.shape[1], 0
    for n in range(count):
        result = (refs[n][...] + dot(refs[count + n][...], weight[...])).astype(BF16)
        for at in range(0, result.shape[0], span):
            out_ref[order_ref[slot]] = result[at : at + span]
            slot += 1


def last_step(order, shape, residuals, mids, w_fc2):
    return pl.pallas_call(
        layer_out_kernel,
        in_specs=[SMEM] + [VMEM] * (2 * len(mids) + 1),
        out_shape=jax.ShapeDtypeStruct(shape, BF16),
        compiler_params=kernel_params(),
        cost_estimate=cost(0, 1024),
        name="layer_out",
    )(order, *residuals, *mids, w_fc2)


def flip(value, axis, bit):
    size = lax.axis_size(axis)
    return lax.ppermute(value, axis, [(i, i ^ (1 << bit)) for i in range(size)])


def bits(axis):
    return (lax.axis_size(axis) - 1).bit_length()


PARTS = 4


def weight_kernel(count, rows, added, shards, part_ref, *refs):
    out_ref = refs[-1]
    high = out_ref.shape[1]
    per = rows * (shards + 1)
    extras = refs[per * count : per * count + added]
    at = 0
    for n in range(count):
        mine = refs[n * per : (n + 1) * per]
        rights = mine[rows * shards :]
        width = rights[0].shape[1]
        total = 0.0
        for r in range(rows):
            left = [ref[...] for ref in mine[r * shards : (r + 1) * shards]]
            left = jnp.concatenate(left, axis=1) if shards > 1 else left[0]
            total += dot_first(left, rights[r][...])
        for i in range(shards):
            piece = total[i * high : (i + 1) * high]
            for extra in extras:
                piece = piece + extra[i, :, at : at + width].astype(F32)
            out_ref[i, :, at : at + width] = piece.astype(BF16)
        at += width


def weight_part_plain(pairs, part, parts, extras, group):
    pieces = []
    for lefts, rights, kind in pairs:
        left, right = jnp.concatenate(lefts), jnp.concatenate(rights)
        if kind == "columns":
            wide = right.shape[1] // parts
            right = lax.dynamic_slice(right, (0, part * wide), (right.shape[0], wide))
            left = left.reshape(left.shape[0], group, -1)
        else:
            left = left.reshape(left.shape[0], group, parts, -1)
            left = lax.dynamic_index_in_dim(left, part, 2, keepdims=False)
        pieces.append(jnp.einsum("tsd,te->sde", left, right, preferred_element_type=F32))
    total = jnp.concatenate(pieces, axis=2)
    axis = 2 if pairs[0][2] == "columns" else 1
    for extra, at in extras:
        size = total.shape[axis]
        total = total + lax.dynamic_slice_in_dim(extra, at * size, size, axis).astype(F32)
    return total.astype(BF16)


def weight_part(pairs, part, parts, extras, group):
    shards = 2
    specs, arrays, width = [], [], 0
    for lefts, rights, kind in pairs:
        model = lefts[0].shape[1]
        stride = 1 if kind == "columns" else parts
        high = model // group // stride
        wide = rights[0].shape[1] // (parts if kind == "columns" else 1)
        for left in lefts:
            for i in range(shards):

                def left_at(g, p, i=i, stride=stride):
                    return (0, (g * shards + i) * stride + (p[0] if stride > 1 else 0))

                specs.append(pl.BlockSpec((left.shape[0], high), left_at))
                arrays.append(left)
        for right in rights:

            def right_at(g, p, stride=stride):
                return (0, p[0] if stride == 1 else 0)

            specs.append(pl.BlockSpec((right.shape[0], wide), right_at))
            arrays.append(right)
        width += wide
    if high % 128:
        return weight_part_plain(pairs, part, parts, extras, group)
    block = pl.BlockSpec((shards, high, width), lambda g, p: (g, 0, 0))
    by_row = pairs[0][2] == "rows"

    def extra_spec(n):
        def block_at(g, p):
            return (g, p[n], 0) if by_row else (g, 0, p[n])

        return pl.BlockSpec((shards, high, width), block_at)

    numbers = jnp.stack([part] + [at for _, at in extras]).astype(jnp.int32)
    return pl.pallas_call(
        functools.partial(weight_kernel, len(pairs), len(pairs[0][0]), len(extras), shards),
        grid_spec=pltpu.PrefetchScalarGridSpec(
            num_scalar_prefetch=1,
            grid=(group // shards,),
            in_specs=specs + [extra_spec(n + 1) for n in range(len(extras))],
            out_specs=block,
        ),
        out_shape=jax.ShapeDtypeStruct((group, high, width), BF16),
        compiler_params=kernel_params(),
        cost_estimate=cost(0, 1024),
        name="weight_part",
    )(numbers, *arrays, *[extra for extra, _ in extras])


class WeightSum:
    def __init__(self, *pairs):
        self.pairs = pairs
        batch_at = lax.axis_index("batch")
        self.near, self.far = batch_at & 1, (batch_at >> 1) & 1
        self.zero = batch_at * 0

    def piece(self, order, near, far, *extras):
        def part_of(part):
            return weight_part(self.pairs, part, PARTS, extras, lax.axis_size("blk"))

        return order(part_of, near * 2 + far)

    def half(self, order, near, *extras):
        def part_of(part):
            return weight_part(self.pairs, part, 2, extras, lax.axis_size("blk"))

        return order(part_of, near)

    def away_far(self, order):
        return self.piece(order, 1 - self.near, 1 - self.far)

    def away_near(self, order):
        return self.piece(order, 1 - self.near, self.far)

    def away(self, order):
        return self.half(order, 1 - self.near)

    def send_far(self, order, away):
        return self.piece(order, self.near, 1 - self.far, (away, self.zero))

    def send(self, order, away):
        return self.piece(order, self.near, 1 - self.far, (away, 1 - self.far))

    def keep(self, order, near, arrived):
        return self.piece(order, self.near, self.far, (near, self.zero), (arrived, self.zero))

    def keep_rest(self, order, away, arrived):
        return self.piece(order, self.near, self.far, (away, self.far), (arrived, self.zero))

    def own(self, order, away):
        return self.half(order, self.near, (away, self.zero))


def over_near(sent):
    return flip(sent, "batch", 0)


def over_far(sent):
    return flip(sent, "batch", 1)


class Order:
    def __init__(self):
        self.last = ()

    def __call__(self, step, *values):
        self.last = step(*tie(values, self.last))
        return self.last


def window(always, step):
    def nothing():
        return jax.tree.map(lambda leaf: jnp.zeros(leaf.shape, leaf.dtype), jax.eval_shape(step))

    return lax.cond(always, step, nothing)


def tie(values, *after):
    return lax.optimization_barrier((values, after))[0]


def combine_kernel(plan, at_ref, *refs):
    ins = sum(count for _, count, _ in plan)
    into, out_of = list(refs[:ins]), list(refs[ins:])
    for n, (kind, count, cut) in enumerate(plan):
        terms = [into.pop(0) for _ in range(count)]
        if kind == "small":
            out_of.pop(0)[...] = sum(term[...] for term in terms)
            continue
        if kind == "stack":
            out = out_of.pop(0)
            out[0], out[1] = terms[0][0], terms[1][0]
            continue

        def put(ref, j, i):
            if kind == "add":
                ref[j] = (terms[0][i].astype(F32) + terms[1][i].astype(F32)).astype(BF16)
                return
            at = 0
            for term in terms:
                ref[j, :, at : at + term.shape[2]] = term[i]
                at += term.shape[2]

        if cut:
            keep, send = out_of.pop(0), out_of.pop(0)
            for j in range(keep.shape[0]):
                put(keep, j, 2 * j + at_ref[n])
                put(send, j, 2 * j + 1 - at_ref[n])
        else:
            whole = out_of.pop(0)
            for j in range(whole.shape[0]):
                put(whole, j, j)


class Tree:
    def __init__(self, *mine, halved=2):
        self.steps = [("blk", bit) for bit in range(bits("blk"))]
        self.steps += [("batch", bit) for bit in range(halved, bits("batch"))]
        self.steps += [("far", 1), ("near", 0)][2 - halved :]
        self.terms, self.last = list(mine), "first"

    def start(self):
        kind, bit = self.steps[0]
        return flip(self.send, "blk" if kind == "blk" else "batch", bit)

    def end(self, arrived):
        self.last = self.steps.pop(0)[0]
        self.terms = [self.kept, arrived]


def combine(trees):
    me = lax.axis_index("blk")
    plan, ins, shapes, at = [], [], [], []
    for tree in trees:
        kind, bit = tree.steps[0]
        cut = kind == "blk" and tree.last != "small"
        if tree.last == "small":
            plan.append(("small", len(tree.terms), False))
            ins += tree.terms
            shapes.append(jax.ShapeDtypeStruct(tree.terms[0].shape, F32))
            at.append(me * 0)
            continue
        state = {"first": "first", "far": "stack"}.get(tree.last, "add")
        plan.append((state, len(tree.terms), cut))
        ins += tree.terms
        count, high, wide = tree.terms[0].shape
        if state == "first":
            wide = sum(term.shape[2] for term in tree.terms)
        count = count // 2 if cut else 2 if state == "stack" else count
        shapes += [jax.ShapeDtypeStruct((count, high, wide), BF16)] * (2 if cut else 1)
        at.append((me >> bit) & 1 if cut else me * 0)
    outs = list(
        pl.pallas_call(
            functools.partial(combine_kernel, plan),
            in_specs=[SMEM] + [VMEM] * len(ins),
            out_shape=shapes,
            compiler_params=kernel_params(),
            cost_estimate=cost(0, 1024),
            name="combine",
        )(jnp.stack(at).astype(jnp.int32), *ins)
    )
    for tree, (_, _, cut) in zip(trees, plan):
        tree.kept = outs.pop(0)
        tree.send = outs.pop(0) if cut else tree.kept


def place_kernel(layout, lines, part_ref, *refs):
    count = 2 * len(layout) + (2 if lines else 0)
    ins, outs = list(refs[:count]), list(refs[count:])
    if lines:
        one, other = ins[-2:]
        for (start, size, cut), out in zip(lines, outs[-len(lines) :]):
            at = pl.ds(start, size)
            if cut:
                at = pl.ds(pl.multiple_of(start + part_ref[2] * size, 128), size)
            out[...] = one[:, at] + other[:, at]
    near, far = part_ref[0], part_ref[1]
    order = [near * 2 + far, near * 2 + 1 - far, (1 - near) * 2 + far, (1 - near) * 2 + 1 - far]
    for spans in layout:
        both = [ins.pop(0), ins.pop(0)]
        count = 2 * both[0].shape[0]
        for start, width, kind in spans:
            out = outs.pop(0)
            for n, part in enumerate(order if count == 4 else [near, 1 - near]):
                value = both[n * 2 // count][n % (count // 2), :, start : start + width]
                value = value.astype(F32)
                if kind == "columns":
                    out[:, pl.ds(pl.multiple_of(part * width, 128), width)] = value
                else:
                    high = value.shape[0]
                    out[pl.ds(pl.multiple_of(part * high, 8), high), :] = value


def place(trees, layout, small=None, lines=()):
    batch_at = lax.axis_index("batch")
    parts = jnp.stack([batch_at & 1, (batch_at >> 1) & 1, lax.axis_index("blk")])
    parts = parts.astype(jnp.int32)
    ins, shapes = [], []
    for tree, spans in zip(trees, layout):
        ins += tree.terms
        count, high = 2 * tree.kept.shape[0], tree.kept.shape[1]
        for _, width, kind in spans:
            shape = (high, count * width) if kind == "columns" else (count * high, width)
            shapes.append(jax.ShapeDtypeStruct(shape, F32))
    if lines:
        ins += small.terms
        shapes += [jax.ShapeDtypeStruct((1, size), F32) for _, size, _ in lines]
    return pl.pallas_call(
        functools.partial(place_kernel, layout, lines),
        in_specs=[SMEM] + [VMEM] * len(ins),
        out_shape=shapes,
        compiler_params=kernel_params(),
        cost_estimate=cost(0, 1024),
        name="place",
    )(parts, *ins)


class SmallSum:
    def __init__(self, mine):
        self.steps = [("batch", bit) for bit in range(bits("batch"))]
        self.steps += [("blk", bit) for bit in range(bits("blk"))]
        self.terms, self.last = [mine], "small"

    def start(self):
        return flip(self.send, *self.steps[0])

    def end(self, arrived):
        self.steps.pop(0)
        self.terms = [self.kept, arrived]


def input_grad_kernel(parts, order_ref, x_ref, gain_ref, wq_ref, wk_ref, wv_ref, *refs):
    out_ref, sum_ref = refs[-2:]
    rows, span, model = x_ref.shape
    piece = model // parts
    total = jnp.zeros(sum_ref.shape, F32)
    residuals = [
        held.at[pl.ds(at, span)] for held in refs[2 * rows : -2] for at in range(0, held.shape[0], span)
    ]
    for r in range(rows):
        d_ref, value_ref, res_ref = refs[r], refs[rows + r], residuals[r]
        grad = dot_last(value_ref[...], wv_ref[...])
        for p in range(parts):
            for n, weight in enumerate((wq_ref, wk_ref)):
                at = (p * 2 + n) * piece
                grad += dot_last(d_ref[:, at : at + piece], weight[:, p * piece : (p + 1) * piece])
        row = order_ref[r]
        hat, spread = norm_parts(x_ref[row].astype(F32))
        out_ref[row] = res_ref[...] + norm_back(hat, spread, gain_ref[...], grad)
        total += jnp.sum(grad * hat, axis=0, keepdims=True)
    sum_ref[...] = total


def input_grad(order, x, gain, w_query, w_key, w_value, d_rows, d_values, d_residuals):
    return pl.pallas_call(
        functools.partial(input_grad_kernel, PARTS),
        in_specs=[SMEM] + [VMEM] * (5 + 2 * len(d_rows) + len(d_residuals)),
        out_shape=[
            jax.ShapeDtypeStruct(x.shape, F32),
            jax.ShapeDtypeStruct((1, x.shape[2]), F32),
        ],
        compiler_params=kernel_params(),
        cost_estimate=cost(0, 1024),
        name="input_grad",
    )(order, x, gain, w_query, w_key, w_value, *d_rows, *d_values, *d_residuals)


def on_device(
    inputs,
    ln_attn,
    w_query,
    w_key,
    w_value,
    w_out,
    head_scale,
    ln_post,
    ln_ffn,
    w_fc1,
    ln_mid,
    w_fc2,
    offsets,
    cotangent,
):
    row_count, span, model = inputs.shape
    head_count = head_scale.shape[0]
    head_dim = model // head_count
    tokens = row_count * span
    group = lax.axis_size("blk")
    heads = head_count // group
    width = heads * head_dim
    my_index = lax.axis_index("blk")
    rows = range(row_count)

    always = offsets[0, 0] == 0
    gain = ln_attn.reshape(1, model)
    last = row_count - 1
    my_scale = lax.dynamic_slice(head_scale, (my_index * heads,), (heads,))
    scale_lanes = jnp.repeat(my_scale, head_dim).reshape(1, width)
    layer_gains = [
        ln_post.reshape(1, model),
        ln_ffn.reshape(1, model),
        ln_mid.reshape(1, -1),
        jnp.repeat(head_scale, head_dim).reshape(1, model),
    ]

    def project_row(r, x):
        return project(offsets, r, x, gain, w_query, w_key, w_value, group)

    def attend_one(r, held, into=None):
        place = (r, last) if r < last else (0, 1)
        return attend(by_work, offsets, r, held, scale_lanes, heads, head_dim, *place, into)

    def layer_rows(slots, blocks):
        return layer(by_work, slots, blocks, inputs, cotangent, layer_gains, w_out, d_mid, w_fc1)

    def back(order, r, row_heads, at=0):
        def back_row(held):
            return attend_back(
                by_work,
                offsets,
                r,
                held,
                row_heads,
                at,
                *((first_out, r) if r < last else (last_out, 0)),
                1.0 / scale_lanes,
                lse[r],
                heads,
                head_dim,
            )

        return order(back_row, qkv[r])

    def first_window():
        order = Order()
        return exchange(sent), [
            order(functools.partial(project_row, r), inputs) for r in rows[1:]
        ]

    normed_first, sent, by_work = project_row(0, inputs)
    held, projected = first_window()
    qkv = [held]
    normed = [normed_first] + [part[0] for part in projected]
    first_out, lse = None, []
    for r in rows[1:]:

        def next_window():
            order = Order()
            extra = ()
            if r == 1:
                d_mid = jnp.einsum(
                    "td,fd->tf",
                    cotangent.reshape(tokens, model),
                    w_fc2,
                    preferred_element_type=F32,
                )
                extra = d_mid
            if r == last:
                d_out = [
                    lax.dynamic_index_in_dim(cotangent, by_work[n], keepdims=False) for n in rows
                ]
                extra = d_out[0], jnp.concatenate(d_out[1:])
            return exchange(projected[r - 1][1]), attend_one(r - 1, qkv[r - 1], first_out), extra

        held, (first_out, log_total), extra = window(always, next_window)
        d_mid = extra if r == 1 else d_mid
        qkv.append(held)
        lse.append(log_total)

    d_out = list(extra)

    def early_window():
        return (
            exchange(first_out),
            attend_one(last, qkv[last]),
        )

    early, (last_out, log_total) = window(always, early_window)
    lse.append(log_total)

    def late_window():
        return exchange(last_out), layer_rows([0], [(early, 0)])

    late, layer_first = window(always, late_window)

    def layer_window():
        blocks = [(early, r) if r < last else (late, 0) for r in rows[1:]]
        return exchange(layer_first[7]), layer_rows(list(rows[1:]), blocks)

    first_heads, layer_rest = window(always, layer_window)
    (
        scaled,
        ffn_in,
        residual,
        mid,
        d_pre,
        d_proj,
        d_residual,
        d_attn,
        g_post,
        g_ffn,
        g_mid,
    ) = zip(layer_first, layer_rest)
    sum_one = WeightSum((mid, d_out, "rows"))
    sum_two = WeightSum((ffn_in, d_pre, "columns"))
    sum_three = WeightSum((scaled, d_proj, "columns"))
    order = Order()
    away_one = over_near(sum_one.away(order))
    away_two = sum_two.away_far(order)
    sent_one = sum_one.send(order, away_one)

    def back_first():
        order = Order()
        arrived = over_far(sent_one)
        heads_in = exchange(d_attn[1])
        away = over_near(away_two)
        out = back(order, 0, first_heads)
        return arrived, heads_in, out, sum_two.send_far(order, away)

    far_one, rest_heads, (sent, total), sent_two = window(always, back_first)
    totals = [total]

    def back_second():
        order = Order()
        arrived = over_far(sent_two)
        grad = exchange(sent)
        out = back(order, 1, rest_heads, 0)
        near = sum_two.away_near(order), sum_three.away(order)
        return grad, out, arrived, near, sum_one.keep_rest(order, away_one, far_one)

    grad, (sent, total), far_two, near, mine_one = window(always, back_second)
    near_two, away_three = near
    totals.append(total)
    grads = [grad]
    tree_one = Tree(mine_one)
    combine([tree_one])
    for r in rows[2:]:

        def back_next():
            order = Order()
            moved, over, out_of = (), (), ()
            if r == 2:
                moved = tree_one.start()
                over = over_near(near_two), over_near(away_three)
            grad = exchange(sent)
            out = back(order, r, rest_heads, r - 1)
            if r == 2:
                mine = sum_two.keep(order, over[0], far_two)
                out_of = mine, sum_three.own(order, over[1])
            return grad, moved, out_of, out

        grad, moved, out_of, (sent, total) = window(always, back_next)
        totals.append(total)
        grads.append(grad)
        if r == 2:
            tree_one.end(moved)
            mine_two, mine_three = out_of
    tree_two = Tree(mine_two)
    combine([tree_one, tree_two])

    def back_last():
        order = Order()
        moved = tree_one.start(), tree_two.start()
        grad = exchange(sent)
        joined = [order(join_grads, part) for part in grads]

        def output_step(weight):
            return last_step(by_work, inputs.shape, residual, mid, weight)

        return grad, moved, joined, order(output_step, w_fc2)

    grad, moved, joined, layer_out = window(always, back_last)
    tree_one.end(moved[0])
    tree_two.end(moved[1])
    order = Order()
    joined = joined + [order(join_grads, grad)]
    d_rows, d_values = zip(*joined)
    sum_qk = WeightSum((normed, d_rows, "columns"))
    sum_v = WeightSum((normed, d_values, "columns"))
    away_qk = over_near(sum_qk.away(order))
    away_v = over_near(sum_v.away(order))
    sent_qk = sum_qk.send(order, away_qk)
    tree_v = Tree(sum_v.own(order, away_v), mine_three, halved=1)
    combine([tree_one, tree_two, tree_v])

    def advance(trees, extra=lambda: ()):
        def step():
            return [tree.start() for tree in trees], extra()

        moved, out = window(always, step)
        for tree, arrived in zip(trees, moved):
            tree.end(arrived)
        return out

    def beside():
        order = Order()
        arrived = over_far(sent_qk)

        def input_step(x):
            return input_grad(
                by_work, x, gain, w_query, w_key, w_value, d_rows, d_values, d_residual
            )

        return arrived, order(input_step, inputs)

    far_qk, (grad_inputs, grad_ln_attn) = advance(
        [tree_one, tree_two, tree_v], beside
    )
    tree_qk = Tree(sum_qk.keep_rest(order, away_qk, far_qk))
    delta_sum = sum(jnp.sum(total, axis=1) for total in totals)
    my_grad = delta_sum[:heads] / my_scale
    scale_part = lax.dynamic_update_slice(
        jnp.zeros((head_count,), F32), my_grad, (my_index * heads,)
    )
    small = SmallSum(
        jnp.concatenate(
            [grad_ln_attn[0], sum(g_post)[0], sum(g_ffn)[0], sum(g_mid)[0], scale_part]
        ).reshape(1, -1)
    )
    piece = model // PARTS
    ff_piece = w_fc1.shape[1] // PARTS
    trees = [tree_qk, tree_v, tree_two, tree_one]
    placed = None
    while any(tree.steps for tree in trees + [small]):
        combine([tree for tree in trees + [small] if tree.steps])

        def place_early():
            if tree_two.steps or tree_one.steps or placed is not None:
                return ()
            return place(
                [tree_one, tree_two], [[(0, model, "rows")], [(0, ff_piece, "columns")]]
            )

        early_out = advance([tree for tree in trees + [small] if tree.steps], place_early)
        placed = early_out or placed
    if placed is None:
        placed = place([tree_one, tree_two], [[(0, model, "rows")], [(0, ff_piece, "columns")]])
    grad_fc2, grad_fc1 = placed
    lines = [(0, model), (model, model), (2 * model, model), (3 * model, ln_mid.shape[0])]
    ends = lines[-1][0] + lines[-1][1]
    layout = [
        [(n * piece, piece, "columns") for n in range(2)],
        [(n * 2 * piece, 2 * piece, "columns") for n in range(2)],
    ]
    if model // group % 128:
        grad_query, grad_key, grad_value, grad_out = place([tree_qk, tree_v], layout)
        total = sum(small.terms)[0]
        gains = [
            lax.dynamic_slice(total, (start + my_index * (size // group),), (size // group,))
            for start, size in lines
        ]
        gains.append(total[ends:])
    else:
        lines = [(start, size // group, True) for start, size in lines]
        lines.append((ends, head_count, False))
        grad_query, grad_key, grad_value, grad_out, *gains = place(
            [tree_qk, tree_v], layout, small, lines
        )
        gains = [line[0] for line in gains]
    return (
        layer_out,
        grad_inputs,
        gains[0],
        grad_query,
        grad_key,
        grad_value,
        grad_out,
        gains[4],
        gains[1],
        gains[2],
        grad_fc1,
        gains[3],
        grad_fc2,
    )


def solution(mesh):
    rows = P("batch", "blk", None)
    shard = P("blk", None)
    return jax.shard_map(
        on_device,
        mesh=mesh,
        in_specs=(rows,) + (P(),) * 11 + (P("batch", None), rows),
        out_specs=(
            rows,
            rows,
            P("blk"),
            shard,
            shard,
            shard,
            shard,
            P(),
            P("blk"),
            P("blk"),
            shard,
            P("blk"),
            shard,
        ),
        check_vma=False,
    )
```

```python
import functools

import jax
import jax.numpy as jnp
from jax import lax
from jax.experimental import pallas as pl
from jax.experimental.pallas import tpu as pltpu
from jax.sharding import PartitionSpec as P

EPSILON = 1e-05
MASKED = -1e30
VMEM_BYTES = 50 * 1024 * 1024
F32 = jnp.float32
BF16 = jnp.bfloat16
LAST = (((1,), (1,)), ((), ()))
FIRST = (((0,), (0,)), ((), ()))
SMEM = pl.BlockSpec(memory_space=pltpu.SMEM)
VMEM = pl.BlockSpec(memory_space=pltpu.VMEM)


def dot_last(left, right):
    return lax.dot_general(left, right, LAST, preferred_element_type=F32)


def dot_first(left, right):
    return lax.dot_general(left, right, FIRST, preferred_element_type=F32)


def dot(left, right):
    return jnp.dot(left, right, preferred_element_type=F32)


def kernel_params():
    return pltpu.CompilerParams(vmem_limit_bytes=VMEM_BYTES)


def cost(flops, size):
    return pl.CostEstimate(flops=int(flops), bytes_accessed=int(size), transcendentals=0)


def exchange(parts):
    return lax.all_to_all(parts, "blk", 0, 0, tiled=True)


def norm_parts(rows_in):
    average = jnp.mean(rows_in, axis=-1, keepdims=True)
    centred = rows_in - average
    spread = lax.rsqrt(jnp.mean(centred * centred, axis=-1, keepdims=True) + EPSILON)
    return centred * spread, spread


def norm_back(hat, spread, gain, grad):
    weighted = grad * gain
    return spread * (
        weighted
        - jnp.mean(weighted, axis=-1, keepdims=True)
        - hat * jnp.mean(weighted * hat, axis=-1, keepdims=True)
    )


def rows_by_work(offs_ref, length):
    rows, docs = offs_ref.shape
    work = []
    for r in range(rows):
        total = jnp.int32(0)
        for d in range(docs):
            end = offs_ref[r, d + 1] if d + 1 < docs else length
            total += (end - offs_ref[r, d]) * (end - offs_ref[r, d])
        work.append(total)
    ranks = []
    for r in range(rows):
        rank = jnp.int32(0)
        for other in range(rows):
            if other < r:
                rank += (work[other] >= work[r]).astype(jnp.int32)
            elif other > r:
                rank += (work[other] > work[r]).astype(jnp.int32)
        ranks.append(rank)
    return [
        sum(jnp.where(ranks[r] == slot, jnp.int32(r), jnp.int32(0)) for r in range(rows))
        for slot in range(rows)
    ]


def project_kernel(
    slot,
    offs_ref,
    gain_ref,
    x_hbm,
    wq_hbm,
    wk_hbm,
    wv_hbm,
    normed_ref,
    out_ref,
    order_ref,
    x_ref,
    weight_ref,
    sems,
):
    group, _, span, width = out_ref.shape
    order = rows_by_work(offs_ref, group * span)
    copy_x = pltpu.make_async_copy(x_hbm.at[order[slot]], x_ref, sems.at[3])
    copy_x.start()
    copies = [
        pltpu.make_async_copy(weight, weight_ref.at[n], sems.at[n])
        for n, weight in enumerate((wq_hbm, wk_hbm, wv_hbm))
    ]
    for copy in copies:
        copy.start()
    for r, row in enumerate(order):
        order_ref[r] = row
    copy_x.wait()
    hat, _ = norm_parts(x_ref[...].astype(F32))
    normed = (hat * gain_ref[...]).astype(BF16)
    normed_ref[...] = normed
    for n in range(3):
        copies[n].wait()
        product = dot(normed, weight_ref[n]).astype(BF16)
        for s in range(group):
            out_ref[s, n] = product[:, s * width : (s + 1) * width]


def project(offsets, slot, x, gain, w_query, w_key, w_value, group):
    rows, span, model = x.shape
    return pl.pallas_call(
        functools.partial(project_kernel, slot),
        in_specs=[SMEM, VMEM] + [pl.BlockSpec(memory_space=pl.ANY)] * 4,
        out_specs=[VMEM, VMEM, SMEM],
        scratch_shapes=[
            pltpu.VMEM((span, model), BF16),
            pltpu.VMEM((3, model, model), BF16),
            pltpu.SemaphoreType.DMA((4,)),
        ],
        out_shape=[
            jax.ShapeDtypeStruct((span, model), BF16),
            jax.ShapeDtypeStruct((group, 3, span, model // group), BF16),
            jax.ShapeDtypeStruct((rows,), jnp.int32),
        ],
        compiler_params=kernel_params(),
        cost_estimate=cost(0, 1024),
        name="project",
    )(offsets, gain, x, w_query, w_key, w_value)


def doc_start(offs_ref, row, pos):
    start = jnp.zeros_like(pos)
    for d in range(offs_ref.shape[1]):
        first = offs_ref[row, d]
        start = jnp.where(pos >= first, first, start)
    return start


def doc_end(offs_ref, row, pos, length):
    end = jnp.int32(length)
    for d in reversed(range(offs_ref.shape[1])):
        first = offs_ref[row, d]
        end = jnp.where(first > pos, first, end)
    return end


def head_lanes(shape, head, head_dim):
    lane = lax.broadcasted_iota(jnp.int32, shape, 1)
    return (lane >= head * head_dim) & (lane < (head + 1) * head_dim)


def attend_kernel(slot, heads, head_dim, order_ref, offs_ref, scale_ref, held, *refs):
    result_ref, lse_ref, score_ref = refs[-3:]
    attend_row(
        order_ref[slot], heads, head_dim, offs_ref, scale_ref, held, result_ref, lse_ref, score_ref
    )


def attend_row(
    row, heads, head_dim, offs_ref, scale_ref, held, result_ref, lse_ref, score_ref
):
    blocks, _, span, width = held.shape
    wide = score_ref.shape[-1]
    per = wide // span
    lanes = min(128, wide)
    score_scale = head_dim ** (-0.5)

    def query_block(i, carry):
        first_pos = i * span
        queries = held[i, 0] * jnp.asarray(score_scale, BF16)
        query_head = [
            jnp.where(head_lanes((span, width), h, head_dim), queries, 0).astype(BF16)
            for h in range(heads)
        ]
        query_pos = first_pos + lax.broadcasted_iota(jnp.int32, (span, 1), 0)
        query_start = doc_start(offs_ref, row, query_pos)
        low = doc_start(offs_ref, row, first_pos) // wide
        high = (first_pos + span - 1) // wide + 1

        def score_step(j, tops):
            keys = held[pl.ds(j * per, per), 1].reshape(wide, width)
            key_pos = j * wide + lax.broadcasted_iota(jnp.int32, (span, wide), 1)
            allowed = (key_pos >= query_start) & (key_pos <= query_pos)
            new = []
            for h in range(heads):
                scores = jnp.where(allowed, dot_last(query_head[h], keys), MASKED)
                score_ref[h, j] = scores
                top = tops[h]
                for c in range(0, wide, lanes):
                    top = jnp.maximum(top, scores[:, c : c + lanes])
                new.append(top)
            return tuple(new)

        tops = lax.fori_loop(
            low, high, score_step, tuple(jnp.full((span, lanes), MASKED, F32) for h in range(heads))
        )
        tops = [jnp.max(top, axis=1, keepdims=True) for top in tops]

        def value_step(j, state):
            values = held[pl.ds(j * per, per), 2].reshape(wide, width)
            new = []
            for h in range(heads):
                total, acc = state[h]
                probs = jnp.exp(score_ref[h, j] - tops[h])
                for c in range(0, wide, lanes):
                    total = total + probs[:, c : c + lanes]
                acc = acc + dot(probs.astype(BF16), values)
                new.append((total, acc))
            return tuple(new)

        state = lax.fori_loop(
            low,
            high,
            value_step,
            tuple(
                (jnp.zeros((span, lanes), F32), jnp.zeros((span, width), F32)) for h in range(heads)
            ),
        )
        result = jnp.zeros((span, width), F32)
        for h in range(heads):
            total = jnp.sum(state[h][0], axis=1, keepdims=True)
            result = jnp.where(head_lanes((span, width), h, head_dim), state[h][1] / total, result)
            log_total = tops[h] + jnp.log(total)
            lse_ref[i, h : h + 1, :] = jnp.transpose(jnp.broadcast_to(log_total, (span, 128)))[
                0:1, :
            ]
        result_ref[i] = (result * scale_ref[...]).astype(BF16)
        return carry

    lax.fori_loop(0, blocks, query_block, 0)


def attend(order, offsets, slot, qkv, scale_lanes, heads, head_dim, at=0, count=1, into=None):
    group, _, span, width = qkv.shape
    length = group * span
    wide = max(span, min(512, length))
    held = [] if into is None else [into]
    return pl.pallas_call(
        functools.partial(attend_kernel, slot, heads, head_dim),
        grid=(1,),
        in_specs=[SMEM, SMEM, VMEM, VMEM] + [pl.BlockSpec(memory_space=pl.ANY)] * len(held),
        out_specs=[pl.BlockSpec((group, None, span, width), lambda i: (0, at, 0, 0)), VMEM],
        out_shape=[
            jax.ShapeDtypeStruct((group, count, span, width), BF16),
            jax.ShapeDtypeStruct((group, heads, span), F32),
        ],
        scratch_shapes=[pltpu.VMEM((heads, length // wide, span, wide), F32)],
        input_output_aliases={4: 0} if held else {},
        compiler_params=kernel_params(),
        cost_estimate=cost(0, 1024),
        name="attend",
    )(order, offsets, scale_lanes, qkv, *held)


def attend_back_kernel(slot, heads, head_dim, order_ref, offs_ref, *refs):
    attend_back_row(order_ref[slot], heads, head_dim, offs_ref, *refs)


def attend_back_row(
    row,
    heads,
    head_dim,
    offs_ref,
    inv_ref,
    lse_ref,
    held,
    grad_ref,
    out_ref,
    dqkv_ref,
    total_ref,
    q_ref,
    k_ref,
    g_ref,
    delta_ref,
    dq_ref,
):
    blocks, _, span, width = held.shape
    score_scale = head_dim ** (-0.5)
    picks = lax.broadcasted_iota(jnp.int32, (8, width), 0)
    lane = lax.broadcasted_iota(jnp.int32, (8, width), 1)
    ones = jnp.where(lane // head_dim == picks, 1.0, 0.0).astype(F32)

    def prepare(i, carry):
        queries = held[i, 0] * jnp.asarray(score_scale, BF16)
        keys = held[i, 1]
        grads = grad_ref[i]
        for h in range(heads):
            mine = head_lanes((span, width), h, head_dim)
            q_ref[h, i] = jnp.where(mine, queries, 0).astype(BF16)
            k_ref[h, i] = jnp.where(mine, keys, 0).astype(BF16)
            g_ref[h, i] = jnp.where(mine, grads, 0).astype(BF16)
        product = grads.astype(F32) * out_ref[i].astype(F32) * inv_ref[...]
        delta_ref[i] = lax.dot_general(
            ones, product, LAST, precision=lax.Precision.HIGHEST, preferred_element_type=F32
        )
        dq_ref[i] = jnp.zeros((span, width), F32)
        return carry + delta_ref[i]

    per = 2 if span * 2 <= 512 and blocks % 2 == 0 else 1
    wide = per * span
    total_ref[...] = lax.fori_loop(0, blocks, prepare, jnp.zeros((8, span), F32))

    def key_block(j, carry):
        keys = held[j, 1]
        values = held[j, 2]
        key_pos = j * span + lax.broadcasted_iota(jnp.int32, (span, 1), 0)
        last = (doc_end(offs_ref, row, (j + 1) * span - 1, blocks * span) - 1) // wide + 1

        def query_step(i, state):
            dk, dv = state
            query_pos = i * wide + lax.broadcasted_iota(jnp.int32, (1, wide), 1)
            query_start = doc_start(offs_ref, row, query_pos)
            allowed = (key_pos >= query_start) & (key_pos <= query_pos)
            at = pl.ds(i * per, per)
            dq = dq_ref[at].reshape(wide, width)
            for h in range(heads):
                queries = q_ref[h, at].reshape(wide, width)
                grads = g_ref[h, at].reshape(wide, width)
                log_total = jnp.concatenate(
                    [lse_ref[i * per + n, h : h + 1, :] for n in range(per)], axis=1
                )
                delta = jnp.concatenate(
                    [delta_ref[i * per + n, h : h + 1, :] for n in range(per)], axis=1
                )
                scores = dot_last(keys, queries)
                probs = jnp.exp(jnp.where(allowed, scores - log_total, MASKED))
                d_scores = (probs * (dot_last(values, grads) - delta)).astype(BF16)
                dv = dv + dot(probs.astype(BF16), grads)
                dk = dk + dot(d_scores, queries)
                dq = dq + dot_first(d_scores, k_ref[h, j])
            dq_ref[at] = dq.reshape(per, span, width)
            return (dk, dv)

        zero = jnp.zeros((span, width), F32)
        dk, dv = lax.fori_loop(j // per, last, query_step, (zero, zero))
        dqkv_ref[j, 1] = dk.astype(BF16)
        dqkv_ref[j, 2] = dv.astype(BF16)
        dqkv_ref[j, 0] = (dq_ref[j] * score_scale).astype(BF16)
        return carry

    lax.fori_loop(0, blocks, key_block, 0)


def attend_back(
    order, offsets, slot, qkv, grads, grads_at, scaled, scaled_at, inverse_lanes, lse, heads, head_dim
):
    group, _, span, width = qkv.shape

    def block_spec(at):
        return pl.BlockSpec((group, None, span, width), lambda i: (0, at, 0, 0))

    return pl.pallas_call(
        functools.partial(attend_back_kernel, slot, heads, head_dim),
        grid=(1,),
        in_specs=[SMEM, SMEM, VMEM, VMEM, VMEM, block_spec(grads_at), block_spec(scaled_at)],
        out_specs=[pl.BlockSpec((group, None, 3, span, width), lambda i: (0, 0, 0, 0, 0)), VMEM],
        out_shape=[
            jax.ShapeDtypeStruct((group, 1, 3, span, width), BF16),
            jax.ShapeDtypeStruct((8, span), F32),
        ],
        scratch_shapes=[pltpu.VMEM((heads, group, span, width), BF16)] * 3
        + [pltpu.VMEM((group, 8, span), F32), pltpu.VMEM((group, span, width), F32)],
        compiler_params=kernel_params(),
        cost_estimate=cost(0, 1024),
        name="attend_back",
    )(order, offsets, inverse_lanes, lse, qkv, grads, scaled)


def join_grads_kernel(parts, in_ref, out_ref, value_ref):
    group = in_ref.shape[0]
    for n in range(3):
        whole = jnp.concatenate([in_ref[s, 0, n] for s in range(group)], axis=1)
        piece = whole.shape[1] // parts
        if n == 2:
            value_ref[...] = whole
            continue
        for p in range(parts):
            to = (p * 2 + n) * piece
            out_ref[:, to : to + piece] = whole[:, p * piece : (p + 1) * piece]


def join_grads(block):
    group, _, _, span, width = block.shape
    return pl.pallas_call(
        functools.partial(join_grads_kernel, PARTS),
        out_shape=[
            jax.ShapeDtypeStruct((span, 2 * group * width), BF16),
            jax.ShapeDtypeStruct((span, group * width), BF16),
        ],
        compiler_params=kernel_params(),
        cost_estimate=cost(0, 1024),
        name="join_grads",
    )(block)


FF_STEP = 1024
LAYER_VMEM = 62 * 1024 * 1024


def layer_kernel(
    slots,
    order_ref,
    post_ref,
    ffn_ref,
    mid_gain_ref,
    scale_ref,
    w_out_ref,
    x_hbm,
    d_out_hbm,
    d_mid_hbm,
    w_fc1_hbm,
    *refs,
):
    count = len(slots)
    o_refs = refs[:count]
    (
        scaled_ref,
        ffn_in_ref,
        residual_ref,
        mid_ref,
        d_pre_ref,
        d_proj_ref,
        d_residual_ref,
        d_attn_ref,
        g_post_ref,
        g_ffn_ref,
        g_mid_ref,
        x_ref,
        d_out_ref,
        d_mid_ref,
        w_fc1_ref,
        act_ref,
        slope_ref,
        sems,
        row_sems,
    ) = refs[count:]
    group, _, span, width = o_refs[0].shape
    tokens, hidden = act_ref.shape
    step = FF_STEP // count
    steps = [slice(c, c + step) for c in range(0, hidden, step)]
    weight_copies = [
        pltpu.make_async_copy(
            w_fc1_hbm.at[:, c : c + FF_STEP], w_fc1_ref.at[:, c : c + FF_STEP], sems.at[n]
        )
        for n, c in enumerate(range(0, hidden, FF_STEP))
    ]
    x_copies, mid_copies = [], []
    for n, slot in enumerate(slots):
        row = order_ref[slot]
        to = slice(n * span, (n + 1) * span)
        x_copies.append(pltpu.make_async_copy(x_hbm.at[row], x_ref.at[to], row_sems.at[0, n]))
        x_copies.append(
            pltpu.make_async_copy(d_out_hbm.at[row], d_out_ref.at[to], row_sems.at[1, n])
        )
        rows = pl.ds(pl.multiple_of(row * span, span), span)
        mid_copies.append(
            pltpu.make_async_copy(d_mid_hbm.at[rows], d_mid_ref.at[to], row_sems.at[2, n])
        )
    for copy in x_copies + weight_copies + mid_copies:
        copy.start()

    for n in range(count):
        for s in range(group):
            scaled_ref[n * span : (n + 1) * span, s * width : (s + 1) * width] = o_refs[n][s, 0]
    proj_hat, proj_spread = norm_parts(dot(scaled_ref[...], w_out_ref[...]))
    for copy in x_copies:
        copy.wait()
    residual = x_ref[...].astype(F32) + proj_hat * post_ref[...]
    residual_ref[...] = residual
    res_hat, res_spread = norm_parts(residual)
    ffn_in = (res_hat * ffn_ref[...]).astype(BF16)
    ffn_in_ref[...] = ffn_in

    total = jnp.zeros((tokens, 1), F32)
    for n, at in enumerate(steps):
        if n % count == 0:
            weight_copies[n // count].wait()
        pre = dot(ffn_in, w_fc1_ref[:, at])
        phi = 0.5 + 0.5 * lax.erf(pre * (0.5**0.5))
        act = pre * phi
        act_ref[:, at] = act
        slope = phi + pre * jnp.exp(-0.5 * pre * pre) * 0.3989422804014327
        slope_ref[:, at] = slope.astype(slope_ref.dtype)
        total += jnp.sum(act, axis=1, keepdims=True)
    average = total / hidden
    total = jnp.zeros((tokens, 1), F32)
    for at in steps:
        centred = act_ref[:, at] - average
        total += jnp.sum(centred * centred, axis=1, keepdims=True)
    spread = lax.rsqrt(total / hidden + EPSILON)

    for copy in mid_copies:
        copy.wait()
    sum_weighted = jnp.zeros((tokens, 1), F32)
    sum_hat = jnp.zeros((tokens, 1), F32)
    for at in steps:
        hat = (act_ref[:, at] - average) * spread
        act_ref[:, at] = hat
        gain = mid_gain_ref[:, at]
        mid_ref[:, at] = (hat * gain).astype(BF16)
        grad = d_mid_ref[:, at]
        product = grad * hat
        g_mid_ref[:, at] = jnp.sum(product, axis=0, keepdims=True)
        sum_weighted += jnp.sum(grad * gain, axis=1, keepdims=True)
        sum_hat += jnp.sum(product * gain, axis=1, keepdims=True)
    sum_weighted = sum_weighted / hidden
    sum_hat = sum_hat / hidden
    d_ffn = jnp.zeros(x_ref.shape, F32)
    for at in steps:
        weighted = d_mid_ref[:, at] * mid_gain_ref[:, at]
        d_act = spread * (weighted - sum_weighted - act_ref[:, at] * sum_hat)
        d_pre = (d_act * slope_ref[:, at].astype(F32)).astype(BF16)
        d_pre_ref[:, at] = d_pre
        d_ffn += dot_last(d_pre, w_fc1_ref[:, at])

    g_ffn_ref[...] = jnp.sum(d_ffn * res_hat, axis=0, keepdims=True)
    d_residual = d_out_ref[...].astype(F32) + norm_back(res_hat, res_spread, ffn_ref[...], d_ffn)
    d_residual_ref[...] = d_residual
    g_post_ref[...] = jnp.sum(d_residual * proj_hat, axis=0, keepdims=True)
    d_proj = norm_back(proj_hat, proj_spread, post_ref[...], d_residual).astype(BF16)
    d_proj_ref[...] = d_proj
    d_attn = (dot_last(d_proj, w_out_ref[...]) * scale_ref[...]).astype(BF16)
    for n in range(count):
        for s in range(group):
            d_attn_ref[s, n] = d_attn[n * span : (n + 1) * span, s * width : (s + 1) * width]


def layer(order, slots, blocks, x, d_out, gains, w_out, d_mid, w_fc1):
    group, _, span, width = blocks[0][0].shape
    model, hidden = w_fc1.shape
    tokens = len(slots) * span
    shape = jax.ShapeDtypeStruct

    def block_spec(at):
        return pl.BlockSpec((group, 1, span, width), lambda i, o: (0, at, 0, 0))

    return pl.pallas_call(
        functools.partial(layer_kernel, slots),
        grid_spec=pltpu.PrefetchScalarGridSpec(
            num_scalar_prefetch=1,
            grid=(1,),
            in_specs=[VMEM] * 5
            + [pl.BlockSpec(memory_space=pl.ANY)] * 4
            + [block_spec(at) for _, at in blocks],
            out_specs=[VMEM] * 11,
            scratch_shapes=[
                pltpu.VMEM((tokens, model), BF16),
                pltpu.VMEM((tokens, model), BF16),
                pltpu.VMEM((tokens, hidden), d_mid.dtype),
                pltpu.VMEM(w_fc1.shape, BF16),
                pltpu.VMEM((tokens, hidden), F32),
                pltpu.VMEM((tokens, hidden), F32 if len(slots) == 1 else BF16),
                pltpu.SemaphoreType.DMA((hidden // FF_STEP,)),
                pltpu.SemaphoreType.DMA((3, len(slots))),
            ],
        ),
        out_shape=[
            shape((tokens, model), BF16),
            shape((tokens, model), BF16),
            shape((tokens, model), F32),
            shape((tokens, hidden), BF16),
            shape((tokens, hidden), BF16),
            shape((tokens, model), BF16),
            shape((tokens, model), F32),
            shape((group, len(slots), span, width), BF16),
            shape((1, model), F32),
            shape((1, model), F32),
            shape((1, hidden), F32),
        ],
        compiler_params=pltpu.CompilerParams(vmem_limit_bytes=LAYER_VMEM),
        cost_estimate=cost(0, 1024),
        name="layer",
    )(order, *gains, w_out, x, d_out, d_mid, w_fc1, *[block for block, _ in blocks])


def layer_out_kernel(order_ref, *refs):
    count = (len(refs) - 2) // 2
    weight, out_ref = refs[-2], refs[-1]
    span, slot = out_ref.shape[1], 0
    for n in range(count):
        result = (refs[n][...] + dot(refs[count + n][...], weight[...])).astype(BF16)
        for at in range(0, result.shape[0], span):
            out_ref[order_ref[slot]] = result[at : at + span]
            slot += 1


def last_step(order, shape, residuals, mids, w_fc2):
    return pl.pallas_call(
        layer_out_kernel,
        in_specs=[SMEM] + [VMEM] * (2 * len(mids) + 1),
        out_shape=jax.ShapeDtypeStruct(shape, BF16),
        compiler_params=kernel_params(),
        cost_estimate=cost(0, 1024),
        name="layer_out",
    )(order, *residuals, *mids, w_fc2)


def flip(value, axis, bit):
    size = lax.axis_size(axis)
    return lax.ppermute(value, axis, [(i, i ^ (1 << bit)) for i in range(size)])


def bits(axis):
    return (lax.axis_size(axis) - 1).bit_length()


PARTS = 4


def weight_kernel(count, rows, added, shards, part_ref, *refs):
    out_ref = refs[-1]
    high = out_ref.shape[1]
    per = rows * (shards + 1)
    extras = refs[per * count : per * count + added]
    at = 0
    for n in range(count):
        mine = refs[n * per : (n + 1) * per]
        rights = mine[rows * shards :]
        width = rights[0].shape[1]
        total = 0.0
        for r in range(rows):
            left = [ref[...] for ref in mine[r * shards : (r + 1) * shards]]
            left = jnp.concatenate(left, axis=1) if shards > 1 else left[0]
            total += dot_first(left, rights[r][...])
        for i in range(shards):
            piece = total[i * high : (i + 1) * high]
            for extra in extras:
                piece = piece + extra[i, :, at : at + width].astype(F32)
            out_ref[i, :, at : at + width] = piece.astype(BF16)
        at += width


def weight_part_plain(pairs, part, parts, extras, group):
    pieces = []
    for lefts, rights, kind in pairs:
        left, right = jnp.concatenate(lefts), jnp.concatenate(rights)
        if kind == "columns":
            wide = right.shape[1] // parts
            right = lax.dynamic_slice(right, (0, part * wide), (right.shape[0], wide))
            left = left.reshape(left.shape[0], group, -1)
        else:
            left = left.reshape(left.shape[0], group, parts, -1)
            left = lax.dynamic_index_in_dim(left, part, 2, keepdims=False)
        pieces.append(jnp.einsum("tsd,te->sde", left, right, preferred_element_type=F32))
    total = jnp.concatenate(pieces, axis=2)
    axis = 2 if pairs[0][2] == "columns" else 1
    for extra, at in extras:
        size = total.shape[axis]
        total = total + lax.dynamic_slice_in_dim(extra, at * size, size, axis).astype(F32)
    return total.astype(BF16)


def weight_part(pairs, part, parts, extras, group):
    shards = 2
    specs, arrays, width = [], [], 0
    for lefts, rights, kind in pairs:
        model = lefts[0].shape[1]
        stride = 1 if kind == "columns" else parts
        high = model // group // stride
        wide = rights[0].shape[1] // (parts if kind == "columns" else 1)
        for left in lefts:
            for i in range(shards):

                def left_at(g, p, i=i, stride=stride):
                    return (0, (g * shards + i) * stride + (p[0] if stride > 1 else 0))

                specs.append(pl.BlockSpec((left.shape[0], high), left_at))
                arrays.append(left)
        for right in rights:

            def right_at(g, p, stride=stride):
                return (0, p[0] if stride == 1 else 0)

            specs.append(pl.BlockSpec((right.shape[0], wide), right_at))
            arrays.append(right)
        width += wide
    if high % 128:
        return weight_part_plain(pairs, part, parts, extras, group)
    block = pl.BlockSpec((shards, high, width), lambda g, p: (g, 0, 0))
    by_row = pairs[0][2] == "rows"

    def extra_spec(n):
        def block_at(g, p):
            return (g, p[n], 0) if by_row else (g, 0, p[n])

        return pl.BlockSpec((shards, high, width), block_at)

    numbers = jnp.stack([part] + [at for _, at in extras]).astype(jnp.int32)
    return pl.pallas_call(
        functools.partial(weight_kernel, len(pairs), len(pairs[0][0]), len(extras), shards),
        grid_spec=pltpu.PrefetchScalarGridSpec(
            num_scalar_prefetch=1,
            grid=(group // shards,),
            in_specs=specs + [extra_spec(n + 1) for n in range(len(extras))],
            out_specs=block,
        ),
        out_shape=jax.ShapeDtypeStruct((group, high, width), BF16),
        compiler_params=kernel_params(),
        cost_estimate=cost(0, 1024),
        name="weight_part",
    )(numbers, *arrays, *[extra for extra, _ in extras])


class WeightSum:
    def __init__(self, *pairs):
        self.pairs = pairs
        batch_at = lax.axis_index("batch")
        self.near, self.far = batch_at & 1, (batch_at >> 1) & 1
        self.zero = batch_at * 0

    def piece(self, order, near, far, *extras):
        def part_of(part):
            return weight_part(self.pairs, part, PARTS, extras, lax.axis_size("blk"))

        return order(part_of, near * 2 + far)

    def half(self, order, near, *extras):
        def part_of(part):
            return weight_part(self.pairs, part, 2, extras, lax.axis_size("blk"))

        return order(part_of, near)

    def away_far(self, order):
        return self.piece(order, 1 - self.near, 1 - self.far)

    def away_near(self, order):
        return self.piece(order, 1 - self.near, self.far)

    def away(self, order, *more):
        return self.half(order, 1 - self.near, *more)

    def send_far(self, order, away):
        return self.piece(order, self.near, 1 - self.far, (away, self.zero))

    def send(self, order, *aways):
        extras = [(away, 1 - self.far) for away in aways]
        return self.piece(order, self.near, 1 - self.far, *extras)

    def keep(self, order, near, arrived):
        return self.piece(order, self.near, self.far, (near, self.zero), (arrived, self.zero))

    def keep_rest(self, order, arrived, *aways):
        extras = [(away, self.far) for away in aways]
        return self.piece(order, self.near, self.far, (arrived, self.zero), *extras)

    def own(self, order, *aways):
        return self.half(order, self.near, *[(away, self.zero) for away in aways])


def over_near(sent):
    return flip(sent, "batch", 0)


def over_far(sent):
    return flip(sent, "batch", 1)


class Order:
    def __init__(self):
        self.last = ()

    def __call__(self, step, *values):
        self.last = step(*tie(values, self.last))
        return self.last


def window(always, step):
    def nothing():
        return jax.tree.map(lambda leaf: jnp.zeros(leaf.shape, leaf.dtype), jax.eval_shape(step))

    return lax.cond(always, step, nothing)


def tie(values, *after):
    return lax.optimization_barrier((values, after))[0]


def combine_kernel(plan, at_ref, *refs):
    ins = sum(count for _, count, _ in plan)
    into, out_of = list(refs[:ins]), list(refs[ins:])
    for n, (kind, count, cut) in enumerate(plan):
        terms = [into.pop(0) for _ in range(count)]
        if kind == "small":
            out_of.pop(0)[...] = sum(term[...] for term in terms)
            continue
        if kind == "stack":
            out = out_of.pop(0)
            out[0], out[1] = terms[0][0], terms[1][0]
            continue

        def put(ref, j, i):
            if kind == "add":
                ref[j] = (terms[0][i].astype(F32) + terms[1][i].astype(F32)).astype(BF16)
                return
            at = 0
            for term in terms:
                ref[j, :, at : at + term.shape[2]] = term[i]
                at += term.shape[2]

        if cut:
            keep, send = out_of.pop(0), out_of.pop(0)
            for j in range(keep.shape[0]):
                put(keep, j, 2 * j + at_ref[n])
                put(send, j, 2 * j + 1 - at_ref[n])
        else:
            whole = out_of.pop(0)
            for j in range(whole.shape[0]):
                put(whole, j, j)


class Tree:
    def __init__(self, *mine, halved=2):
        self.steps = [("blk", bit) for bit in range(bits("blk"))]
        self.steps += [("batch", bit) for bit in range(halved, bits("batch"))]
        self.steps += [("far", 1), ("near", 0)][2 - halved :]
        self.terms, self.last = list(mine), "first"

    def start(self):
        kind, bit = self.steps[0]
        return flip(self.send, "blk" if kind == "blk" else "batch", bit)

    def end(self, arrived):
        self.last = self.steps.pop(0)[0]
        self.terms = [self.kept, arrived]


def combine(trees):
    me = lax.axis_index("blk")
    plan, ins, shapes, at = [], [], [], []
    for tree in trees:
        kind, bit = tree.steps[0]
        cut = kind == "blk" and tree.last != "small"
        if tree.last == "small":
            plan.append(("small", len(tree.terms), False))
            ins += tree.terms
            shapes.append(jax.ShapeDtypeStruct(tree.terms[0].shape, F32))
            at.append(me * 0)
            continue
        state = {"first": "first", "far": "stack"}.get(tree.last, "add")
        plan.append((state, len(tree.terms), cut))
        ins += tree.terms
        count, high, wide = tree.terms[0].shape
        if state == "first":
            wide = sum(term.shape[2] for term in tree.terms)
        count = count // 2 if cut else 2 if state == "stack" else count
        shapes += [jax.ShapeDtypeStruct((count, high, wide), BF16)] * (2 if cut else 1)
        at.append((me >> bit) & 1 if cut else me * 0)
    outs = list(
        pl.pallas_call(
            functools.partial(combine_kernel, plan),
            in_specs=[SMEM] + [VMEM] * len(ins),
            out_shape=shapes,
            compiler_params=kernel_params(),
            cost_estimate=cost(0, 1024),
            name="combine",
        )(jnp.stack(at).astype(jnp.int32), *ins)
    )
    for tree, (_, _, cut) in zip(trees, plan):
        tree.kept = outs.pop(0)
        tree.send = outs.pop(0) if cut else tree.kept


def place_kernel(layout, lines, part_ref, *refs):
    count = 2 * len(layout) + (2 if lines else 0)
    ins, outs = list(refs[:count]), list(refs[count:])
    if lines:
        one, other = ins[-2:]
        for (start, size, cut), out in zip(lines, outs[-len(lines) :]):
            at = pl.ds(start, size)
            if cut:
                at = pl.ds(pl.multiple_of(start + part_ref[2] * size, 128), size)
            out[...] = one[:, at] + other[:, at]
    near, far = part_ref[0], part_ref[1]
    order = [near * 2 + far, near * 2 + 1 - far, (1 - near) * 2 + far, (1 - near) * 2 + 1 - far]
    for spans in layout:
        both = [ins.pop(0), ins.pop(0)]
        count = 2 * both[0].shape[0]
        for start, width, kind in spans:
            out = outs.pop(0)
            for n, part in enumerate(order if count == 4 else [near, 1 - near]):
                value = both[n * 2 // count][n % (count // 2), :, start : start + width]
                value = value.astype(F32)
                if kind == "columns":
                    out[:, pl.ds(pl.multiple_of(part * width, 128), width)] = value
                else:
                    high = value.shape[0]
                    out[pl.ds(pl.multiple_of(part * high, 8), high), :] = value


def place(trees, layout, small=None, lines=()):
    batch_at = lax.axis_index("batch")
    parts = jnp.stack([batch_at & 1, (batch_at >> 1) & 1, lax.axis_index("blk")])
    parts = parts.astype(jnp.int32)
    ins, shapes = [], []
    for tree, spans in zip(trees, layout):
        ins += tree.terms
        count, high = 2 * tree.kept.shape[0], tree.kept.shape[1]
        for _, width, kind in spans:
            shape = (high, count * width) if kind == "columns" else (count * high, width)
            shapes.append(jax.ShapeDtypeStruct(shape, F32))
    if lines:
        ins += small.terms
        shapes += [jax.ShapeDtypeStruct((1, size), F32) for _, size, _ in lines]
    return pl.pallas_call(
        functools.partial(place_kernel, layout, lines),
        in_specs=[SMEM] + [VMEM] * len(ins),
        out_shape=shapes,
        compiler_params=kernel_params(),
        cost_estimate=cost(0, 1024),
        name="place",
    )(parts, *ins)


class SmallSum:
    def __init__(self, mine):
        self.steps = [("batch", bit) for bit in range(bits("batch"))]
        self.steps += [("blk", bit) for bit in range(bits("blk"))]
        self.terms, self.last = [mine], "small"

    def start(self):
        return flip(self.send, *self.steps[0])

    def end(self, arrived):
        self.steps.pop(0)
        self.terms = [self.kept, arrived]


def input_grad_kernel(parts, order_ref, x_ref, gain_ref, wq_ref, wk_ref, wv_ref, *refs):
    out_ref, sum_ref = refs[-2:]
    rows, span, model = x_ref.shape
    piece = model // parts
    total = jnp.zeros(sum_ref.shape, F32)
    residuals = [
        held.at[pl.ds(at, span)] for held in refs[2 * rows : -2] for at in range(0, held.shape[0], span)
    ]
    for r in range(rows):
        d_ref, value_ref, res_ref = refs[r], refs[rows + r], residuals[r]
        grad = dot_last(value_ref[...], wv_ref[...])
        for p in range(parts):
            for n, weight in enumerate((wq_ref, wk_ref)):
                at = (p * 2 + n) * piece
                grad += dot_last(d_ref[:, at : at + piece], weight[:, p * piece : (p + 1) * piece])
        row = order_ref[r]
        hat, spread = norm_parts(x_ref[row].astype(F32))
        out_ref[row] = res_ref[...] + norm_back(hat, spread, gain_ref[...], grad)
        total += jnp.sum(grad * hat, axis=0, keepdims=True)
    sum_ref[...] = total


def input_grad(order, x, gain, w_query, w_key, w_value, d_rows, d_values, d_residuals):
    return pl.pallas_call(
        functools.partial(input_grad_kernel, PARTS),
        in_specs=[SMEM] + [VMEM] * (5 + 2 * len(d_rows) + len(d_residuals)),
        out_shape=[
            jax.ShapeDtypeStruct(x.shape, F32),
            jax.ShapeDtypeStruct((1, x.shape[2]), F32),
        ],
        compiler_params=kernel_params(),
        cost_estimate=cost(0, 1024),
        name="input_grad",
    )(order, x, gain, w_query, w_key, w_value, *d_rows, *d_values, *d_residuals)


def on_device(
    inputs,
    ln_attn,
    w_query,
    w_key,
    w_value,
    w_out,
    head_scale,
    ln_post,
    ln_ffn,
    w_fc1,
    ln_mid,
    w_fc2,
    offsets,
    cotangent,
):
    row_count, span, model = inputs.shape
    head_count = head_scale.shape[0]
    head_dim = model // head_count
    tokens = row_count * span
    group = lax.axis_size("blk")
    heads = head_count // group
    width = heads * head_dim
    my_index = lax.axis_index("blk")
    rows = range(row_count)

    always = offsets[0, 0] == 0
    gain = ln_attn.reshape(1, model)
    last = row_count - 1
    my_scale = lax.dynamic_slice(head_scale, (my_index * heads,), (heads,))
    scale_lanes = jnp.repeat(my_scale, head_dim).reshape(1, width)
    layer_gains = [
        ln_post.reshape(1, model),
        ln_ffn.reshape(1, model),
        ln_mid.reshape(1, -1),
        jnp.repeat(head_scale, head_dim).reshape(1, model),
    ]

    def project_row(r, x):
        return project(offsets, r, x, gain, w_query, w_key, w_value, group)

    def attend_one(r, held, into=None):
        place = (r, last) if r < last else (0, 1)
        return attend(by_work, offsets, r, held, scale_lanes, heads, head_dim, *place, into)

    def layer_rows(slots, blocks):
        return layer(by_work, slots, blocks, inputs, cotangent, layer_gains, w_out, d_mid, w_fc1)

    def back(order, r, row_heads, at=0):
        def back_row(held):
            return attend_back(
                by_work,
                offsets,
                r,
                held,
                row_heads,
                at,
                *((first_out, r) if r < last else (last_out, 0)),
                1.0 / scale_lanes,
                lse[r],
                heads,
                head_dim,
            )

        return order(back_row, qkv[r])

    def first_window():
        order = Order()
        return exchange(sent), [
            order(functools.partial(project_row, r), inputs) for r in rows[1:]
        ]

    normed_first, sent, by_work = project_row(0, inputs)
    held, projected = first_window()
    qkv = [held]
    normed = [normed_first] + [part[0] for part in projected]
    first_out, lse = None, []
    for r in rows[1:]:

        def next_window():
            order = Order()
            extra = ()
            if r == 1:
                d_mid = jnp.einsum(
                    "td,fd->tf",
                    cotangent.reshape(tokens, model),
                    w_fc2,
                    preferred_element_type=F32,
                )
                extra = d_mid
            if r == last:
                d_out = [
                    lax.dynamic_index_in_dim(cotangent, by_work[n], keepdims=False) for n in rows
                ]
                extra = d_out[0], jnp.concatenate(d_out[1:])
            return exchange(projected[r - 1][1]), attend_one(r - 1, qkv[r - 1], first_out), extra

        held, (first_out, log_total), extra = window(always, next_window)
        d_mid = extra if r == 1 else d_mid
        qkv.append(held)
        lse.append(log_total)

    d_out = list(extra)

    def early_window():
        return (
            exchange(first_out),
            attend_one(last, qkv[last]),
        )

    early, (last_out, log_total) = window(always, early_window)
    lse.append(log_total)

    def late_window():
        return exchange(last_out), layer_rows([0], [(early, 0)])

    late, layer_first = window(always, late_window)

    def layer_window():
        blocks = [(early, r) if r < last else (late, 0) for r in rows[1:]]
        return exchange(layer_first[7]), layer_rows(list(rows[1:]), blocks)

    first_heads, layer_rest = window(always, layer_window)
    (
        scaled,
        ffn_in,
        residual,
        mid,
        d_pre,
        d_proj,
        d_residual,
        d_attn,
        g_post,
        g_ffn,
        g_mid,
    ) = zip(layer_first, layer_rest)
    sum_one = WeightSum((mid, d_out, "rows"))
    sum_two = WeightSum((ffn_in, d_pre, "columns"))
    sum_three = WeightSum((scaled, d_proj, "columns"))
    order = Order()
    away_one = over_near(sum_one.away_far(order))
    near_one = over_near(sum_one.away_near(order))
    far_one = over_far(sum_one.send_far(order, away_one))

    def back_first():
        order = Order()
        heads_in = exchange(d_attn[1])
        away = over_near(sum_two.away_far(order))
        out = back(order, 0, first_heads)
        return heads_in, out, sum_two.send_far(order, away)

    rest_heads, (sent, total), sent_two = window(always, back_first)
    far_two = over_far(sent_two)
    totals = [total]

    def back_second():
        order = Order()
        grad = exchange(sent)
        out = back(order, 1, rest_heads, 0)
        near = sum_two.away_near(order), sum_three.away(order)
        return grad, out, near, sum_one.keep(order, near_one, far_one)

    grad, (sent, total), near, mine_one = window(always, back_second)
    near_two, away_three = near
    totals.append(total)
    grads = [grad]
    tree_one = Tree(mine_one)
    combine([tree_one])
    moved = tree_one.start()
    sent = tie(sent, tree_one.send)
    near_two, away_three = over_near(near_two), over_near(away_three)
    for r in rows[2:]:

        def back_next():
            order = Order()
            out_of = ()
            grad = exchange(sent)
            out = back(order, r, rest_heads, r - 1)
            if r == 2:
                mine = sum_two.keep(order, near_two, far_two)
                out_of = mine, sum_three.own(order, away_three)
            return grad, out_of, out

        grad, out_of, (sent, total) = window(always, back_next)
        totals.append(total)
        grads.append(grad)
        if r == 2:
            mine_two, mine_three = out_of
    tree_one.end(moved)
    tree_two = Tree(mine_two)
    combine([tree_one, tree_two])

    moved = tree_one.start(), tree_two.start()
    sent = tie(sent, tree_one.send, tree_two.send)

    def back_last():
        order = Order()
        grad = exchange(sent)
        joined = [order(join_grads, part) for part in grads]

        def output_step(weight):
            return last_step(by_work, inputs.shape, residual, mid, weight)

        d_rows, d_values = zip(*joined)
        early_qk = WeightSum((normed[:last], d_rows, "columns"))
        early_v = WeightSum((normed[:last], d_values, "columns"))
        early = [early_qk.away(order), early_v.away(order), early_qk.own(order), early_v.own(order)]
        return grad, joined, order(output_step, w_fc2), early

    grad, joined, layer_out, early_sums = window(always, back_last)
    early_away_qk, early_away_v, early_qk, early_v = early_sums
    grad, moved = tie((grad, moved))
    tree_one.end(moved[0])
    tree_two.end(moved[1])
    order = Order()
    joined = joined + [order(join_grads, grad)]
    d_rows, d_values = zip(*joined)
    sum_qk = WeightSum((normed[last:], d_rows[last:], "columns"))
    sum_v = WeightSum((normed[last:], d_values[last:], "columns"))
    away_qk = over_near(sum_qk.away(order, (early_away_qk, sum_qk.zero)))
    away_v = over_near(sum_v.away(order, (early_away_v, sum_v.zero)))
    sent_qk = sum_qk.send(order, away_qk, early_qk)
    tree_v = Tree(sum_v.own(order, away_v, early_v), mine_three, halved=1)
    combine([tree_one, tree_two, tree_v])

    def advance(trees, extra=lambda: ()):
        def step():
            return [tree.start() for tree in trees], extra()

        moved, out = window(always, step)
        for tree, arrived in zip(trees, moved):
            tree.end(arrived)
        return out

    def beside():
        order = Order()
        arrived = over_far(sent_qk)

        def input_step(x):
            return input_grad(
                by_work, x, gain, w_query, w_key, w_value, d_rows, d_values, d_residual
            )

        return arrived, order(input_step, inputs)

    far_qk, (grad_inputs, grad_ln_attn) = advance(
        [tree_one, tree_two, tree_v], beside
    )
    tree_qk = Tree(sum_qk.keep_rest(order, far_qk, away_qk, early_qk))
    delta_sum = sum(jnp.sum(total, axis=1) for total in totals)
    my_grad = delta_sum[:heads] / my_scale
    scale_part = lax.dynamic_update_slice(
        jnp.zeros((head_count,), F32), my_grad, (my_index * heads,)
    )
    small = SmallSum(
        jnp.concatenate(
            [grad_ln_attn[0], sum(g_post)[0], sum(g_ffn)[0], sum(g_mid)[0], scale_part]
        ).reshape(1, -1)
    )
    piece = model // PARTS
    ff_piece = w_fc1.shape[1] // PARTS
    trees = [tree_qk, tree_v, tree_two, tree_one]
    placed = None
    while any(tree.steps for tree in trees + [small]):
        combine([tree for tree in trees + [small] if tree.steps])

        def place_early():
            if tree_two.steps or tree_one.steps or placed is not None:
                return ()
            return place(
                [tree_one, tree_two], [[(0, model, "rows")], [(0, ff_piece, "columns")]]
            )

        early_out = advance([tree for tree in trees + [small] if tree.steps], place_early)
        placed = early_out or placed
    if placed is None:
        placed = place([tree_one, tree_two], [[(0, model, "rows")], [(0, ff_piece, "columns")]])
    grad_fc2, grad_fc1 = placed
    lines = [(0, model), (model, model), (2 * model, model), (3 * model, ln_mid.shape[0])]
    ends = lines[-1][0] + lines[-1][1]
    layout = [
        [(n * piece, piece, "columns") for n in range(2)],
        [(n * 2 * piece, 2 * piece, "columns") for n in range(2)],
    ]
    if model // group % 128:
        grad_query, grad_key, grad_value, grad_out = place([tree_qk, tree_v], layout)
        total = sum(small.terms)[0]
        gains = [
            lax.dynamic_slice(total, (start + my_index * (size // group),), (size // group,))
            for start, size in lines
        ]
        gains.append(total[ends:])
    else:
        lines = [(start, size // group, True) for start, size in lines]
        lines.append((ends, head_count, False))
        grad_query, grad_key, grad_value, grad_out, *gains = place(
            [tree_qk, tree_v], layout, small, lines
        )
        gains = [line[0] for line in gains]
    return (
        layer_out,
        grad_inputs,
        gains[0],
        grad_query,
        grad_key,
        grad_value,
        grad_out,
        gains[4],
        gains[1],
        gains[2],
        grad_fc1,
        gains[3],
        grad_fc2,
    )


def solution(mesh):
    rows = P("batch", "blk", None)
    shard = P("blk", None)
    return jax.shard_map(
        on_device,
        mesh=mesh,
        in_specs=(rows,) + (P(),) * 11 + (P("batch", None), rows),
        out_specs=(
            rows,
            rows,
            P("blk"),
            shard,
            shard,
            shard,
            shard,
            P(),
            P("blk"),
            P("blk"),
            shard,
            P("blk"),
            shard,
        ),
        check_vma=False,
    )
```

```python
import functools

import jax
import jax.numpy as jnp
from jax import lax
from jax.experimental import pallas as pl
from jax.experimental.pallas import tpu as pltpu
from jax.sharding import PartitionSpec as P

EPSILON = 1e-05
MASKED = -1e30
VMEM_BYTES = 50 * 1024 * 1024
F32 = jnp.float32
BF16 = jnp.bfloat16
LAST = (((1,), (1,)), ((), ()))
FIRST = (((0,), (0,)), ((), ()))
SMEM = pl.BlockSpec(memory_space=pltpu.SMEM)
VMEM = pl.BlockSpec(memory_space=pltpu.VMEM)


def dot_last(left, right):
    return lax.dot_general(left, right, LAST, preferred_element_type=F32)


def dot_first(left, right):
    return lax.dot_general(left, right, FIRST, preferred_element_type=F32)


def dot(left, right):
    return jnp.dot(left, right, preferred_element_type=F32)


def kernel_params():
    return pltpu.CompilerParams(vmem_limit_bytes=VMEM_BYTES)


def cost(flops, size):
    return pl.CostEstimate(flops=int(flops), bytes_accessed=int(size), transcendentals=0)


def exchange(parts):
    return lax.all_to_all(parts, "blk", 0, 0, tiled=True)


def norm_parts(rows_in):
    average = jnp.mean(rows_in, axis=-1, keepdims=True)
    centred = rows_in - average
    spread = lax.rsqrt(jnp.mean(centred * centred, axis=-1, keepdims=True) + EPSILON)
    return centred * spread, spread


def norm_back(hat, spread, gain, grad):
    weighted = grad * gain
    return spread * (
        weighted
        - jnp.mean(weighted, axis=-1, keepdims=True)
        - hat * jnp.mean(weighted * hat, axis=-1, keepdims=True)
    )


def rows_by_work(offs_ref, length):
    rows, docs = offs_ref.shape
    work = []
    for r in range(rows):
        total = jnp.int32(0)
        for d in range(docs):
            end = offs_ref[r, d + 1] if d + 1 < docs else length
            total += (end - offs_ref[r, d]) * (end - offs_ref[r, d])
        work.append(total)
    ranks = []
    for r in range(rows):
        rank = jnp.int32(0)
        for other in range(rows):
            if other < r:
                rank += (work[other] >= work[r]).astype(jnp.int32)
            elif other > r:
                rank += (work[other] > work[r]).astype(jnp.int32)
        ranks.append(rank)
    return [
        sum(jnp.where(ranks[r] == slot, jnp.int32(r), jnp.int32(0)) for r in range(rows))
        for slot in range(rows)
    ]


def project_kernel(
    slot,
    offs_ref,
    gain_ref,
    x_hbm,
    wq_hbm,
    wk_hbm,
    wv_hbm,
    normed_ref,
    out_ref,
    order_ref,
    x_ref,
    weight_ref,
    sems,
):
    group, _, span, width = out_ref.shape
    order = rows_by_work(offs_ref, group * span)
    copy_x = pltpu.make_async_copy(x_hbm.at[order[slot]], x_ref, sems.at[3])
    copy_x.start()
    copies = [
        pltpu.make_async_copy(weight, weight_ref.at[n], sems.at[n])
        for n, weight in enumerate((wq_hbm, wk_hbm, wv_hbm))
    ]
    for copy in copies:
        copy.start()
    for r, row in enumerate(order):
        order_ref[r] = row
    copy_x.wait()
    hat, _ = norm_parts(x_ref[...].astype(F32))
    normed = (hat * gain_ref[...]).astype(BF16)
    normed_ref[...] = normed
    for n in range(3):
        copies[n].wait()
        product = dot(normed, weight_ref[n]).astype(BF16)
        for s in range(group):
            out_ref[s, n] = product[:, s * width : (s + 1) * width]


def project(offsets, slot, x, gain, w_query, w_key, w_value, group):
    rows, span, model = x.shape
    return pl.pallas_call(
        functools.partial(project_kernel, slot),
        in_specs=[SMEM, VMEM] + [pl.BlockSpec(memory_space=pl.ANY)] * 4,
        out_specs=[VMEM, VMEM, SMEM],
        scratch_shapes=[
            pltpu.VMEM((span, model), BF16),
            pltpu.VMEM((3, model, model), BF16),
            pltpu.SemaphoreType.DMA((4,)),
        ],
        out_shape=[
            jax.ShapeDtypeStruct((span, model), BF16),
            jax.ShapeDtypeStruct((group, 3, span, model // group), BF16),
            jax.ShapeDtypeStruct((rows,), jnp.int32),
        ],
        compiler_params=kernel_params(),
        cost_estimate=cost(0, 1024),
        name="project",
    )(offsets, gain, x, w_query, w_key, w_value)


def doc_start(offs_ref, row, pos):
    start = jnp.zeros_like(pos)
    for d in range(offs_ref.shape[1]):
        first = offs_ref[row, d]
        start = jnp.where(pos >= first, first, start)
    return start


def doc_end(offs_ref, row, pos, length):
    end = jnp.int32(length)
    for d in reversed(range(offs_ref.shape[1])):
        first = offs_ref[row, d]
        end = jnp.where(first > pos, first, end)
    return end


def head_lanes(shape, head, head_dim):
    lane = lax.broadcasted_iota(jnp.int32, shape, 1)
    return (lane >= head * head_dim) & (lane < (head + 1) * head_dim)


def attend_kernel(slot, heads, head_dim, order_ref, offs_ref, scale_ref, held, *refs):
    result_ref, lse_ref, score_ref = refs[-3:]
    attend_row(
        order_ref[slot], heads, head_dim, offs_ref, scale_ref, held, result_ref, lse_ref, score_ref
    )


def attend_row(
    row, heads, head_dim, offs_ref, scale_ref, held, result_ref, lse_ref, score_ref
):
    blocks, _, span, width = held.shape
    wide = score_ref.shape[-1]
    per = wide // span
    lanes = min(128, wide)
    score_scale = head_dim ** (-0.5)

    def query_block(i, carry):
        first_pos = i * span
        queries = held[i, 0] * jnp.asarray(score_scale, BF16)
        query_head = [
            jnp.where(head_lanes((span, width), h, head_dim), queries, 0).astype(BF16)
            for h in range(heads)
        ]
        query_pos = first_pos + lax.broadcasted_iota(jnp.int32, (span, 1), 0)
        query_start = doc_start(offs_ref, row, query_pos)
        low = doc_start(offs_ref, row, first_pos) // wide
        high = (first_pos + span - 1) // wide + 1

        def score_step(j, tops):
            keys = held[pl.ds(j * per, per), 1].reshape(wide, width)
            key_pos = j * wide + lax.broadcasted_iota(jnp.int32, (span, wide), 1)
            allowed = (key_pos >= query_start) & (key_pos <= query_pos)
            new = []
            for h in range(heads):
                scores = jnp.where(allowed, dot_last(query_head[h], keys), MASKED)
                score_ref[h, j] = scores
                top = tops[h]
                for c in range(0, wide, lanes):
                    top = jnp.maximum(top, scores[:, c : c + lanes])
                new.append(top)
            return tuple(new)

        tops = lax.fori_loop(
            low, high, score_step, tuple(jnp.full((span, lanes), MASKED, F32) for h in range(heads))
        )
        tops = [jnp.max(top, axis=1, keepdims=True) for top in tops]

        def value_step(j, state):
            values = held[pl.ds(j * per, per), 2].reshape(wide, width)
            new = []
            for h in range(heads):
                total, acc = state[h]
                probs = jnp.exp(score_ref[h, j] - tops[h])
                for c in range(0, wide, lanes):
                    total = total + probs[:, c : c + lanes]
                acc = acc + dot(probs.astype(BF16), values)
                new.append((total, acc))
            return tuple(new)

        state = lax.fori_loop(
            low,
            high,
            value_step,
            tuple(
                (jnp.zeros((span, lanes), F32), jnp.zeros((span, width), F32)) for h in range(heads)
            ),
        )
        result = jnp.zeros((span, width), F32)
        for h in range(heads):
            total = jnp.sum(state[h][0], axis=1, keepdims=True)
            result = jnp.where(head_lanes((span, width), h, head_dim), state[h][1] / total, result)
            log_total = tops[h] + jnp.log(total)
            lse_ref[i, h : h + 1, :] = jnp.transpose(jnp.broadcast_to(log_total, (span, 128)))[
                0:1, :
            ]
        result_ref[i] = (result * scale_ref[...]).astype(BF16)
        return carry

    lax.fori_loop(0, blocks, query_block, 0)


def attend(order, offsets, slot, qkv, scale_lanes, heads, head_dim, at=0, count=1, into=None):
    group, _, span, width = qkv.shape
    length = group * span
    wide = max(span, min(512, length))
    held = [] if into is None else [into]
    return pl.pallas_call(
        functools.partial(attend_kernel, slot, heads, head_dim),
        grid=(1,),
        in_specs=[SMEM, SMEM, VMEM, VMEM] + [pl.BlockSpec(memory_space=pl.ANY)] * len(held),
        out_specs=[pl.BlockSpec((group, None, span, width), lambda i: (0, at, 0, 0)), VMEM],
        out_shape=[
            jax.ShapeDtypeStruct((group, count, span, width), BF16),
            jax.ShapeDtypeStruct((group, heads, span), F32),
        ],
        scratch_shapes=[pltpu.VMEM((heads, length // wide, span, wide), F32)],
        input_output_aliases={4: 0} if held else {},
        compiler_params=kernel_params(),
        cost_estimate=cost(0, 1024),
        name="attend",
    )(order, offsets, scale_lanes, qkv, *held)


def attend_back_kernel(slot, heads, head_dim, order_ref, offs_ref, *refs):
    attend_back_row(order_ref[slot], heads, head_dim, offs_ref, *refs)


def attend_back_row(
    row,
    heads,
    head_dim,
    offs_ref,
    inv_ref,
    lse_ref,
    held,
    grad_ref,
    out_ref,
    dqkv_ref,
    total_ref,
    q_ref,
    k_ref,
    g_ref,
    delta_ref,
    dq_ref,
):
    blocks, _, span, width = held.shape
    score_scale = head_dim ** (-0.5)
    picks = lax.broadcasted_iota(jnp.int32, (8, width), 0)
    lane = lax.broadcasted_iota(jnp.int32, (8, width), 1)
    ones = jnp.where(lane // head_dim == picks, 1.0, 0.0).astype(F32)

    def prepare(i, carry):
        queries = held[i, 0] * jnp.asarray(score_scale, BF16)
        keys = held[i, 1]
        grads = grad_ref[i]
        for h in range(heads):
            mine = head_lanes((span, width), h, head_dim)
            q_ref[h, i] = jnp.where(mine, queries, 0).astype(BF16)
            k_ref[h, i] = jnp.where(mine, keys, 0).astype(BF16)
            g_ref[h, i] = jnp.where(mine, grads, 0).astype(BF16)
        product = grads.astype(F32) * out_ref[i].astype(F32) * inv_ref[...]
        delta_ref[i] = lax.dot_general(
            ones, product, LAST, precision=lax.Precision.HIGHEST, preferred_element_type=F32
        )
        dq_ref[i] = jnp.zeros((span, width), F32)
        return carry + delta_ref[i]

    per = 2 if span * 2 <= 512 and blocks % 2 == 0 else 1
    wide = per * span
    total_ref[...] = lax.fori_loop(0, blocks, prepare, jnp.zeros((8, span), F32))

    def key_block(j, carry):
        keys = held[j, 1]
        values = held[j, 2]
        key_pos = j * span + lax.broadcasted_iota(jnp.int32, (span, 1), 0)
        last = (doc_end(offs_ref, row, (j + 1) * span - 1, blocks * span) - 1) // wide + 1

        def query_step(i, state):
            dk, dv = state
            query_pos = i * wide + lax.broadcasted_iota(jnp.int32, (1, wide), 1)
            query_start = doc_start(offs_ref, row, query_pos)
            allowed = (key_pos >= query_start) & (key_pos <= query_pos)
            at = pl.ds(i * per, per)
            dq = dq_ref[at].reshape(wide, width)
            for h in range(heads):
                queries = q_ref[h, at].reshape(wide, width)
                grads = g_ref[h, at].reshape(wide, width)
                log_total = jnp.concatenate(
                    [lse_ref[i * per + n, h : h + 1, :] for n in range(per)], axis=1
                )
                delta = jnp.concatenate(
                    [delta_ref[i * per + n, h : h + 1, :] for n in range(per)], axis=1
                )
                scores = dot_last(keys, queries)
                probs = jnp.exp(jnp.where(allowed, scores - log_total, MASKED))
                d_scores = (probs * (dot_last(values, grads) - delta)).astype(BF16)
                dv = dv + dot(probs.astype(BF16), grads)
                dk = dk + dot(d_scores, queries)
                dq = dq + dot_first(d_scores, k_ref[h, j])
            dq_ref[at] = dq.reshape(per, span, width)
            return (dk, dv)

        zero = jnp.zeros((span, width), F32)
        dk, dv = lax.fori_loop(j // per, last, query_step, (zero, zero))
        dqkv_ref[j, 1] = dk.astype(BF16)
        dqkv_ref[j, 2] = dv.astype(BF16)
        dqkv_ref[j, 0] = (dq_ref[j] * score_scale).astype(BF16)
        return carry

    lax.fori_loop(0, blocks, key_block, 0)


def attend_back(
    order, offsets, slot, qkv, grads, grads_at, scaled, scaled_at, inverse_lanes, lse, heads, head_dim
):
    group, _, span, width = qkv.shape

    def block_spec(at):
        return pl.BlockSpec((group, None, span, width), lambda i: (0, at, 0, 0))

    return pl.pallas_call(
        functools.partial(attend_back_kernel, slot, heads, head_dim),
        grid=(1,),
        in_specs=[SMEM, SMEM, VMEM, VMEM, VMEM, block_spec(grads_at), block_spec(scaled_at)],
        out_specs=[pl.BlockSpec((group, None, 3, span, width), lambda i: (0, 0, 0, 0, 0)), VMEM],
        out_shape=[
            jax.ShapeDtypeStruct((group, 1, 3, span, width), BF16),
            jax.ShapeDtypeStruct((8, span), F32),
        ],
        scratch_shapes=[pltpu.VMEM((heads, group, span, width), BF16)] * 3
        + [pltpu.VMEM((group, 8, span), F32), pltpu.VMEM((group, span, width), F32)],
        compiler_params=kernel_params(),
        cost_estimate=cost(0, 1024),
        name="attend_back",
    )(order, offsets, inverse_lanes, lse, qkv, grads, scaled)


def join_grads_kernel(parts, in_ref, out_ref, value_ref):
    group = in_ref.shape[0]
    for n in range(3):
        whole = jnp.concatenate([in_ref[s, 0, n] for s in range(group)], axis=1)
        piece = whole.shape[1] // parts
        if n == 2:
            value_ref[...] = whole
            continue
        for p in range(parts):
            to = (p * 2 + n) * piece
            out_ref[:, to : to + piece] = whole[:, p * piece : (p + 1) * piece]


def join_grads(block):
    group, _, _, span, width = block.shape
    return pl.pallas_call(
        functools.partial(join_grads_kernel, PARTS),
        out_shape=[
            jax.ShapeDtypeStruct((span, 2 * group * width), BF16),
            jax.ShapeDtypeStruct((span, group * width), BF16),
        ],
        compiler_params=kernel_params(),
        cost_estimate=cost(0, 1024),
        name="join_grads",
    )(block)


FF_STEP = 1024
LAYER_VMEM = 62 * 1024 * 1024


def layer_kernel(
    slots,
    order_ref,
    post_ref,
    ffn_ref,
    mid_gain_ref,
    scale_ref,
    w_out_ref,
    x_hbm,
    d_out_hbm,
    d_mid_hbm,
    w_fc1_hbm,
    *refs,
):
    count = len(slots)
    o_refs = refs[:count]
    (
        scaled_ref,
        ffn_in_ref,
        residual_ref,
        mid_ref,
        d_pre_ref,
        d_proj_ref,
        d_residual_ref,
        d_attn_ref,
        g_post_ref,
        g_ffn_ref,
        g_mid_ref,
        x_ref,
        d_out_ref,
        d_mid_ref,
        w_fc1_ref,
        act_ref,
        slope_ref,
        sems,
        row_sems,
    ) = refs[count:]
    group, _, span, width = o_refs[0].shape
    tokens, hidden = act_ref.shape
    step = FF_STEP // count
    steps = [slice(c, c + step) for c in range(0, hidden, step)]
    weight_copies = [
        pltpu.make_async_copy(
            w_fc1_hbm.at[:, c : c + FF_STEP], w_fc1_ref.at[:, c : c + FF_STEP], sems.at[n]
        )
        for n, c in enumerate(range(0, hidden, FF_STEP))
    ]
    x_copies, mid_copies = [], []
    for n, slot in enumerate(slots):
        row = order_ref[slot]
        to = slice(n * span, (n + 1) * span)
        x_copies.append(pltpu.make_async_copy(x_hbm.at[row], x_ref.at[to], row_sems.at[0, n]))
        x_copies.append(
            pltpu.make_async_copy(d_out_hbm.at[row], d_out_ref.at[to], row_sems.at[1, n])
        )
        rows = pl.ds(pl.multiple_of(row * span, span), span)
        mid_copies.append(
            pltpu.make_async_copy(d_mid_hbm.at[rows], d_mid_ref.at[to], row_sems.at[2, n])
        )
    for copy in x_copies + weight_copies + mid_copies:
        copy.start()

    for n in range(count):
        for s in range(group):
            scaled_ref[n * span : (n + 1) * span, s * width : (s + 1) * width] = o_refs[n][s, 0]
    proj_hat, proj_spread = norm_parts(dot(scaled_ref[...], w_out_ref[...]))
    for copy in x_copies:
        copy.wait()
    residual = x_ref[...].astype(F32) + proj_hat * post_ref[...]
    residual_ref[...] = residual
    res_hat, res_spread = norm_parts(residual)
    ffn_in = (res_hat * ffn_ref[...]).astype(BF16)
    ffn_in_ref[...] = ffn_in

    total = jnp.zeros((tokens, 1), F32)
    for n, at in enumerate(steps):
        if n % count == 0:
            weight_copies[n // count].wait()
        pre = dot(ffn_in, w_fc1_ref[:, at])
        phi = 0.5 + 0.5 * lax.erf(pre * (0.5**0.5))
        act = pre * phi
        act_ref[:, at] = act
        slope = phi + pre * jnp.exp(-0.5 * pre * pre) * 0.3989422804014327
        slope_ref[:, at] = slope.astype(slope_ref.dtype)
        total += jnp.sum(act, axis=1, keepdims=True)
    average = total / hidden
    total = jnp.zeros((tokens, 1), F32)
    for at in steps:
        centred = act_ref[:, at] - average
        total += jnp.sum(centred * centred, axis=1, keepdims=True)
    spread = lax.rsqrt(total / hidden + EPSILON)

    for copy in mid_copies:
        copy.wait()
    sum_weighted = jnp.zeros((tokens, 1), F32)
    sum_hat = jnp.zeros((tokens, 1), F32)
    for at in steps:
        hat = (act_ref[:, at] - average) * spread
        act_ref[:, at] = hat
        gain = mid_gain_ref[:, at]
        mid_ref[:, at] = (hat * gain).astype(BF16)
        grad = d_mid_ref[:, at]
        product = grad * hat
        g_mid_ref[:, at] = jnp.sum(product, axis=0, keepdims=True)
        sum_weighted += jnp.sum(grad * gain, axis=1, keepdims=True)
        sum_hat += jnp.sum(product * gain, axis=1, keepdims=True)
    sum_weighted = sum_weighted / hidden
    sum_hat = sum_hat / hidden
    d_ffn = jnp.zeros(x_ref.shape, F32)
    for at in steps:
        weighted = d_mid_ref[:, at] * mid_gain_ref[:, at]
        d_act = spread * (weighted - sum_weighted - act_ref[:, at] * sum_hat)
        d_pre = (d_act * slope_ref[:, at].astype(F32)).astype(BF16)
        d_pre_ref[:, at] = d_pre
        d_ffn += dot_last(d_pre, w_fc1_ref[:, at])

    g_ffn_ref[...] = jnp.sum(d_ffn * res_hat, axis=0, keepdims=True)
    d_residual = d_out_ref[...].astype(F32) + norm_back(res_hat, res_spread, ffn_ref[...], d_ffn)
    d_residual_ref[...] = d_residual
    g_post_ref[...] = jnp.sum(d_residual * proj_hat, axis=0, keepdims=True)
    d_proj = norm_back(proj_hat, proj_spread, post_ref[...], d_residual).astype(BF16)
    d_proj_ref[...] = d_proj
    d_attn = (dot_last(d_proj, w_out_ref[...]) * scale_ref[...]).astype(BF16)
    for n in range(count):
        for s in range(group):
            d_attn_ref[s, n] = d_attn[n * span : (n + 1) * span, s * width : (s + 1) * width]


def layer(order, slots, blocks, x, d_out, gains, w_out, d_mid, w_fc1):
    group, _, span, width = blocks[0][0].shape
    model, hidden = w_fc1.shape
    tokens = len(slots) * span
    shape = jax.ShapeDtypeStruct

    def block_spec(at):
        return pl.BlockSpec((group, 1, span, width), lambda i, o: (0, at, 0, 0))

    return pl.pallas_call(
        functools.partial(layer_kernel, slots),
        grid_spec=pltpu.PrefetchScalarGridSpec(
            num_scalar_prefetch=1,
            grid=(1,),
            in_specs=[VMEM] * 5
            + [pl.BlockSpec(memory_space=pl.ANY)] * 4
            + [block_spec(at) for _, at in blocks],
            out_specs=[VMEM] * 11,
            scratch_shapes=[
                pltpu.VMEM((tokens, model), BF16),
                pltpu.VMEM((tokens, model), BF16),
                pltpu.VMEM((tokens, hidden), d_mid.dtype),
                pltpu.VMEM(w_fc1.shape, BF16),
                pltpu.VMEM((tokens, hidden), F32),
                pltpu.VMEM((tokens, hidden), F32 if len(slots) == 1 else BF16),
                pltpu.SemaphoreType.DMA((hidden // FF_STEP,)),
                pltpu.SemaphoreType.DMA((3, len(slots))),
            ],
        ),
        out_shape=[
            shape((tokens, model), BF16),
            shape((tokens, model), BF16),
            shape((tokens, model), F32),
            shape((tokens, hidden), BF16),
            shape((tokens, hidden), BF16),
            shape((tokens, model), BF16),
            shape((tokens, model), F32),
            shape((group, len(slots), span, width), BF16),
            shape((1, model), F32),
            shape((1, model), F32),
            shape((1, hidden), F32),
        ],
        compiler_params=pltpu.CompilerParams(vmem_limit_bytes=LAYER_VMEM),
        cost_estimate=cost(0, 1024),
        name="layer",
    )(order, *gains, w_out, x, d_out, d_mid, w_fc1, *[block for block, _ in blocks])


def layer_out_kernel(order_ref, *refs):
    count = (len(refs) - 2) // 2
    weight, out_ref = refs[-2], refs[-1]
    span, slot = out_ref.shape[1], 0
    for n in range(count):
        result = (refs[n][...] + dot(refs[count + n][...], weight[...])).astype(BF16)
        for at in range(0, result.shape[0], span):
            out_ref[order_ref[slot]] = result[at : at + span]
            slot += 1


def last_step(order, shape, residuals, mids, w_fc2):
    return pl.pallas_call(
        layer_out_kernel,
        in_specs=[SMEM] + [VMEM] * (2 * len(mids) + 1),
        out_shape=jax.ShapeDtypeStruct(shape, BF16),
        compiler_params=kernel_params(),
        cost_estimate=cost(0, 1024),
        name="layer_out",
    )(order, *residuals, *mids, w_fc2)


def flip(value, axis, bit):
    size = lax.axis_size(axis)
    return lax.ppermute(value, axis, [(i, i ^ (1 << bit)) for i in range(size)])


def bits(axis):
    return (lax.axis_size(axis) - 1).bit_length()


PARTS = 4


def weight_kernel(count, rows, added, shards, part_ref, *refs):
    out_ref = refs[-1]
    high = out_ref.shape[1]
    per = rows * (shards + 1)
    extras = refs[per * count : per * count + added]
    at = 0
    for n in range(count):
        mine = refs[n * per : (n + 1) * per]
        rights = mine[rows * shards :]
        width = rights[0].shape[1]
        total = 0.0
        for r in range(rows):
            left = [ref[...] for ref in mine[r * shards : (r + 1) * shards]]
            left = jnp.concatenate(left, axis=1) if shards > 1 else left[0]
            total += dot_first(left, rights[r][...])
        for i in range(shards):
            piece = total[i * high : (i + 1) * high]
            for extra in extras:
                piece = piece + extra[i, :, at : at + width].astype(F32)
            out_ref[i, :, at : at + width] = piece.astype(BF16)
        at += width


def weight_part_plain(pairs, part, parts, extras, group):
    pieces = []
    for lefts, rights, kind in pairs:
        left, right = jnp.concatenate(lefts), jnp.concatenate(rights)
        if kind == "columns":
            wide = right.shape[1] // parts
            right = lax.dynamic_slice(right, (0, part * wide), (right.shape[0], wide))
            left = left.reshape(left.shape[0], group, -1)
        else:
            left = left.reshape(left.shape[0], group, parts, -1)
            left = lax.dynamic_index_in_dim(left, part, 2, keepdims=False)
        pieces.append(jnp.einsum("tsd,te->sde", left, right, preferred_element_type=F32))
    total = jnp.concatenate(pieces, axis=2)
    axis = 2 if pairs[0][2] == "columns" else 1
    for extra, at in extras:
        size = total.shape[axis]
        total = total + lax.dynamic_slice_in_dim(extra, at * size, size, axis).astype(F32)
    return total.astype(BF16)


def weight_part(pairs, part, parts, extras, group):
    shards = 2
    specs, arrays, width = [], [], 0
    for lefts, rights, kind in pairs:
        model = lefts[0].shape[1]
        stride = 1 if kind == "columns" else parts
        high = model // group // stride
        wide = rights[0].shape[1] // (parts if kind == "columns" else 1)
        for left in lefts:
            for i in range(shards):

                def left_at(g, p, i=i, stride=stride):
                    return (0, (g * shards + i) * stride + (p[0] if stride > 1 else 0))

                specs.append(pl.BlockSpec((left.shape[0], high), left_at))
                arrays.append(left)
        for right in rights:

            def right_at(g, p, stride=stride):
                return (0, p[0] if stride == 1 else 0)

            specs.append(pl.BlockSpec((right.shape[0], wide), right_at))
            arrays.append(right)
        width += wide
    if high % 128:
        return weight_part_plain(pairs, part, parts, extras, group)
    block = pl.BlockSpec((shards, high, width), lambda g, p: (g, 0, 0))
    by_row = pairs[0][2] == "rows"

    def extra_spec(n):
        def block_at(g, p):
            return (g, p[n], 0) if by_row else (g, 0, p[n])

        return pl.BlockSpec((shards, high, width), block_at)

    numbers = jnp.stack([part] + [at for _, at in extras]).astype(jnp.int32)
    return pl.pallas_call(
        functools.partial(weight_kernel, len(pairs), len(pairs[0][0]), len(extras), shards),
        grid_spec=pltpu.PrefetchScalarGridSpec(
            num_scalar_prefetch=1,
            grid=(group // shards,),
            in_specs=specs + [extra_spec(n + 1) for n in range(len(extras))],
            out_specs=block,
        ),
        out_shape=jax.ShapeDtypeStruct((group, high, width), BF16),
        compiler_params=kernel_params(),
        cost_estimate=cost(0, 1024),
        name="weight_part",
    )(numbers, *arrays, *[extra for extra, _ in extras])


class WeightSum:
    def __init__(self, *pairs):
        self.pairs = pairs
        batch_at = lax.axis_index("batch")
        self.near, self.far = batch_at & 1, (batch_at >> 1) & 1
        self.zero = batch_at * 0

    def piece(self, order, near, far, *extras):
        def part_of(part):
            return weight_part(self.pairs, part, PARTS, extras, lax.axis_size("blk"))

        return order(part_of, near * 2 + far)

    def half(self, order, near, *extras):
        def part_of(part):
            return weight_part(self.pairs, part, 2, extras, lax.axis_size("blk"))

        return order(part_of, near)

    def away_far(self, order):
        return self.piece(order, 1 - self.near, 1 - self.far)

    def away_near(self, order):
        return self.piece(order, 1 - self.near, self.far)

    def away(self, order, *more):
        return self.half(order, 1 - self.near, *more)

    def send_far(self, order, away):
        return self.piece(order, self.near, 1 - self.far, (away, self.zero))

    def send(self, order, *aways):
        extras = [(away, 1 - self.far) for away in aways]
        return self.piece(order, self.near, 1 - self.far, *extras)

    def keep(self, order, near, arrived):
        return self.piece(order, self.near, self.far, (near, self.zero), (arrived, self.zero))

    def keep_rest(self, order, arrived, *aways):
        extras = [(away, self.far) for away in aways]
        return self.piece(order, self.near, self.far, (arrived, self.zero), *extras)

    def own(self, order, *aways):
        return self.half(order, self.near, *[(away, self.zero) for away in aways])


def over_near(sent):
    return flip(sent, "batch", 0)


def over_far(sent):
    return flip(sent, "batch", 1)


class Order:
    def __init__(self):
        self.last = ()

    def __call__(self, step, *values):
        self.last = step(*tie(values, self.last))
        return self.last


def window(always, step):
    def nothing():
        return jax.tree.map(lambda leaf: jnp.zeros(leaf.shape, leaf.dtype), jax.eval_shape(step))

    return lax.cond(always, step, nothing)


def tie(values, *after):
    return lax.optimization_barrier((values, after))[0]


def combine_kernel(plan, at_ref, *refs):
    ins = sum(count for _, count, _ in plan)
    into, out_of = list(refs[:ins]), list(refs[ins:])
    for n, (kind, count, cut) in enumerate(plan):
        terms = [into.pop(0) for _ in range(count)]
        if kind == "small":
            out_of.pop(0)[...] = sum(term[...] for term in terms)
            continue
        if kind == "stack":
            out = out_of.pop(0)
            out[0], out[1] = terms[0][0], terms[1][0]
            continue

        def put(ref, j, i):
            at, each = 0, 2 if kind == "add" else 1
            for m in range(0, len(terms), each):
                to = slice(at, at + terms[m].shape[2])
                if kind == "add":
                    total = terms[m][i].astype(F32) + terms[m + 1][i].astype(F32)
                    ref[j, :, to] = total.astype(BF16)
                else:
                    ref[j, :, to] = terms[m][i]
                at = to.stop

        if cut:
            keep, send = out_of.pop(0), out_of.pop(0)
            for j in range(keep.shape[0]):
                put(keep, j, 2 * j + at_ref[n])
                put(send, j, 2 * j + 1 - at_ref[n])
        else:
            whole = out_of.pop(0)
            for j in range(whole.shape[0]):
                put(whole, j, j)


class Tree:
    def __init__(self, *mine, halved=2):
        self.steps = [("blk", bit) for bit in range(bits("blk"))]
        self.steps += [("batch", bit) for bit in range(halved, bits("batch"))]
        self.steps += [("far", 1), ("near", 0)][2 - halved :]
        self.terms, self.last = list(mine), "first"

    def start(self):
        kind, bit = self.steps[0]
        return flip(self.send, "blk" if kind == "blk" else "batch", bit)

    def end(self, arrived):
        self.last = self.steps.pop(0)[0]
        self.terms = [self.kept, arrived]


def combine(trees):
    me = lax.axis_index("blk")
    plan, ins, shapes, at = [], [], [], []
    for tree in trees:
        kind, bit = tree.steps[0]
        cut = kind == "blk" and tree.last != "small"
        if tree.last == "small":
            plan.append(("small", len(tree.terms), False))
            ins += tree.terms
            shapes.append(jax.ShapeDtypeStruct(tree.terms[0].shape, F32))
            at.append(me * 0)
            continue
        state = {"first": "first", "far": "stack"}.get(tree.last, "add")
        plan.append((state, len(tree.terms), cut))
        ins += tree.terms
        count, high, wide = tree.terms[0].shape
        if state != "stack":
            each = 1 if state == "first" else 2
            wide = sum(term.shape[2] for term in tree.terms[::each])
        count = count // 2 if cut else 2 if state == "stack" else count
        shapes += [jax.ShapeDtypeStruct((count, high, wide), BF16)] * (2 if cut else 1)
        at.append((me >> bit) & 1 if cut else me * 0)
    outs = list(
        pl.pallas_call(
            functools.partial(combine_kernel, plan),
            in_specs=[SMEM] + [VMEM] * len(ins),
            out_shape=shapes,
            compiler_params=kernel_params(),
            cost_estimate=cost(0, 1024),
            name="combine",
        )(jnp.stack(at).astype(jnp.int32), *ins)
    )
    for tree, (_, _, cut) in zip(trees, plan):
        tree.kept = outs.pop(0)
        tree.send = outs.pop(0) if cut else tree.kept


def place_kernel(layout, lines, part_ref, *refs):
    count = 2 * len(layout) + (2 if lines else 0)
    ins, outs = list(refs[:count]), list(refs[count:])
    if lines:
        one, other = ins[-2:]
        for (start, size, cut), out in zip(lines, outs[-len(lines) :]):
            at = pl.ds(start, size)
            if cut:
                at = pl.ds(pl.multiple_of(start + part_ref[2] * size, 128), size)
            out[...] = one[:, at] + other[:, at]
    near, far = part_ref[0], part_ref[1]
    order = [near * 2 + far, near * 2 + 1 - far, (1 - near) * 2 + far, (1 - near) * 2 + 1 - far]
    for spans in layout:
        both = [ins.pop(0), ins.pop(0)]
        count = 2 * both[0].shape[0]
        for start, width, kind in spans:
            out = outs.pop(0)
            for n, part in enumerate(order if count == 4 else [near, 1 - near]):
                value = both[n * 2 // count][n % (count // 2), :, start : start + width]
                value = value.astype(F32)
                if kind == "columns":
                    out[:, pl.ds(pl.multiple_of(part * width, 128), width)] = value
                else:
                    high = value.shape[0]
                    out[pl.ds(pl.multiple_of(part * high, 8), high), :] = value


def place(trees, layout, small=None, lines=()):
    batch_at = lax.axis_index("batch")
    parts = jnp.stack([batch_at & 1, (batch_at >> 1) & 1, lax.axis_index("blk")])
    parts = parts.astype(jnp.int32)
    ins, shapes = [], []
    for tree, spans in zip(trees, layout):
        ins += tree.terms
        count, high = 2 * tree.kept.shape[0], tree.kept.shape[1]
        for _, width, kind in spans:
            shape = (high, count * width) if kind == "columns" else (count * high, width)
            shapes.append(jax.ShapeDtypeStruct(shape, F32))
    if lines:
        ins += small.terms
        shapes += [jax.ShapeDtypeStruct((1, size), F32) for _, size, _ in lines]
    return pl.pallas_call(
        functools.partial(place_kernel, layout, lines),
        in_specs=[SMEM] + [VMEM] * len(ins),
        out_shape=shapes,
        compiler_params=kernel_params(),
        cost_estimate=cost(0, 1024),
        name="place",
    )(parts, *ins)


class SmallSum:
    def __init__(self, mine):
        self.steps = [("batch", bit) for bit in range(bits("batch"))]
        self.steps += [("blk", bit) for bit in range(bits("blk"))]
        self.terms, self.last = [mine], "small"

    def start(self):
        return flip(self.send, *self.steps[0])

    def end(self, arrived):
        self.steps.pop(0)
        self.terms = [self.kept, arrived]


def input_grad_kernel(slots, parts, order_ref, gain_ref, x_hbm, *refs):
    wq_ref, wk_ref, wv_ref = refs[:3]
    count = len(slots)
    d_refs, value_refs, res_refs = refs[3 : 3 + count], refs[3 + count : 3 + 2 * count], refs[3 + 2 * count : -4]
    out_ref, sum_ref, x_ref, sems = refs[-4:]
    span, model = x_ref.shape[1:]
    piece = model // parts
    copies = [
        pltpu.make_async_copy(x_hbm.at[order_ref[slot]], x_ref.at[n], sems.at[n])
        for n, slot in enumerate(slots)
    ]
    for copy in copies:
        copy.start()
    residuals = [held.at[pl.ds(at, span)] for held in res_refs for at in range(0, held.shape[0], span)]
    residuals = residuals[-count:] if slots[0] else residuals[:count]
    for copy in copies:
        copy.wait()
    total = jnp.zeros(sum_ref.shape, F32)
    for n in range(count):
        grad = dot_last(value_refs[n][...], wv_ref[...])
        for p in range(parts):
            for m, weight in enumerate((wq_ref, wk_ref)):
                at = (p * 2 + m) * piece
                grad += dot_last(d_refs[n][:, at : at + piece], weight[:, p * piece : (p + 1) * piece])
        hat, spread = norm_parts(x_ref[n].astype(F32))
        out_ref[n] = residuals[n][...] + norm_back(hat, spread, gain_ref[...], grad)
        total += jnp.sum(grad * hat, axis=0, keepdims=True)
    sum_ref[...] = total


def input_grad(order, slots, x, gain, weights, d_rows, d_values, d_residuals):
    _, span, model = x.shape
    count = len(slots)
    return pl.pallas_call(
        functools.partial(input_grad_kernel, slots, PARTS),
        in_specs=[SMEM, VMEM, pl.BlockSpec(memory_space=pl.ANY)]
        + [VMEM] * (3 + 2 * count + len(d_residuals)),
        out_shape=[
            jax.ShapeDtypeStruct((count, span, model), F32),
            jax.ShapeDtypeStruct((1, model), F32),
        ],
        scratch_shapes=[
            pltpu.VMEM((count, span, model), BF16),
            pltpu.SemaphoreType.DMA((count,)),
        ],
        compiler_params=kernel_params(),
        cost_estimate=cost(0, 1024),
        name="input_grad",
    )(order, gain, x, *weights, *d_rows, *d_values, *d_residuals)


def in_place_kernel(order_ref, *refs):
    *ins, out_ref, sems = refs
    copies, slot = [], 0
    for part in ins:
        for n in range(part.shape[0]):
            copies.append(
                pltpu.make_async_copy(part.at[n], out_ref.at[order_ref[slot]], sems.at[slot])
            )
            slot += 1
    for copy in copies:
        copy.start()
    for copy in copies:
        copy.wait()


def in_place(order, parts):
    rows = order.shape[0]
    return pl.pallas_call(
        in_place_kernel,
        in_specs=[SMEM] + [pl.BlockSpec(memory_space=pl.ANY)] * len(parts),
        out_specs=pl.BlockSpec(memory_space=pl.ANY),
        out_shape=jax.ShapeDtypeStruct((rows, *parts[0].shape[1:]), parts[0].dtype),
        scratch_shapes=[pltpu.SemaphoreType.DMA((rows,))],
        compiler_params=kernel_params(),
        cost_estimate=cost(0, 1024),
        name="in_place",
    )(order, *parts)


def on_device(
    inputs,
    ln_attn,
    w_query,
    w_key,
    w_value,
    w_out,
    head_scale,
    ln_post,
    ln_ffn,
    w_fc1,
    ln_mid,
    w_fc2,
    offsets,
    cotangent,
):
    row_count, span, model = inputs.shape
    head_count = head_scale.shape[0]
    head_dim = model // head_count
    tokens = row_count * span
    group = lax.axis_size("blk")
    heads = head_count // group
    width = heads * head_dim
    my_index = lax.axis_index("blk")
    rows = range(row_count)

    always = offsets[0, 0] == 0
    gain = ln_attn.reshape(1, model)
    last = row_count - 1
    my_scale = lax.dynamic_slice(head_scale, (my_index * heads,), (heads,))
    scale_lanes = jnp.repeat(my_scale, head_dim).reshape(1, width)
    layer_gains = [
        ln_post.reshape(1, model),
        ln_ffn.reshape(1, model),
        ln_mid.reshape(1, -1),
        jnp.repeat(head_scale, head_dim).reshape(1, model),
    ]

    def project_row(r, x):
        return project(offsets, r, x, gain, w_query, w_key, w_value, group)

    def attend_one(r, held, into=None):
        place = (r, last) if r < last else (0, 1)
        return attend(by_work, offsets, r, held, scale_lanes, heads, head_dim, *place, into)

    def layer_rows(slots, blocks):
        return layer(by_work, slots, blocks, inputs, cotangent, layer_gains, w_out, d_mid, w_fc1)

    def back(order, r, row_heads, at=0):
        def back_row(held):
            return attend_back(
                by_work,
                offsets,
                r,
                held,
                row_heads,
                at,
                *((first_out, r) if r < last else (last_out, 0)),
                1.0 / scale_lanes,
                lse[r],
                heads,
                head_dim,
            )

        return order(back_row, qkv[r])

    def first_window():
        order = Order()
        return exchange(sent), [
            order(functools.partial(project_row, r), inputs) for r in rows[1:]
        ]

    normed_first, sent, by_work = project_row(0, inputs)
    held, projected = first_window()
    qkv = [held]
    normed = [normed_first] + [part[0] for part in projected]
    first_out, lse = None, []
    for r in rows[1:]:

        def next_window():
            order = Order()
            extra = ()
            if r == 1:
                d_mid = jnp.einsum(
                    "td,fd->tf",
                    cotangent.reshape(tokens, model),
                    w_fc2,
                    preferred_element_type=F32,
                )
                extra = d_mid
            if r == last:
                d_out = [
                    lax.dynamic_index_in_dim(cotangent, by_work[n], keepdims=False) for n in rows
                ]
                extra = d_out[0], jnp.concatenate(d_out[1:])
            return exchange(projected[r - 1][1]), attend_one(r - 1, qkv[r - 1], first_out), extra

        held, (first_out, log_total), extra = window(always, next_window)
        d_mid = extra if r == 1 else d_mid
        qkv.append(held)
        lse.append(log_total)

    d_out = list(extra)

    def early_window():
        return (
            exchange(first_out),
            attend_one(last, qkv[last]),
        )

    early, (last_out, log_total) = window(always, early_window)
    lse.append(log_total)

    def late_window():
        return exchange(last_out), layer_rows([0], [(early, 0)])

    late, layer_first = window(always, late_window)

    def layer_window():
        blocks = [(early, r) if r < last else (late, 0) for r in rows[1:]]
        return exchange(layer_first[7]), layer_rows(list(rows[1:]), blocks)

    first_heads, layer_rest = window(always, layer_window)
    (
        scaled,
        ffn_in,
        residual,
        mid,
        d_pre,
        d_proj,
        d_residual,
        d_attn,
        g_post,
        g_ffn,
        g_mid,
    ) = zip(layer_first, layer_rest)
    sum_one = WeightSum((mid, d_out, "rows"))
    sum_two = WeightSum((ffn_in, d_pre, "columns"))
    sum_three = WeightSum((scaled, d_proj, "columns"))
    order = Order()
    away_one = over_near(sum_one.away_far(order))
    near_one = over_near(sum_one.away_near(order))
    far_one = over_far(sum_one.send_far(order, away_one))

    def back_first():
        order = Order()
        heads_in = exchange(d_attn[1])
        away = over_near(sum_two.away_far(order))
        out = back(order, 0, first_heads)
        return heads_in, out, sum_two.send_far(order, away)

    rest_heads, (sent, total), sent_two = window(always, back_first)
    far_two = over_far(sent_two)
    totals = [total]

    def back_second():
        order = Order()
        grad = exchange(sent)
        out = back(order, 1, rest_heads, 0)
        near = sum_two.away_near(order), sum_three.away(order)
        return grad, out, near, sum_one.keep(order, near_one, far_one)

    grad, (sent, total), near, mine_one = window(always, back_second)
    near_two, away_three = near
    totals.append(total)
    grads = [grad]
    tree_one = Tree(mine_one)
    combine([tree_one])
    moved = tree_one.start()
    sent = tie(sent, tree_one.send)
    near_two, away_three = over_near(near_two), over_near(away_three)
    for r in rows[2:]:

        def back_next():
            order = Order()
            out_of = ()
            grad = exchange(sent)
            out = back(order, r, rest_heads, r - 1)
            if r == 2:
                mine = sum_two.keep(order, near_two, far_two)
                out_of = mine, sum_three.own(order, away_three)
            return grad, out_of, out

        grad, out_of, (sent, total) = window(always, back_next)
        totals.append(total)
        grads.append(grad)
        if r == 2:
            mine_two, mine_three = out_of
    tree_one.end(moved)
    tree_two = Tree(mine_two)
    tree_three = Tree(mine_three, halved=1)
    combine([tree_one, tree_two, tree_three])
    moved = tree_one.start(), tree_two.start()
    moved_three = tree_three.start()
    sent = tie(sent, tree_one.send, tree_two.send)

    def back_last():
        order = Order()
        grad = exchange(sent)
        joined = [order(join_grads, part) for part in grads]
        d_rows, d_values = zip(*joined)
        early_qk = WeightSum((normed[:last], d_rows, "columns"))
        early_v = WeightSum((normed[:last], d_values, "columns"))
        early = [early_qk.away(order), early_v.away(order), early_qk.own(order), early_v.own(order)]
        part = order(
            lambda x: input_grad(
                by_work,
                list(rows[:last]),
                x,
                gain,
                (w_query, w_key, w_value),
                d_rows,
                d_values,
                d_residual,
            ),
            inputs,
        )
        return grad, joined, part, early

    grad, joined, part, early_sums = window(always, back_last)
    early_grads, early_gain = part
    early_away_qk, early_away_v, early_qk, early_v = early_sums
    grad, moved = tie((grad, moved))
    tree_one.end(moved[0])
    tree_two.end(moved[1])
    order = Order()
    joined = joined + [order(join_grads, grad)]
    d_rows, d_values = zip(*joined)
    sum_qk = WeightSum((normed[last:], d_rows[last:], "columns"))
    sum_v = WeightSum((normed[last:], d_values[last:], "columns"))
    away_qk = over_near(sum_qk.away(order, (early_away_qk, sum_qk.zero)))
    away_v = over_near(sum_v.away(order, (early_away_v, sum_v.zero)))
    sent_qk = sum_qk.send(order, away_qk, early_qk)
    far_qk = over_far(sent_qk)
    for tree in (tree_one, tree_two):
        tree.terms = list(tie(tree.terms, sent_qk))
    combine([tree_one, tree_two])
    moved = tree_one.start(), tree_two.start()
    away_v = tie(away_v, tree_one.send, tree_two.send)

    def advance(trees, extra=lambda: ()):
        def step():
            return [tree.start() for tree in trees], extra()

        moved, out = window(always, step)
        for tree, arrived in zip(trees, moved):
            tree.end(arrived)
        return out

    def beside():
        order = Order()
        tree = Tree(sum_v.own(order, away_v, early_v), halved=1)
        combine([tree])

        def input_step(x):
            return input_grad(
                by_work,
                [last],
                x,
                gain,
                (w_query, w_key, w_value),
                d_rows[last:],
                d_values[last:],
                d_residual,
            )

        return tree.kept, tree.start(), order(input_step, inputs)

    kept, arrived, (late_grads, late_gain) = window(always, beside)
    moved, arrived = tie((moved, arrived))
    tree_one.end(moved[0])
    tree_two.end(moved[1])
    grad_ln_attn = early_gain + late_gain
    tree_v = Tree(halved=1)
    tree_v.kept = kept
    tree_v.end(arrived)
    tree_v.terms += [tree_three.kept, moved_three]
    tree_qk = Tree(sum_qk.keep_rest(order, far_qk, away_qk, early_qk))
    delta_sum = sum(jnp.sum(total, axis=1) for total in totals)
    my_grad = delta_sum[:heads] / my_scale
    scale_part = lax.dynamic_update_slice(
        jnp.zeros((head_count,), F32), my_grad, (my_index * heads,)
    )
    small = SmallSum(
        jnp.concatenate(
            [grad_ln_attn[0], sum(g_post)[0], sum(g_ffn)[0], sum(g_mid)[0], scale_part]
        ).reshape(1, -1)
    )
    piece = model // PARTS
    ff_piece = w_fc1.shape[1] // PARTS
    trees = [tree_qk, tree_v, tree_two, tree_one]
    placed = layer_out = grad_inputs = None
    while any(tree.steps for tree in trees + [small]):
        combine([tree for tree in trees + [small] if tree.steps])

        def beside_step():
            if layer_out is None:
                order = Order()

                def output_step(weight):
                    return last_step(by_work, inputs.shape, residual, mid, weight)

                return order(output_step, w_fc2)
            if grad_inputs is None:
                return in_place(by_work, [early_grads, late_grads])
            if tree_two.steps or tree_one.steps or placed is not None:
                return ()
            return place(
                [tree_one, tree_two], [[(0, model, "rows")], [(0, ff_piece, "columns")]]
            )

        beside_out = advance([tree for tree in trees + [small] if tree.steps], beside_step)
        if layer_out is None:
            layer_out = beside_out
        elif grad_inputs is None:
            grad_inputs = beside_out
        else:
            placed = beside_out or placed
    if placed is None:
        placed = place([tree_one, tree_two], [[(0, model, "rows")], [(0, ff_piece, "columns")]])
    grad_fc2, grad_fc1 = placed
    lines = [(0, model), (model, model), (2 * model, model), (3 * model, ln_mid.shape[0])]
    ends = lines[-1][0] + lines[-1][1]
    layout = [
        [(n * piece, piece, "columns") for n in range(2)],
        [(n * 2 * piece, 2 * piece, "columns") for n in range(2)],
    ]
    if model // group % 128:
        grad_query, grad_key, grad_value, grad_out = place([tree_qk, tree_v], layout)
        total = sum(small.terms)[0]
        gains = [
            lax.dynamic_slice(total, (start + my_index * (size // group),), (size // group,))
            for start, size in lines
        ]
        gains.append(total[ends:])
    else:
        lines = [(start, size // group, True) for start, size in lines]
        lines.append((ends, head_count, False))
        grad_query, grad_key, grad_value, grad_out, *gains = place(
            [tree_qk, tree_v], layout, small, lines
        )
        gains = [line[0] for line in gains]
    return (
        layer_out,
        grad_inputs,
        gains[0],
        grad_query,
        grad_key,
        grad_value,
        grad_out,
        gains[4],
        gains[1],
        gains[2],
        grad_fc1,
        gains[3],
        grad_fc2,
    )


def solution(mesh):
    rows = P("batch", "blk", None)
    shard = P("blk", None)
    return jax.shard_map(
        on_device,
        mesh=mesh,
        in_specs=(rows,) + (P(),) * 11 + (P("batch", None), rows),
        out_specs=(
            rows,
            rows,
            P("blk"),
            shard,
            shard,
            shard,
            shard,
            P(),
            P("blk"),
            P("blk"),
            shard,
            P("blk"),
            shard,
        ),
        check_vma=False,
    )
```

```python
import functools

import jax
import jax.numpy as jnp
from jax import lax
from jax.experimental import pallas as pl
from jax.experimental.pallas import tpu as pltpu
from jax.sharding import PartitionSpec as P

EPSILON = 1e-05
MASKED = -1e30
VMEM_BYTES = 50 * 1024 * 1024
F32 = jnp.float32
BF16 = jnp.bfloat16
LAST = (((1,), (1,)), ((), ()))
FIRST = (((0,), (0,)), ((), ()))
SMEM = pl.BlockSpec(memory_space=pltpu.SMEM)
VMEM = pl.BlockSpec(memory_space=pltpu.VMEM)


def dot_last(left, right):
    return lax.dot_general(left, right, LAST, preferred_element_type=F32)


def dot_first(left, right):
    return lax.dot_general(left, right, FIRST, preferred_element_type=F32)


def dot(left, right):
    return jnp.dot(left, right, preferred_element_type=F32)


def kernel_params():
    return pltpu.CompilerParams(vmem_limit_bytes=VMEM_BYTES)


def cost(flops, size):
    return pl.CostEstimate(flops=int(flops), bytes_accessed=int(size), transcendentals=0)


def exchange(parts):
    return lax.all_to_all(parts, "blk", 0, 0, tiled=True)


def norm_parts(rows_in):
    average = jnp.mean(rows_in, axis=-1, keepdims=True)
    centred = rows_in - average
    spread = lax.rsqrt(jnp.mean(centred * centred, axis=-1, keepdims=True) + EPSILON)
    return centred * spread, spread


def norm_back(hat, spread, gain, grad):
    weighted = grad * gain
    return spread * (
        weighted
        - jnp.mean(weighted, axis=-1, keepdims=True)
        - hat * jnp.mean(weighted * hat, axis=-1, keepdims=True)
    )


def rows_by_work(offs_ref, length):
    rows, docs = offs_ref.shape
    work = []
    for r in range(rows):
        total = jnp.int32(0)
        for d in range(docs):
            end = offs_ref[r, d + 1] if d + 1 < docs else length
            total += (end - offs_ref[r, d]) * (end - offs_ref[r, d])
        work.append(total)
    ranks = []
    for r in range(rows):
        rank = jnp.int32(0)
        for other in range(rows):
            if other < r:
                rank += (work[other] >= work[r]).astype(jnp.int32)
            elif other > r:
                rank += (work[other] > work[r]).astype(jnp.int32)
        ranks.append(rank)
    return [
        sum(jnp.where(ranks[r] == slot, jnp.int32(r), jnp.int32(0)) for r in range(rows))
        for slot in range(rows)
    ]


def project_kernel(
    slot,
    offs_ref,
    gain_ref,
    x_hbm,
    wq_hbm,
    wk_hbm,
    wv_hbm,
    normed_ref,
    out_ref,
    order_ref,
    x_ref,
    weight_ref,
    sems,
):
    group, _, span, width = out_ref.shape
    order = rows_by_work(offs_ref, group * span)
    copy_x = pltpu.make_async_copy(x_hbm.at[order[slot]], x_ref, sems.at[3])
    copy_x.start()
    copies = [
        pltpu.make_async_copy(weight, weight_ref.at[n], sems.at[n])
        for n, weight in enumerate((wq_hbm, wk_hbm, wv_hbm))
    ]
    for copy in copies:
        copy.start()
    for r, row in enumerate(order):
        order_ref[r] = row
    copy_x.wait()
    hat, _ = norm_parts(x_ref[...].astype(F32))
    normed = (hat * gain_ref[...]).astype(BF16)
    normed_ref[...] = normed
    for n in range(3):
        copies[n].wait()
        product = dot(normed, weight_ref[n]).astype(BF16)
        for s in range(group):
            out_ref[s, n] = product[:, s * width : (s + 1) * width]


def project(offsets, slot, x, gain, w_query, w_key, w_value, group):
    rows, span, model = x.shape
    return pl.pallas_call(
        functools.partial(project_kernel, slot),
        in_specs=[SMEM, VMEM] + [pl.BlockSpec(memory_space=pl.ANY)] * 4,
        out_specs=[VMEM, VMEM, SMEM],
        scratch_shapes=[
            pltpu.VMEM((span, model), BF16),
            pltpu.VMEM((3, model, model), BF16),
            pltpu.SemaphoreType.DMA((4,)),
        ],
        out_shape=[
            jax.ShapeDtypeStruct((span, model), BF16),
            jax.ShapeDtypeStruct((group, 3, span, model // group), BF16),
            jax.ShapeDtypeStruct((rows,), jnp.int32),
        ],
        compiler_params=kernel_params(),
        cost_estimate=cost(0, 1024),
        name="project",
    )(offsets, gain, x, w_query, w_key, w_value)


def doc_start(offs_ref, row, pos):
    start = jnp.zeros_like(pos)
    for d in range(offs_ref.shape[1]):
        first = offs_ref[row, d]
        start = jnp.where(pos >= first, first, start)
    return start


def doc_end(offs_ref, row, pos, length):
    end = jnp.int32(length)
    for d in reversed(range(offs_ref.shape[1])):
        first = offs_ref[row, d]
        end = jnp.where(first > pos, first, end)
    return end


def head_lanes(shape, head, head_dim):
    lane = lax.broadcasted_iota(jnp.int32, shape, 1)
    return (lane >= head * head_dim) & (lane < (head + 1) * head_dim)


def attend_kernel(slot, heads, head_dim, order_ref, offs_ref, scale_ref, held, *refs):
    result_ref, lse_ref, score_ref = refs[-3:]
    attend_row(
        order_ref[slot], heads, head_dim, offs_ref, scale_ref, held, result_ref, lse_ref, score_ref
    )


def attend_row(
    row, heads, head_dim, offs_ref, scale_ref, held, result_ref, lse_ref, score_ref
):
    blocks, _, span, width = held.shape
    wide = score_ref.shape[-1]
    per = wide // span
    lanes = min(128, wide)
    score_scale = head_dim ** (-0.5)

    def query_block(i, carry):
        first_pos = i * span
        queries = held[i, 0] * jnp.asarray(score_scale, BF16)
        query_head = [
            jnp.where(head_lanes((span, width), h, head_dim), queries, 0).astype(BF16)
            for h in range(heads)
        ]
        query_pos = first_pos + lax.broadcasted_iota(jnp.int32, (span, 1), 0)
        query_start = doc_start(offs_ref, row, query_pos)
        low = doc_start(offs_ref, row, first_pos) // wide
        high = (first_pos + span - 1) // wide + 1

        def score_step(j, tops):
            keys = held[pl.ds(j * per, per), 1].reshape(wide, width)
            key_pos = j * wide + lax.broadcasted_iota(jnp.int32, (span, wide), 1)
            allowed = (key_pos >= query_start) & (key_pos <= query_pos)
            new = []
            for h in range(heads):
                scores = jnp.where(allowed, dot_last(query_head[h], keys), MASKED)
                score_ref[h, j] = scores
                top = tops[h]
                for c in range(0, wide, lanes):
                    top = jnp.maximum(top, scores[:, c : c + lanes])
                new.append(top)
            return tuple(new)

        tops = lax.fori_loop(
            low, high, score_step, tuple(jnp.full((span, lanes), MASKED, F32) for h in range(heads))
        )
        tops = [jnp.max(top, axis=1, keepdims=True) for top in tops]

        def value_step(j, state):
            values = held[pl.ds(j * per, per), 2].reshape(wide, width)
            new = []
            for h in range(heads):
                total, acc = state[h]
                probs = jnp.exp(score_ref[h, j] - tops[h])
                for c in range(0, wide, lanes):
                    total = total + probs[:, c : c + lanes]
                acc = acc + dot(probs.astype(BF16), values)
                new.append((total, acc))
            return tuple(new)

        state = lax.fori_loop(
            low,
            high,
            value_step,
            tuple(
                (jnp.zeros((span, lanes), F32), jnp.zeros((span, width), F32)) for h in range(heads)
            ),
        )
        result = jnp.zeros((span, width), F32)
        for h in range(heads):
            total = jnp.sum(state[h][0], axis=1, keepdims=True)
            result = jnp.where(head_lanes((span, width), h, head_dim), state[h][1] / total, result)
            log_total = tops[h] + jnp.log(total)
            lse_ref[i, h : h + 1, :] = jnp.transpose(jnp.broadcast_to(log_total, (span, 128)))[
                0:1, :
            ]
        result_ref[i] = (result * scale_ref[...]).astype(BF16)
        return carry

    lax.fori_loop(0, blocks, query_block, 0)


def attend(order, offsets, slot, qkv, scale_lanes, heads, head_dim, at=0, count=1, into=None):
    group, _, span, width = qkv.shape
    length = group * span
    wide = max(span, min(512, length))
    held = [] if into is None else [into]
    return pl.pallas_call(
        functools.partial(attend_kernel, slot, heads, head_dim),
        grid=(1,),
        in_specs=[SMEM, SMEM, VMEM, VMEM] + [pl.BlockSpec(memory_space=pl.ANY)] * len(held),
        out_specs=[pl.BlockSpec((group, None, span, width), lambda i: (0, at, 0, 0)), VMEM],
        out_shape=[
            jax.ShapeDtypeStruct((group, count, span, width), BF16),
            jax.ShapeDtypeStruct((group, heads, span), F32),
        ],
        scratch_shapes=[pltpu.VMEM((heads, length // wide, span, wide), F32)],
        input_output_aliases={4: 0} if held else {},
        compiler_params=kernel_params(),
        cost_estimate=cost(0, 1024),
        name="attend",
    )(order, offsets, scale_lanes, qkv, *held)


def attend_back_kernel(slot, heads, head_dim, order_ref, offs_ref, *refs):
    attend_back_row(order_ref[slot], heads, head_dim, offs_ref, *refs)


def attend_back_row(
    row,
    heads,
    head_dim,
    offs_ref,
    inv_ref,
    lse_ref,
    held,
    grad_ref,
    out_ref,
    dqkv_ref,
    total_ref,
    q_ref,
    k_ref,
    g_ref,
    delta_ref,
    dq_ref,
):
    blocks, _, span, width = held.shape
    score_scale = head_dim ** (-0.5)
    picks = lax.broadcasted_iota(jnp.int32, (8, width), 0)
    lane = lax.broadcasted_iota(jnp.int32, (8, width), 1)
    ones = jnp.where(lane // head_dim == picks, 1.0, 0.0).astype(F32)

    def prepare(i, carry):
        queries = held[i, 0] * jnp.asarray(score_scale, BF16)
        keys = held[i, 1]
        grads = grad_ref[i]
        for h in range(heads):
            mine = head_lanes((span, width), h, head_dim)
            q_ref[h, i] = jnp.where(mine, queries, 0).astype(BF16)
            k_ref[h, i] = jnp.where(mine, keys, 0).astype(BF16)
            g_ref[h, i] = jnp.where(mine, grads, 0).astype(BF16)
        product = grads.astype(F32) * out_ref[i].astype(F32) * inv_ref[...]
        delta_ref[i] = lax.dot_general(
            ones, product, LAST, precision=lax.Precision.HIGHEST, preferred_element_type=F32
        )
        dq_ref[i] = jnp.zeros((span, width), F32)
        return carry + delta_ref[i]

    per = 2 if span * 2 <= 512 and blocks % 2 == 0 else 1
    wide = per * span
    total_ref[...] = lax.fori_loop(0, blocks, prepare, jnp.zeros((8, span), F32))

    def key_block(j, carry):
        keys = held[j, 1]
        values = held[j, 2]
        key_pos = j * span + lax.broadcasted_iota(jnp.int32, (span, 1), 0)
        last = (doc_end(offs_ref, row, (j + 1) * span - 1, blocks * span) - 1) // wide + 1

        def query_step(i, state):
            dk, dv = state
            query_pos = i * wide + lax.broadcasted_iota(jnp.int32, (1, wide), 1)
            query_start = doc_start(offs_ref, row, query_pos)
            allowed = (key_pos >= query_start) & (key_pos <= query_pos)
            at = pl.ds(i * per, per)
            dq = dq_ref[at].reshape(wide, width)
            for h in range(heads):
                queries = q_ref[h, at].reshape(wide, width)
                grads = g_ref[h, at].reshape(wide, width)
                log_total = jnp.concatenate(
                    [lse_ref[i * per + n, h : h + 1, :] for n in range(per)], axis=1
                )
                delta = jnp.concatenate(
                    [delta_ref[i * per + n, h : h + 1, :] for n in range(per)], axis=1
                )
                scores = dot_last(keys, queries)
                probs = jnp.exp(jnp.where(allowed, scores - log_total, MASKED))
                d_scores = (probs * (dot_last(values, grads) - delta)).astype(BF16)
                dv = dv + dot(probs.astype(BF16), grads)
                dk = dk + dot(d_scores, queries)
                dq = dq + dot_first(d_scores, k_ref[h, j])
            dq_ref[at] = dq.reshape(per, span, width)
            return (dk, dv)

        zero = jnp.zeros((span, width), F32)
        dk, dv = lax.fori_loop(j // per, last, query_step, (zero, zero))
        dqkv_ref[j, 1] = dk.astype(BF16)
        dqkv_ref[j, 2] = dv.astype(BF16)
        dqkv_ref[j, 0] = (dq_ref[j] * score_scale).astype(BF16)
        return carry

    lax.fori_loop(0, blocks, key_block, 0)


def attend_back(
    order, offsets, slot, qkv, grads, grads_at, scaled, scaled_at, inverse_lanes, lse, heads, head_dim
):
    group, _, span, width = qkv.shape

    def block_spec(at):
        return pl.BlockSpec((group, None, span, width), lambda i: (0, at, 0, 0))

    return pl.pallas_call(
        functools.partial(attend_back_kernel, slot, heads, head_dim),
        grid=(1,),
        in_specs=[SMEM, SMEM, VMEM, VMEM, VMEM, block_spec(grads_at), block_spec(scaled_at)],
        out_specs=[pl.BlockSpec((group, None, 3, span, width), lambda i: (0, 0, 0, 0, 0)), VMEM],
        out_shape=[
            jax.ShapeDtypeStruct((group, 1, 3, span, width), BF16),
            jax.ShapeDtypeStruct((8, span), F32),
        ],
        scratch_shapes=[pltpu.VMEM((heads, group, span, width), BF16)] * 3
        + [pltpu.VMEM((group, 8, span), F32), pltpu.VMEM((group, span, width), F32)],
        compiler_params=kernel_params(),
        cost_estimate=cost(0, 1024),
        name="attend_back",
    )(order, offsets, inverse_lanes, lse, qkv, grads, scaled)


def join_grads_kernel(parts, in_ref, out_ref, value_ref):
    group = in_ref.shape[0]
    for n in range(3):
        whole = jnp.concatenate([in_ref[s, 0, n] for s in range(group)], axis=1)
        piece = whole.shape[1] // parts
        if n == 2:
            value_ref[...] = whole
            continue
        for p in range(parts):
            to = (p * 2 + n) * piece
            out_ref[:, to : to + piece] = whole[:, p * piece : (p + 1) * piece]


def join_grads(block):
    group, _, _, span, width = block.shape
    return pl.pallas_call(
        functools.partial(join_grads_kernel, PARTS),
        out_shape=[
            jax.ShapeDtypeStruct((span, 2 * group * width), BF16),
            jax.ShapeDtypeStruct((span, group * width), BF16),
        ],
        compiler_params=kernel_params(),
        cost_estimate=cost(0, 1024),
        name="join_grads",
    )(block)


FF_STEP = 1024
LAYER_VMEM = 62 * 1024 * 1024


def layer_kernel(
    slots,
    order_ref,
    post_ref,
    ffn_ref,
    mid_gain_ref,
    scale_ref,
    w_out_ref,
    x_hbm,
    d_out_hbm,
    d_mid_hbm,
    w_fc1_hbm,
    *refs,
):
    count = len(slots)
    o_refs = refs[:count]
    (
        scaled_ref,
        ffn_in_ref,
        residual_ref,
        mid_ref,
        d_pre_ref,
        d_proj_ref,
        d_residual_ref,
        d_attn_ref,
        g_post_ref,
        g_ffn_ref,
        g_mid_ref,
        x_ref,
        d_out_ref,
        d_mid_ref,
        w_fc1_ref,
        act_ref,
        slope_ref,
        sems,
        row_sems,
    ) = refs[count:]
    group, _, span, width = o_refs[0].shape
    tokens, hidden = act_ref.shape
    step = FF_STEP // count
    steps = [slice(c, c + step) for c in range(0, hidden, step)]
    weight_copies = [
        pltpu.make_async_copy(
            w_fc1_hbm.at[:, c : c + FF_STEP], w_fc1_ref.at[:, c : c + FF_STEP], sems.at[n]
        )
        for n, c in enumerate(range(0, hidden, FF_STEP))
    ]
    x_copies, mid_copies = [], []
    for n, slot in enumerate(slots):
        row = order_ref[slot]
        to = slice(n * span, (n + 1) * span)
        x_copies.append(pltpu.make_async_copy(x_hbm.at[row], x_ref.at[to], row_sems.at[0, n]))
        x_copies.append(
            pltpu.make_async_copy(d_out_hbm.at[row], d_out_ref.at[to], row_sems.at[1, n])
        )
        rows = pl.ds(pl.multiple_of(row * span, span), span)
        mid_copies.append(
            pltpu.make_async_copy(d_mid_hbm.at[rows], d_mid_ref.at[to], row_sems.at[2, n])
        )
    for copy in x_copies + weight_copies + mid_copies:
        copy.start()

    for n in range(count):
        for s in range(group):
            scaled_ref[n * span : (n + 1) * span, s * width : (s + 1) * width] = o_refs[n][s, 0]
    proj_hat, proj_spread = norm_parts(dot(scaled_ref[...], w_out_ref[...]))
    for copy in x_copies:
        copy.wait()
    residual = x_ref[...].astype(F32) + proj_hat * post_ref[...]
    residual_ref[...] = residual
    res_hat, res_spread = norm_parts(residual)
    ffn_in = (res_hat * ffn_ref[...]).astype(BF16)
    ffn_in_ref[...] = ffn_in

    total = jnp.zeros((tokens, 1), F32)
    for n, at in enumerate(steps):
        if n % count == 0:
            weight_copies[n // count].wait()
        pre = dot(ffn_in, w_fc1_ref[:, at])
        phi = 0.5 + 0.5 * lax.erf(pre * (0.5**0.5))
        act = pre * phi
        act_ref[:, at] = act
        slope = phi + pre * jnp.exp(-0.5 * pre * pre) * 0.3989422804014327
        slope_ref[:, at] = slope.astype(slope_ref.dtype)
        total += jnp.sum(act, axis=1, keepdims=True)
    average = total / hidden
    total = jnp.zeros((tokens, 1), F32)
    for at in steps:
        centred = act_ref[:, at] - average
        total += jnp.sum(centred * centred, axis=1, keepdims=True)
    spread = lax.rsqrt(total / hidden + EPSILON)

    for copy in mid_copies:
        copy.wait()
    sum_weighted = jnp.zeros((tokens, 1), F32)
    sum_hat = jnp.zeros((tokens, 1), F32)
    for at in steps:
        hat = (act_ref[:, at] - average) * spread
        act_ref[:, at] = hat
        gain = mid_gain_ref[:, at]
        mid_ref[:, at] = (hat * gain).astype(BF16)
        grad = d_mid_ref[:, at]
        product = grad * hat
        g_mid_ref[:, at] = jnp.sum(product, axis=0, keepdims=True)
        sum_weighted += jnp.sum(grad * gain, axis=1, keepdims=True)
        sum_hat += jnp.sum(product * gain, axis=1, keepdims=True)
    sum_weighted = sum_weighted / hidden
    sum_hat = sum_hat / hidden
    d_ffn = jnp.zeros(x_ref.shape, F32)
    for at in steps:
        weighted = d_mid_ref[:, at] * mid_gain_ref[:, at]
        d_act = spread * (weighted - sum_weighted - act_ref[:, at] * sum_hat)
        d_pre = (d_act * slope_ref[:, at].astype(F32)).astype(BF16)
        d_pre_ref[:, at] = d_pre
        d_ffn += dot_last(d_pre, w_fc1_ref[:, at])

    g_ffn_ref[...] = jnp.sum(d_ffn * res_hat, axis=0, keepdims=True)
    d_residual = d_out_ref[...].astype(F32) + norm_back(res_hat, res_spread, ffn_ref[...], d_ffn)
    d_residual_ref[...] = d_residual
    g_post_ref[...] = jnp.sum(d_residual * proj_hat, axis=0, keepdims=True)
    d_proj = norm_back(proj_hat, proj_spread, post_ref[...], d_residual).astype(BF16)
    d_proj_ref[...] = d_proj
    d_attn = (dot_last(d_proj, w_out_ref[...]) * scale_ref[...]).astype(BF16)
    for n in range(count):
        for s in range(group):
            d_attn_ref[s, n] = d_attn[n * span : (n + 1) * span, s * width : (s + 1) * width]


def layer(order, slots, blocks, x, d_out, gains, w_out, d_mid, w_fc1):
    group, _, span, width = blocks[0][0].shape
    model, hidden = w_fc1.shape
    tokens = len(slots) * span
    shape = jax.ShapeDtypeStruct

    def block_spec(at):
        return pl.BlockSpec((group, 1, span, width), lambda i, o: (0, at, 0, 0))

    return pl.pallas_call(
        functools.partial(layer_kernel, slots),
        grid_spec=pltpu.PrefetchScalarGridSpec(
            num_scalar_prefetch=1,
            grid=(1,),
            in_specs=[VMEM] * 5
            + [pl.BlockSpec(memory_space=pl.ANY)] * 4
            + [block_spec(at) for _, at in blocks],
            out_specs=[VMEM] * 11,
            scratch_shapes=[
                pltpu.VMEM((tokens, model), BF16),
                pltpu.VMEM((tokens, model), BF16),
                pltpu.VMEM((tokens, hidden), d_mid.dtype),
                pltpu.VMEM(w_fc1.shape, BF16),
                pltpu.VMEM((tokens, hidden), F32),
                pltpu.VMEM((tokens, hidden), F32 if len(slots) == 1 else BF16),
                pltpu.SemaphoreType.DMA((hidden // FF_STEP,)),
                pltpu.SemaphoreType.DMA((3, len(slots))),
            ],
        ),
        out_shape=[
            shape((tokens, model), BF16),
            shape((tokens, model), BF16),
            shape((tokens, model), F32),
            shape((tokens, hidden), BF16),
            shape((tokens, hidden), BF16),
            shape((tokens, model), BF16),
            shape((tokens, model), F32),
            shape((group, len(slots), span, width), BF16),
            shape((1, model), F32),
            shape((1, model), F32),
            shape((1, hidden), F32),
        ],
        compiler_params=pltpu.CompilerParams(vmem_limit_bytes=LAYER_VMEM),
        cost_estimate=cost(0, 1024),
        name="layer",
    )(order, *gains, w_out, x, d_out, d_mid, w_fc1, *[block for block, _ in blocks])


def layer_out_kernel(order_ref, *refs):
    count = (len(refs) - 2) // 2
    weight, out_ref = refs[-2], refs[-1]
    span, slot = out_ref.shape[1], 0
    for n in range(count):
        result = (refs[n][...] + dot(refs[count + n][...], weight[...])).astype(BF16)
        for at in range(0, result.shape[0], span):
            out_ref[order_ref[slot]] = result[at : at + span]
            slot += 1


def last_step(order, shape, residuals, mids, w_fc2):
    return pl.pallas_call(
        layer_out_kernel,
        in_specs=[SMEM] + [VMEM] * (2 * len(mids) + 1),
        out_shape=jax.ShapeDtypeStruct(shape, BF16),
        compiler_params=kernel_params(),
        cost_estimate=cost(0, 1024),
        name="layer_out",
    )(order, *residuals, *mids, w_fc2)


def flip(value, axis, bit):
    size = lax.axis_size(axis)
    return lax.ppermute(value, axis, [(i, i ^ (1 << bit)) for i in range(size)])


def bits(axis):
    return (lax.axis_size(axis) - 1).bit_length()


PARTS = 4


def weight_kernel(count, rows, added, shards, part_ref, *refs):
    out_ref = refs[-1]
    high = out_ref.shape[1]
    per = rows * (shards + 1)
    extras = refs[per * count : per * count + added]
    at = 0
    for n in range(count):
        mine = refs[n * per : (n + 1) * per]
        rights = mine[rows * shards :]
        width = rights[0].shape[1]
        total = 0.0
        for r in range(rows):
            left = [ref[...] for ref in mine[r * shards : (r + 1) * shards]]
            left = jnp.concatenate(left, axis=1) if shards > 1 else left[0]
            total += dot_first(left, rights[r][...])
        for i in range(shards):
            piece = total[i * high : (i + 1) * high]
            for extra in extras:
                piece = piece + extra[i, :, at : at + width].astype(F32)
            out_ref[i, :, at : at + width] = piece.astype(BF16)
        at += width


def weight_part_plain(pairs, part, parts, extras, group):
    pieces = []
    for lefts, rights, kind in pairs:
        left, right = jnp.concatenate(lefts), jnp.concatenate(rights)
        if kind == "columns":
            wide = right.shape[1] // parts
            right = lax.dynamic_slice(right, (0, part * wide), (right.shape[0], wide))
            left = left.reshape(left.shape[0], group, -1)
        else:
            left = left.reshape(left.shape[0], group, parts, -1)
            left = lax.dynamic_index_in_dim(left, part, 2, keepdims=False)
        pieces.append(jnp.einsum("tsd,te->sde", left, right, preferred_element_type=F32))
    total = jnp.concatenate(pieces, axis=2)
    axis = 2 if pairs[0][2] == "columns" else 1
    for extra, at in extras:
        size = total.shape[axis]
        total = total + lax.dynamic_slice_in_dim(extra, at * size, size, axis).astype(F32)
    return total.astype(BF16)


def weight_part(pairs, part, parts, extras, group):
    shards = 2 if pairs[0][2] == "columns" else 4
    specs, arrays, width = [], [], 0
    for lefts, rights, kind in pairs:
        model = lefts[0].shape[1]
        stride = 1 if kind == "columns" else parts
        high = model // group // stride
        wide = rights[0].shape[1] // (parts if kind == "columns" else 1)
        for left in lefts:
            for i in range(shards):

                def left_at(g, p, i=i, stride=stride):
                    return (0, (g * shards + i) * stride + (p[0] if stride > 1 else 0))

                specs.append(pl.BlockSpec((left.shape[0], high), left_at))
                arrays.append(left)
        for right in rights:

            def right_at(g, p, stride=stride):
                return (0, p[0] if stride == 1 else 0)

            specs.append(pl.BlockSpec((right.shape[0], wide), right_at))
            arrays.append(right)
        width += wide
    if high % 128:
        return weight_part_plain(pairs, part, parts, extras, group)
    block = pl.BlockSpec((shards, high, width), lambda g, p: (g, 0, 0))
    by_row = pairs[0][2] == "rows"

    def extra_spec(n):
        def block_at(g, p):
            return (g, p[n], 0) if by_row else (g, 0, p[n])

        return pl.BlockSpec((shards, high, width), block_at)

    numbers = jnp.stack([part] + [at for _, at in extras]).astype(jnp.int32)
    return pl.pallas_call(
        functools.partial(weight_kernel, len(pairs), len(pairs[0][0]), len(extras), shards),
        grid_spec=pltpu.PrefetchScalarGridSpec(
            num_scalar_prefetch=1,
            grid=(group // shards,),
            in_specs=specs + [extra_spec(n + 1) for n in range(len(extras))],
            out_specs=block,
        ),
        out_shape=jax.ShapeDtypeStruct((group, high, width), BF16),
        compiler_params=kernel_params(),
        cost_estimate=cost(0, 1024),
        name="weight_part",
    )(numbers, *arrays, *[extra for extra, _ in extras])


class WeightSum:
    def __init__(self, *pairs):
        self.pairs = pairs
        batch_at = lax.axis_index("batch")
        self.near, self.far = batch_at & 1, (batch_at >> 1) & 1
        self.zero = batch_at * 0

    def piece(self, order, near, far, *extras):
        def part_of(part):
            return weight_part(self.pairs, part, PARTS, extras, lax.axis_size("blk"))

        return order(part_of, near * 2 + far)

    def half(self, order, near, *extras):
        def part_of(part):
            return weight_part(self.pairs, part, 2, extras, lax.axis_size("blk"))

        return order(part_of, near)

    def away_far(self, order):
        return self.piece(order, 1 - self.near, 1 - self.far)

    def away_near(self, order):
        return self.piece(order, 1 - self.near, self.far)

    def away(self, order, *more):
        return self.half(order, 1 - self.near, *more)

    def send_far(self, order, away):
        return self.piece(order, self.near, 1 - self.far, (away, self.zero))

    def send(self, order, *aways):
        extras = [(away, 1 - self.far) for away in aways]
        return self.piece(order, self.near, 1 - self.far, *extras)

    def keep(self, order, near, arrived):
        return self.piece(order, self.near, self.far, (near, self.zero), (arrived, self.zero))

    def keep_rest(self, order, arrived, *aways):
        extras = [(away, self.far) for away in aways]
        return self.piece(order, self.near, self.far, (arrived, self.zero), *extras)

    def own(self, order, *aways):
        return self.half(order, self.near, *[(away, self.zero) for away in aways])


def over_near(sent):
    return flip(sent, "batch", 0)


def over_far(sent):
    return flip(sent, "batch", 1)


class Order:
    def __init__(self):
        self.last = ()

    def __call__(self, step, *values):
        self.last = step(*tie(values, self.last))
        return self.last


def window(always, step):
    def nothing():
        return jax.tree.map(lambda leaf: jnp.zeros(leaf.shape, leaf.dtype), jax.eval_shape(step))

    return lax.cond(always, step, nothing)


def tie(values, *after):
    return lax.optimization_barrier((values, after))[0]


def combine_kernel(plan, at_ref, *refs):
    ins = sum(count for _, count, _ in plan)
    into, out_of = list(refs[:ins]), list(refs[ins:])
    for n, (kind, count, cut) in enumerate(plan):
        terms = [into.pop(0) for _ in range(count)]
        if kind == "small":
            out_of.pop(0)[...] = sum(term[...] for term in terms)
            continue
        if kind == "stack":
            out = out_of.pop(0)
            out[0], out[1] = terms[0][0], terms[1][0]
            continue

        def put(ref, j, i):
            at, each = 0, 2 if kind == "add" else 1
            for m in range(0, len(terms), each):
                to = slice(at, at + terms[m].shape[2])
                if kind == "add":
                    total = terms[m][i].astype(F32) + terms[m + 1][i].astype(F32)
                    ref[j, :, to] = total.astype(BF16)
                else:
                    ref[j, :, to] = terms[m][i]
                at = to.stop

        if cut:
            keep, send = out_of.pop(0), out_of.pop(0)
            for j in range(keep.shape[0]):
                put(keep, j, 2 * j + at_ref[n])
                put(send, j, 2 * j + 1 - at_ref[n])
        else:
            whole = out_of.pop(0)
            for j in range(whole.shape[0]):
                put(whole, j, j)


class Tree:
    def __init__(self, *mine, halved=2):
        self.steps = [("blk", bit) for bit in range(bits("blk"))]
        self.steps += [("batch", bit) for bit in range(halved, bits("batch"))]
        self.steps += [("far", 1), ("near", 0)][2 - halved :]
        self.terms, self.last = list(mine), "first"

    def start(self):
        kind, bit = self.steps[0]
        return flip(self.send, "blk" if kind == "blk" else "batch", bit)

    def end(self, arrived):
        self.last = self.steps.pop(0)[0]
        self.terms = [self.kept, arrived]


def combine(trees):
    me = lax.axis_index("blk")
    plan, ins, shapes, at = [], [], [], []
    for tree in trees:
        kind, bit = tree.steps[0]
        cut = kind == "blk" and tree.last != "small"
        if tree.last == "small":
            plan.append(("small", len(tree.terms), False))
            ins += tree.terms
            shapes.append(jax.ShapeDtypeStruct(tree.terms[0].shape, F32))
            at.append(me * 0)
            continue
        state = {"first": "first", "far": "stack"}.get(tree.last, "add")
        plan.append((state, len(tree.terms), cut))
        ins += tree.terms
        count, high, wide = tree.terms[0].shape
        if state != "stack":
            each = 1 if state == "first" else 2
            wide = sum(term.shape[2] for term in tree.terms[::each])
        count = count // 2 if cut else 2 if state == "stack" else count
        shapes += [jax.ShapeDtypeStruct((count, high, wide), BF16)] * (2 if cut else 1)
        at.append((me >> bit) & 1 if cut else me * 0)
    outs = list(
        pl.pallas_call(
            functools.partial(combine_kernel, plan),
            in_specs=[SMEM] + [VMEM] * len(ins),
            out_shape=shapes,
            compiler_params=kernel_params(),
            cost_estimate=cost(0, 1024),
            name="combine",
        )(jnp.stack(at).astype(jnp.int32), *ins)
    )
    for tree, (_, _, cut) in zip(trees, plan):
        tree.kept = outs.pop(0)
        tree.send = outs.pop(0) if cut else tree.kept


def place_kernel(layout, lines, part_ref, *refs):
    count = 2 * len(layout) + (2 if lines else 0)
    ins, outs = list(refs[:count]), list(refs[count:])
    if lines:
        one, other = ins[-2:]
        for (start, size, cut), out in zip(lines, outs[-len(lines) :]):
            at = pl.ds(start, size)
            if cut:
                at = pl.ds(pl.multiple_of(start + part_ref[2] * size, 128), size)
            out[...] = one[:, at] + other[:, at]
    near, far = part_ref[0], part_ref[1]
    order = [near * 2 + far, near * 2 + 1 - far, (1 - near) * 2 + far, (1 - near) * 2 + 1 - far]
    for spans in layout:
        both = [ins.pop(0), ins.pop(0)]
        count = 2 * both[0].shape[0]
        for start, width, kind in spans:
            out = outs.pop(0)
            for n, part in enumerate(order if count == 4 else [near, 1 - near]):
                value = both[n * 2 // count][n % (count // 2), :, start : start + width]
                value = value.astype(F32)
                if kind == "columns":
                    out[:, pl.ds(pl.multiple_of(part * width, 128), width)] = value
                else:
                    high = value.shape[0]
                    out[pl.ds(pl.multiple_of(part * high, 8), high), :] = value


def place(trees, layout, small=None, lines=()):
    batch_at = lax.axis_index("batch")
    parts = jnp.stack([batch_at & 1, (batch_at >> 1) & 1, lax.axis_index("blk")])
    parts = parts.astype(jnp.int32)
    ins, shapes = [], []
    for tree, spans in zip(trees, layout):
        ins += tree.terms
        count, high = 2 * tree.kept.shape[0], tree.kept.shape[1]
        for _, width, kind in spans:
            shape = (high, count * width) if kind == "columns" else (count * high, width)
            shapes.append(jax.ShapeDtypeStruct(shape, F32))
    if lines:
        ins += small.terms
        shapes += [jax.ShapeDtypeStruct((1, size), F32) for _, size, _ in lines]
    return pl.pallas_call(
        functools.partial(place_kernel, layout, lines),
        in_specs=[SMEM] + [VMEM] * len(ins),
        out_shape=shapes,
        compiler_params=kernel_params(),
        cost_estimate=cost(0, 1024),
        name="place",
    )(parts, *ins)


class SmallSum:
    def __init__(self, mine):
        self.steps = [("batch", bit) for bit in range(bits("batch"))]
        self.steps += [("blk", bit) for bit in range(bits("blk"))]
        self.terms, self.last = [mine], "small"

    def start(self):
        return flip(self.send, *self.steps[0])

    def end(self, arrived):
        self.steps.pop(0)
        self.terms = [self.kept, arrived]


def input_grad_kernel(slots, parts, order_ref, gain_ref, x_hbm, *refs):
    wq_ref, wk_ref, wv_ref = refs[:3]
    count = len(slots)
    d_refs, value_refs, res_refs = refs[3 : 3 + count], refs[3 + count : 3 + 2 * count], refs[3 + 2 * count : -4]
    out_ref, sum_ref, x_ref, sems = refs[-4:]
    span, model = x_ref.shape[1:]
    piece = model // parts
    copies = [
        pltpu.make_async_copy(x_hbm.at[order_ref[slot]], x_ref.at[n], sems.at[n])
        for n, slot in enumerate(slots)
    ]
    for copy in copies:
        copy.start()
    residuals = [held.at[pl.ds(at, span)] for held in res_refs for at in range(0, held.shape[0], span)]
    residuals = residuals[-count:] if slots[0] else residuals[:count]
    for copy in copies:
        copy.wait()
    total = jnp.zeros(sum_ref.shape, F32)
    for n in range(count):
        grad = dot_last(value_refs[n][...], wv_ref[...])
        for p in range(parts):
            for m, weight in enumerate((wq_ref, wk_ref)):
                at = (p * 2 + m) * piece
                grad += dot_last(d_refs[n][:, at : at + piece], weight[:, p * piece : (p + 1) * piece])
        hat, spread = norm_parts(x_ref[n].astype(F32))
        out_ref[n] = residuals[n][...] + norm_back(hat, spread, gain_ref[...], grad)
        total += jnp.sum(grad * hat, axis=0, keepdims=True)
    sum_ref[...] = total


def input_grad(order, slots, x, gain, weights, d_rows, d_values, d_residuals):
    _, span, model = x.shape
    count = len(slots)
    return pl.pallas_call(
        functools.partial(input_grad_kernel, slots, PARTS),
        in_specs=[SMEM, VMEM, pl.BlockSpec(memory_space=pl.ANY)]
        + [VMEM] * (3 + 2 * count + len(d_residuals)),
        out_shape=[
            jax.ShapeDtypeStruct((count, span, model), F32),
            jax.ShapeDtypeStruct((1, model), F32),
        ],
        scratch_shapes=[
            pltpu.VMEM((count, span, model), BF16),
            pltpu.SemaphoreType.DMA((count,)),
        ],
        compiler_params=kernel_params(),
        cost_estimate=cost(0, 1024),
        name="input_grad",
    )(order, gain, x, *weights, *d_rows, *d_values, *d_residuals)


def in_place_kernel(order_ref, *refs):
    *ins, out_ref, sems = refs
    copies, slot = [], 0
    for part in ins:
        for n in range(part.shape[0]):
            copies.append(
                pltpu.make_async_copy(part.at[n], out_ref.at[order_ref[slot]], sems.at[slot])
            )
            slot += 1
    for copy in copies:
        copy.start()
    for copy in copies:
        copy.wait()


def in_place(order, parts):
    rows = order.shape[0]
    return pl.pallas_call(
        in_place_kernel,
        in_specs=[SMEM] + [pl.BlockSpec(memory_space=pl.ANY)] * len(parts),
        out_specs=pl.BlockSpec(memory_space=pl.ANY),
        out_shape=jax.ShapeDtypeStruct((rows, *parts[0].shape[1:]), parts[0].dtype),
        scratch_shapes=[pltpu.SemaphoreType.DMA((rows,))],
        compiler_params=kernel_params(),
        cost_estimate=cost(0, 1024),
        name="in_place",
    )(order, *parts)


def on_device(
    inputs,
    ln_attn,
    w_query,
    w_key,
    w_value,
    w_out,
    head_scale,
    ln_post,
    ln_ffn,
    w_fc1,
    ln_mid,
    w_fc2,
    offsets,
    cotangent,
):
    row_count, span, model = inputs.shape
    head_count = head_scale.shape[0]
    head_dim = model // head_count
    tokens = row_count * span
    group = lax.axis_size("blk")
    heads = head_count // group
    width = heads * head_dim
    my_index = lax.axis_index("blk")
    rows = range(row_count)

    always = offsets[0, 0] == 0
    gain = ln_attn.reshape(1, model)
    last = row_count - 1
    my_scale = lax.dynamic_slice(head_scale, (my_index * heads,), (heads,))
    scale_lanes = jnp.repeat(my_scale, head_dim).reshape(1, width)
    layer_gains = [
        ln_post.reshape(1, model),
        ln_ffn.reshape(1, model),
        ln_mid.reshape(1, -1),
        jnp.repeat(head_scale, head_dim).reshape(1, model),
    ]

    def project_row(r, x):
        return project(offsets, r, x, gain, w_query, w_key, w_value, group)

    def attend_one(r, held, into=None):
        place = (r, last) if r < last else (0, 1)
        return attend(by_work, offsets, r, held, scale_lanes, heads, head_dim, *place, into)

    def layer_rows(slots, blocks):
        return layer(by_work, slots, blocks, inputs, cotangent, layer_gains, w_out, d_mid, w_fc1)

    def back(order, r, row_heads, at=0):
        def back_row(held):
            return attend_back(
                by_work,
                offsets,
                r,
                held,
                row_heads,
                at,
                *((first_out, r) if r < last else (last_out, 0)),
                1.0 / scale_lanes,
                lse[r],
                heads,
                head_dim,
            )

        return order(back_row, qkv[r])

    def first_window():
        order = Order()
        return exchange(sent), [
            order(functools.partial(project_row, r), inputs) for r in rows[1:]
        ]

    normed_first, sent, by_work = project_row(0, inputs)
    held, projected = first_window()
    qkv = [held]
    normed = [normed_first] + [part[0] for part in projected]
    first_out, lse = None, []
    for r in rows[1:]:

        def next_window():
            order = Order()
            extra = ()
            if r == 1:
                d_mid = jnp.einsum(
                    "td,fd->tf",
                    cotangent.reshape(tokens, model),
                    w_fc2,
                    preferred_element_type=F32,
                )
                extra = d_mid
            if r == last:
                d_out = [
                    lax.dynamic_index_in_dim(cotangent, by_work[n], keepdims=False) for n in rows
                ]
                extra = d_out[0], jnp.concatenate(d_out[1:])
            return exchange(projected[r - 1][1]), attend_one(r - 1, qkv[r - 1], first_out), extra

        held, (first_out, log_total), extra = window(always, next_window)
        d_mid = extra if r == 1 else d_mid
        qkv.append(held)
        lse.append(log_total)

    d_out = list(extra)

    def early_window():
        return (
            exchange(first_out),
            attend_one(last, qkv[last]),
        )

    early, (last_out, log_total) = window(always, early_window)
    lse.append(log_total)

    def late_window():
        return exchange(last_out), layer_rows([0], [(early, 0)])

    late, layer_first = window(always, late_window)

    def layer_window():
        blocks = [(early, r) if r < last else (late, 0) for r in rows[1:]]
        return exchange(layer_first[7]), layer_rows(list(rows[1:]), blocks)

    first_heads, layer_rest = window(always, layer_window)
    (
        scaled,
        ffn_in,
        residual,
        mid,
        d_pre,
        d_proj,
        d_residual,
        d_attn,
        g_post,
        g_ffn,
        g_mid,
    ) = zip(layer_first, layer_rest)
    sum_one = WeightSum((mid, d_out, "rows"))
    sum_two = WeightSum((ffn_in, d_pre, "columns"))
    sum_three = WeightSum((scaled, d_proj, "columns"))
    order = Order()
    away_one = over_near(sum_one.away_far(order))
    near_one = over_near(sum_one.away_near(order))
    far_one = over_far(sum_one.send_far(order, away_one))

    def back_first():
        order = Order()
        heads_in = exchange(d_attn[1])
        away = over_near(sum_two.away_far(order))
        out = back(order, 0, first_heads)
        return heads_in, out, sum_two.send_far(order, away)

    rest_heads, (sent, total), sent_two = window(always, back_first)
    far_two = over_far(sent_two)
    totals = [total]

    def back_second():
        order = Order()
        grad = exchange(sent)
        out = back(order, 1, rest_heads, 0)
        near = sum_two.away_near(order), sum_three.away(order)
        return grad, out, near, sum_one.keep(order, near_one, far_one)

    grad, (sent, total), near, mine_one = window(always, back_second)
    near_two, away_three = near
    totals.append(total)
    grads = [grad]
    tree_one = Tree(mine_one)
    combine([tree_one])
    moved = tree_one.start()
    sent = tie(sent, tree_one.send)
    near_two, away_three = over_near(near_two), over_near(away_three)
    for r in rows[2:]:

        def back_next():
            order = Order()
            out_of = ()
            grad = exchange(sent)
            out = back(order, r, rest_heads, r - 1)
            if r == 2:
                mine = sum_two.keep(order, near_two, far_two)
                out_of = mine, sum_three.own(order, away_three)
            return grad, out_of, out

        grad, out_of, (sent, total) = window(always, back_next)
        totals.append(total)
        grads.append(grad)
        if r == 2:
            mine_two, mine_three = out_of
    tree_one.end(moved)
    tree_two = Tree(mine_two)
    tree_three = Tree(mine_three, halved=1)
    combine([tree_one, tree_two, tree_three])
    moved = tree_one.start(), tree_two.start()
    moved_three = tree_three.start()
    sent = tie(sent, tree_one.send, tree_two.send)

    def back_last():
        order = Order()
        grad = exchange(sent)
        joined = [order(join_grads, part) for part in grads]
        d_rows, d_values = zip(*joined)
        early_qk = WeightSum((normed[:last], d_rows, "columns"))
        early_v = WeightSum((normed[:last], d_values, "columns"))
        early = [early_qk.away(order), early_v.away(order), early_qk.own(order), early_v.own(order)]
        part = order(
            lambda x: input_grad(
                by_work,
                list(rows[:last]),
                x,
                gain,
                (w_query, w_key, w_value),
                d_rows,
                d_values,
                d_residual,
            ),
            inputs,
        )
        return grad, joined, part, early

    grad, joined, part, early_sums = window(always, back_last)
    early_grads, early_gain = part
    early_away_qk, early_away_v, early_qk, early_v = early_sums
    grad, moved = tie((grad, moved))
    tree_one.end(moved[0])
    tree_two.end(moved[1])
    order = Order()
    joined = joined + [order(join_grads, grad)]
    d_rows, d_values = zip(*joined)
    sum_qk = WeightSum((normed[last:], d_rows[last:], "columns"))
    sum_v = WeightSum((normed[last:], d_values[last:], "columns"))
    away_qk = over_near(sum_qk.away(order, (early_away_qk, sum_qk.zero)))
    away_v = over_near(sum_v.away(order, (early_away_v, sum_v.zero)))
    sent_qk = sum_qk.send(order, away_qk, early_qk)
    far_qk = over_far(sent_qk)
    for tree in (tree_one, tree_two):
        tree.terms = list(tie(tree.terms, sent_qk))
    combine([tree_one, tree_two])
    moved = tree_one.start(), tree_two.start()
    away_v = tie(away_v, tree_one.send, tree_two.send)

    def advance(trees, extra=lambda: ()):
        def step():
            return [tree.start() for tree in trees], extra()

        moved, out = window(always, step)
        for tree, arrived in zip(trees, moved):
            tree.end(arrived)
        return out

    def beside():
        order = Order()
        tree = Tree(sum_v.own(order, away_v, early_v), halved=1)
        combine([tree])

        def input_step(x):
            return input_grad(
                by_work,
                [last],
                x,
                gain,
                (w_query, w_key, w_value),
                d_rows[last:],
                d_values[last:],
                d_residual,
            )

        return tree.kept, tree.start(), order(input_step, inputs)

    kept, arrived, (late_grads, late_gain) = window(always, beside)
    moved, arrived = tie((moved, arrived))
    tree_one.end(moved[0])
    tree_two.end(moved[1])
    grad_ln_attn = early_gain + late_gain
    tree_v = Tree(halved=1)
    tree_v.kept = kept
    tree_v.end(arrived)
    tree_v.terms += [tree_three.kept, moved_three]
    tree_qk = Tree(sum_qk.keep_rest(order, far_qk, away_qk, early_qk))
    delta_sum = sum(jnp.sum(total, axis=1) for total in totals)
    my_grad = delta_sum[:heads] / my_scale
    scale_part = lax.dynamic_update_slice(
        jnp.zeros((head_count,), F32), my_grad, (my_index * heads,)
    )
    small = SmallSum(
        jnp.concatenate(
            [grad_ln_attn[0], sum(g_post)[0], sum(g_ffn)[0], sum(g_mid)[0], scale_part]
        ).reshape(1, -1)
    )
    piece = model // PARTS
    ff_piece = w_fc1.shape[1] // PARTS
    trees = [tree_qk, tree_v, tree_two, tree_one]
    placed = layer_out = grad_inputs = None
    while any(tree.steps for tree in trees + [small]):
        combine([tree for tree in trees + [small] if tree.steps])

        def beside_step():
            if layer_out is None:
                order = Order()

                def output_step(weight):
                    return last_step(by_work, inputs.shape, residual, mid, weight)

                return order(output_step, w_fc2)
            if grad_inputs is None:
                return in_place(by_work, [early_grads, late_grads])
            if tree_two.steps or tree_one.steps or placed is not None:
                return ()
            return place(
                [tree_one, tree_two], [[(0, model, "rows")], [(0, ff_piece, "columns")]]
            )

        beside_out = advance([tree for tree in trees + [small] if tree.steps], beside_step)
        if layer_out is None:
            layer_out = beside_out
        elif grad_inputs is None:
            grad_inputs = beside_out
        else:
            placed = beside_out or placed
    if placed is None:
        placed = place([tree_one, tree_two], [[(0, model, "rows")], [(0, ff_piece, "columns")]])
    grad_fc2, grad_fc1 = placed
    lines = [(0, model), (model, model), (2 * model, model), (3 * model, ln_mid.shape[0])]
    ends = lines[-1][0] + lines[-1][1]
    layout = [
        [(n * piece, piece, "columns") for n in range(2)],
        [(n * 2 * piece, 2 * piece, "columns") for n in range(2)],
    ]
    if model // group % 128:
        grad_query, grad_key, grad_value, grad_out = place([tree_qk, tree_v], layout)
        total = sum(small.terms)[0]
        gains = [
            lax.dynamic_slice(total, (start + my_index * (size // group),), (size // group,))
            for start, size in lines
        ]
        gains.append(total[ends:])
    else:
        lines = [(start, size // group, True) for start, size in lines]
        lines.append((ends, head_count, False))
        grad_query, grad_key, grad_value, grad_out, *gains = place(
            [tree_qk, tree_v], layout, small, lines
        )
        gains = [line[0] for line in gains]
    return (
        layer_out,
        grad_inputs,
        gains[0],
        grad_query,
        grad_key,
        grad_value,
        grad_out,
        gains[4],
        gains[1],
        gains[2],
        grad_fc1,
        gains[3],
        grad_fc2,
    )


def solution(mesh):
    rows = P("batch", "blk", None)
    shard = P("blk", None)
    return jax.shard_map(
        on_device,
        mesh=mesh,
        in_specs=(rows,) + (P(),) * 11 + (P("batch", None), rows),
        out_specs=(
            rows,
            rows,
            P("blk"),
            shard,
            shard,
            shard,
            shard,
            P(),
            P("blk"),
            P("blk"),
            shard,
            P("blk"),
            shard,
        ),
        check_vma=False,
    )
```
